512 devices in a mesh: ctx: 64 (over x, z_hi, y, core), head: 8 (over z_lo).
Axes of the slice: x: 4, y: 4, z: 16 (z_hi: 2, z_lo: 8; z = z_hi * 8 + z_lo), core: 2. Of those that a mesh axis runs over, the one named last changes fastest.
Arguments:
- queries: bfloat16 [64, 2, 512, 1024], P('ctx', None, None, 'head'), may hold values from -8 to 8
- key_states: bfloat16 [64, 2, 512, 128], P('ctx', None, 'head'), may hold values from -6 to 6
- value_states: bfloat16 [64, 2, 512, 128], P('ctx', None, 'head'), may hold values from -6 to 6
- out_grad: bfloat16 [64, 2, 512, 1024], P('ctx', None, None, 'head'), may hold values from -6 to 6
- segments: int32 [65536], replicated, may hold values from 0 to 169, never falling along the last dimension, each value on 1 to 1536 neighbouring positions
Outputs:
- attended: bfloat16 [64, 2, 512, 1024], P('ctx', None, None, 'head')
- query_grad: bfloat16 [64, 2, 512, 1024], P('ctx', None, None, 'head')
- key_grad: bfloat16 [64, 2, 512, 128], P('ctx', None, 'head')
- value_grad: bfloat16 [64, 2, 512, 128], P('ctx', None, 'head')
The draws below stay inside these ranges and needn't reach their ends.
Inputs may be any that keep to these rules, and one draw needn't show every extreme that they name: `segments`: document numbers never fall along the sequence; every document covers at most 1536 positions, and one covers exactly that many.
All inputs are finite; a program needn't handle non-finite values.
Results may differ from the reference program's by a relative error of at most 0.017.
Values may be sent and summed in bfloat16 or wider, within the bound.
No kernel may reach another device: no remote copies, remote signals or barrier semaphores. Data moves between devices by JAX's collectives and lax.ppermute only.
A program may use at most 64 MiB of HBM per device.

```python
import math
import jax
import jax.numpy as jnp
import numpy as np
from jax import lax

HD = 128
QH = 8
SPAN = 512
REACH = 3
PAIRS = 64
SEQ = 65536
DOCS = 170


def draw_key_states(key, part):
    key = jax.random.fold_in(key, 11)
    shape = (PAIRS, 2, SPAN, HD)
    value = jnp.clip(jax.random.normal(key, shape, jnp.float32), -6.0, 6.0)
    return value.astype(jnp.bfloat16)


def draw_queries(key, part):
    key = jax.random.fold_in(key, 23)
    shape = (PAIRS, 2, SPAN, QH * HD)
    value = jnp.clip(jax.random.normal(key, shape, jnp.float32), -6.0, 6.0)
    return value.astype(jnp.bfloat16)


def block_levels(stream_key, shape, shards, smallest, largest):
    gain = 1.0
    for position, parts in shards:
        steps = jax.random.uniform(jax.random.fold_in(jax.random.fold_in(stream_key, 6), position), (parts,), jnp.float32, smallest / len(shards), largest / len(shards))
        gain = gain * jnp.repeat(jnp.exp(steps), shape[position] // parts).reshape((-1,) + (1,) * (len(shape) - 1 - position))
    return gain


def length_profile(number_of, total, limit, slope):
    loads = [(1 << 20) // math.isqrt(grade ** slope) + 1 for grade in range(2, number_of + 1)]
    surplus, holding = total - limit - (number_of - 1), [1] * (number_of - 1)
    while surplus > 0:
        movable = [i for i in range(number_of - 1) if holding[i] < limit]
        whole, remaining = sum([loads[i] for i in movable]), surplus
        for i in movable:
            addition = min(limit - holding[i], max(1, remaining * loads[i] // whole), surplus)
            holding[i] = holding[i] + addition
            surplus = surplus - addition
    return np.array([limit] + holding)


def ragged(own_key, count, total, bound, skew):
    if count == 2:
        one = jax.random.randint(own_key, (), max(1, total - bound), min(bound, total - 1) + 1)
        return jnp.stack([one, total - one])
    lengths = jnp.asarray(length_profile(count, total, bound, skew), jnp.int32)
    twos = (count - 1) // 2
    donor, receiver = lengths[1:1 + 2 * twos:2], lengths[2:2 + 2 * twos:2]
    room = jnp.minimum(donor - 1, bound - receiver)
    shifted = jax.random.randint(jax.random.fold_in(own_key, 1), (twos,), 0, 1 << 20) % (room + 1)
    lengths = lengths.at[1:1 + 2 * twos:2].set(donor - shifted).at[2:2 + 2 * twos:2].set(receiver + shifted)
    return lengths[jax.random.permutation(jax.random.fold_in(own_key, 2), count)]


def centred(own_key, shape, scale, most, pieces=(), kind=jnp.bfloat16):
    array = scale * jax.random.normal(own_key, shape, jnp.float32)
    if pieces:
        array = array * block_levels(own_key, shape, pieces, -0.22, 0.18)
    return jnp.clip(array, -most, most).astype(kind)


def setup_inputs(seed: int = 0) -> dict:
    streams_of = jax.random.split(jax.random.key(seed), 6)
    queries = draw_queries(jax.random.fold_in(streams_of[5], 71), 0)
    key_states = draw_key_states(jax.random.fold_in(streams_of[5], 71), 0)
    value_states = centred(streams_of[2], (PAIRS, 2, SPAN, HD), 1.0, 6.0, ((0, 64), (2, 8)))
    out_grad = centred(streams_of[3], (PAIRS, 2, SPAN, QH * HD), 1.0, 6.0, ((0, 64), (3, 8)))
    segments = jnp.searchsorted(jnp.cumsum(ragged(streams_of[4], DOCS, SEQ, REACH * SPAN, 2)), jnp.arange(SEQ), side="right").astype(jnp.int32)
    return dict(queries=queries, key_states=key_states, value_states=value_states, out_grad=out_grad, segments=segments)


NEG_FILL = -1.0e30


def to_order(blocks):
    return jnp.concatenate([blocks[:, 0], blocks[::-1, 1]], axis=0)


def from_order(ordered):
    half_count = ordered.shape[0] // 2
    return jnp.stack([ordered[:half_count], ordered[half_count:][::-1]], axis=1)


def reference(queries, key_states, value_states, out_grad, segments):
    block_count = 2 * PAIRS
    window = (REACH + 1) * SPAN
    score_scale = HD ** -0.5
    query_rows = to_order(queries).reshape(block_count, SPAN, QH, HD)
    grad_rows = to_order(out_grad).reshape(block_count, SPAN, QH, HD)
    front = jnp.zeros((REACH * SPAN, HD), jnp.bfloat16)
    key_rows = jnp.concatenate([front, to_order(key_states).reshape(block_count * SPAN, HD)], axis=0)
    value_rows = jnp.concatenate([front, to_order(value_states).reshape(block_count * SPAN, HD)], axis=0)
    padded_seg = jnp.concatenate([jnp.full((REACH * SPAN,), -1, jnp.int32), segments.astype(jnp.int32)], axis=0)
    query_offsets = jnp.arange(SPAN, dtype=jnp.int32)
    key_offsets = jnp.arange(window, dtype=jnp.int32)

    def one_block(carry, block):
        key_acc, value_acc = carry
        start = block * SPAN
        query_tile = query_rows[block].astype(jnp.float32)
        grad_tile = grad_rows[block].astype(jnp.float32)
        key_tile = lax.dynamic_slice_in_dim(key_rows, start, window).astype(jnp.float32)
        value_tile = lax.dynamic_slice_in_dim(value_rows, start, window).astype(jnp.float32)
        query_seg = lax.dynamic_slice_in_dim(segments.astype(jnp.int32), start, SPAN)
        key_seg = lax.dynamic_slice_in_dim(padded_seg, start, window)
        query_pos = start + query_offsets
        key_pos = start - REACH * SPAN + key_offsets
        allowed = (query_seg[:, None] == key_seg[None, :]) & (key_pos[None, :] <= query_pos[:, None])
        scores = jnp.einsum("qhd,kd->hqk", query_tile, key_tile) * score_scale
        scores = jnp.where(allowed[None], scores, NEG_FILL)
        top_score = jnp.max(scores, axis=-1, keepdims=True)
        log_total = top_score + jnp.log(jnp.sum(jnp.exp(scores - top_score), axis=-1, keepdims=True))
        probs = jnp.exp(scores - log_total)
        weights = lax.optimization_barrier(probs.astype(jnp.bfloat16)).astype(jnp.float32)
        attended = jnp.einsum("hqk,kd->qhd", weights, value_tile).astype(jnp.bfloat16)
        delta = jnp.einsum("qhd,qhd->hq", grad_tile, attended.astype(jnp.float32))
        dot_grad = jnp.einsum("qhd,kd->hqk", grad_tile, value_tile)
        score_grad = lax.optimization_barrier((probs * (dot_grad - delta[:, :, None])).astype(jnp.bfloat16)).astype(jnp.float32)
        query_grad = (jnp.einsum("hqk,kd->qhd", score_grad, key_tile) * score_scale).astype(jnp.bfloat16)
        key_part = jnp.einsum("hqk,qhd->kd", score_grad, query_tile) * score_scale
        value_part = jnp.einsum("hqk,qhd->kd", weights, grad_tile)
        key_acc = lax.dynamic_update_slice_in_dim(key_acc, lax.dynamic_slice_in_dim(key_acc, start, window) + key_part, start, 0)
        value_acc = lax.dynamic_update_slice_in_dim(value_acc, lax.dynamic_slice_in_dim(value_acc, start, window) + value_part, start, 0)
        return (key_acc, value_acc), (attended.reshape(SPAN, QH * HD), query_grad.reshape(SPAN, QH * HD))

    zero_acc = jnp.zeros(((block_count + REACH) * SPAN, HD), jnp.float32)
    (key_acc, value_acc), (attended, query_grad) = lax.scan(one_block, (zero_acc, zero_acc), jnp.arange(block_count, dtype=jnp.int32))
    key_grad = from_order(key_acc[REACH * SPAN:].reshape(block_count, SPAN, HD)).astype(jnp.bfloat16)
    value_grad = from_order(value_acc[REACH * SPAN:].reshape(block_count, SPAN, HD)).astype(jnp.bfloat16)
    return from_order(attended), from_order(query_grad), key_grad, value_grad
```

```python
import jax
import jax.numpy as jnp
from jax import lax
from jax.experimental import pallas as pl
from jax.experimental.pallas import tpu as pltpu
from jax.sharding import PartitionSpec as P

REACH = 3
GROUP = 8
NEG_FILL = -1e30


def ring_pairs(ctx, step_even, step_odd):
    pairs = []
    for base in range(0, ctx, GROUP):
        for r in range(GROUP):
            chip, core = divmod(r, 2)
            move, target = (step_even, step_odd)[core]
            pairs.append((base + r, base + ((chip + move) % (GROUP // 2)) * 2 + target))
    return pairs


def halo_pairs(ctx):
    pairs = []
    for base in range(0, ctx, GROUP):
        for k in range(REACH):
            high = base + GROUP - 1 - k
            pairs.append((high, high + GROUP if base + GROUP < ctx else base + k))
            if base > 0:
                pairs.append((base + k, base + k - GROUP))
    return pairs


def inverse(pairs):
    return [(b, a) for a, b in pairs]


def attention_kernel(
    lo_ref, core_ref, seg_row, seg_col, q_own, g_own, qg_far, kv_own, kv_a, kv_b, kv_c, kv_d,
    out_own, out_far, p_own, p_a, p_b, p_c, p_d,
    keys, values, keys_t, values_t, scores, key_acc, value_acc, sems,
):
    tile = scores.shape[1]
    width = q_own.shape[1]
    shard = kv_a.shape[2]
    head_dim = q_own.shape[2]
    per_span = width // tile
    shards = kv_a.shape[0]
    scale = head_dim ** -0.5
    core = core_ref[0]
    f32, bf16 = jnp.float32, jnp.bfloat16

    copies = []
    for slot, source in enumerate((kv_d, kv_b, kv_c, kv_own, kv_a)):
        for which, target in enumerate((keys, values)):
            if source is kv_own:
                view = source.at[:, core, which]
            else:
                view = source.at[:, which]
            copy = pltpu.make_async_copy(
                view, target.at[pl.ds(slot * shards, shards)], sems.at[slot, which]
            )
            copy.start()
            copies.append(copy)
    key_acc[...] = jnp.zeros_like(key_acc)
    value_acc[...] = jnp.zeros_like(value_acc)
    for copy in copies:
        copy.wait()

    tile_shards = tile // shard

    def tile_of(ref, j):
        return ref[pl.ds(j * tile_shards, tile_shards)].reshape(tile, head_dim)

    key_tiles = keys.shape[0] // tile_shards
    for j in range(key_tiles):
        keys_t[j] = tile_of(keys, j).T
        values_t[j] = tile_of(values, j).T

    nt = (((1,), (1,)), ((), ()))
    nn = (((1,), (0,)), ((), ()))
    for i in range(2 * per_span):
        span, part = divmod(i, per_span)
        rows = pl.ds(part * tile, tile)
        if span == 0:
            query = q_own[core, rows]
            grad = g_own[core, rows]
        else:
            query = qg_far[0, rows]
            grad = qg_far[1, rows]
        diagonal = REACH * per_span + i
        lo = lo_ref[i]
        query_seg = seg_row[:, pl.ds(diagonal * tile, tile)]

        def score_tile(j, causal):
            raw = lax.dot_general(tile_of(keys, j), query, nt, preferred_element_type=f32) * scale
            if causal:
                allowed = seg_col[pl.ds(j * tile, tile), :] == query_seg
                at_key = lax.broadcasted_iota(jnp.int32, (tile, tile), 0)
                at_query = lax.broadcasted_iota(jnp.int32, (tile, tile), 1)
                allowed = allowed & (at_key <= at_query)
            else:
                start = pl.multiple_of(j * tile, tile)
                allowed = seg_col[pl.ds(start, tile), :] == query_seg
            raw = jnp.where(allowed, raw, NEG_FILL)
            scores[j] = raw
            return jnp.max(raw, axis=0, keepdims=True)

        top = score_tile(diagonal, True)
        top = lax.fori_loop(
            lo, diagonal, lambda j, m: jnp.maximum(m, score_tile(j, False)), top
        )

        def forward(j, carry):
            total, acc = carry
            prob = jnp.exp(scores[j] - top)
            scores[j] = prob
            total = total + jnp.sum(prob, axis=0, keepdims=True)
            acc = acc + lax.dot_general(
                values_t[j], prob.astype(bf16), nn, preferred_element_type=f32
            )
            return total, acc

        total, acc = lax.fori_loop(
            lo,
            diagonal + 1,
            forward,
            (jnp.zeros((1, tile), f32), jnp.zeros((head_dim, tile), f32)),
        )
        inv = 1.0 / total
        attended_t = (acc * inv).astype(bf16).astype(f32)
        attended = attended_t.T.astype(bf16)
        delta = jnp.sum(grad.astype(f32).T * attended_t, axis=0, keepdims=True)

        def backward(j, acc):
            prob = scores[j] * inv
            start = pl.multiple_of(j * tile, tile)
            here = pl.ds(start, tile)
            value_acc[here] += lax.dot_general(
                prob.astype(bf16), grad, nn, preferred_element_type=f32
            )
            dot_grad = lax.dot_general(tile_of(values, j), grad, nt, preferred_element_type=f32)
            score_grad = (prob * (dot_grad - delta)).astype(bf16)
            key_acc[here] += lax.dot_general(score_grad, query, nn, preferred_element_type=f32)
            return acc + lax.dot_general(keys_t[j], score_grad, nn, preferred_element_type=f32)

        acc = lax.fori_loop(lo, diagonal + 1, backward, jnp.zeros((head_dim, tile), f32))
        query_grad = (acc.T * scale).astype(bf16)
        target = out_own if span == 0 else out_far
        target[0, rows] = attended
        target[1, rows] = query_grad

    for slot, target in enumerate((p_d, p_b, p_c, p_own, p_a)):
        here = pl.ds(slot * width, width)
        target[0] = (key_acc[here] * scale).astype(target.dtype)
        target[1] = value_acc[here].astype(target.dtype)


def attention(lo, core, seg_window, queries, out_grad, far, kv_own, kv_a, kv_b, kv_c, kv_d):
    width, head_dim = queries.shape[1:]
    shards, _, shard, _ = kv_a.shape
    tile = max(min(256, width // 2), shard)
    window = (REACH + 2) * width
    part = jax.ShapeDtypeStruct((2, width, head_dim), jnp.bfloat16)
    own_part = jax.ShapeDtypeStruct((2, width, head_dim), jnp.float32)
    vmem = pl.BlockSpec(memory_space=pltpu.VMEM)
    smem = pl.BlockSpec(memory_space=pltpu.SMEM)
    hbm = pl.BlockSpec(memory_space=pl.ANY)
    return pl.pallas_call(
        attention_kernel,
        out_shape=(part, part, own_part, part, part, part, part),
        in_specs=[smem, smem] + [vmem] * 5 + [hbm] * 5,
        out_specs=[vmem] * 7,
        scratch_shapes=[
            pltpu.VMEM(((REACH + 2) * shards, shard, head_dim), jnp.bfloat16),
            pltpu.VMEM(((REACH + 2) * shards, shard, head_dim), jnp.bfloat16),
            pltpu.VMEM((window // tile, head_dim, tile), jnp.bfloat16),
            pltpu.VMEM((window // tile, head_dim, tile), jnp.bfloat16),
            pltpu.VMEM((window // tile, tile, tile), jnp.float32),
            pltpu.VMEM((window, head_dim), jnp.float32),
            pltpu.VMEM((window, head_dim), jnp.float32),
            pltpu.SemaphoreType.DMA((REACH + 2, 2)),
        ],
        compiler_params=pltpu.CompilerParams(vmem_limit_bytes=40 * 1024 * 1024),
        cost_estimate=pl.CostEstimate(
            flops=6 * 2 * 8 * width * width * head_dim,
            bytes_accessed=8 * 1024 * 1024,
            transcendentals=8 * width * width,
        ),
        name="attention",
    )(
        lo, core, seg_window[None, :], seg_window[:, None],
        queries, out_grad, far, kv_own, kv_a, kv_b, kv_c, kv_d,
    )


def body(queries, key_states, value_states, out_grad, segments):
    ctx = lax.axis_size("ctx")
    position = lax.axis_index("ctx")
    ring_place = position % GROUP
    chip, core = ring_place // 2, ring_place % 2
    chips = GROUP // 2
    width = queries.shape[2]
    heads = lax.axis_size("head")
    shard = key_states.shape[2]
    head_dim = key_states.shape[3]

    swap = ring_pairs(ctx, (0, 1), (0, 0))
    pairs_b = ring_pairs(ctx, (1, 0), (-1, 1))
    pairs_c = ring_pairs(ctx, (-1, 1), (1, 0))
    pairs_d = ring_pairs(ctx, (-2, 1), (2, 0))
    halo = halo_pairs(ctx)

    own = jnp.stack([key_states[0], value_states[0]], axis=1)
    sent = jnp.where(ring_place >= GROUP - REACH, own[0], own[1])
    edge = lax.ppermute(sent, "ctx", halo)
    mine = jnp.concatenate([own, edge[None]], axis=0)
    gathered = lax.all_to_all(
        jnp.broadcast_to(mine[None], (heads,) + mine.shape), "head", 0, 0, tiled=False
    )

    queries, out_grad = queries[0], out_grad[0]
    even = core == 0
    far = lax.ppermute(
        jnp.where(
            even,
            jnp.stack([queries[1], out_grad[1]]),
            jnp.stack([queries[0], out_grad[0]]),
        ),
        "ctx",
        swap,
    )

    own_half = jnp.where(even, gathered[:, 0], gathered[:, 1])
    far_half = jnp.where(even, gathered[:, 1], gathered[:, 0])
    kv_edge = gathered[:, 2]
    wrap_b = jnp.where(even, chip == chips - 1, chip == 0)
    wrap_c = jnp.where(even, chip == 0, chip == chips - 1)
    wrap_d = jnp.where(even, chip <= 1, chip >= chips - 2)
    kv_d = lax.ppermute(jnp.where(wrap_d, kv_edge, far_half), "ctx", pairs_d)
    kv_c = lax.ppermute(jnp.where(wrap_c, kv_edge, far_half), "ctx", pairs_c)
    kv_b = lax.ppermute(jnp.where(wrap_b, kv_edge, own_half), "ctx", pairs_b)
    kv_a = lax.ppermute(far_half, "ctx", swap)

    first = jnp.where(even, position, 2 * ctx - 1 - position)
    window = (REACH + 2) * width
    padded = jnp.concatenate([jnp.full((REACH * width,), -1, jnp.int32), segments])
    seg_window = lax.dynamic_slice_in_dim(padded, first * width, window)
    tile = max(min(256, width // 2), shard)
    heads_of_tiles = seg_window[REACH * width :: tile]
    lo = jnp.sum(seg_window[None, :] < heads_of_tiles[:, None], axis=1, dtype=jnp.int32) // tile

    out_own, out_far, p_own, p_a, p_b, p_c, p_d = attention(
        lo, core[None].astype(jnp.int32), seg_window, queries, out_grad, far,
        gathered, kv_a, kv_b, kv_c, kv_d,
    )

    r_d = lax.ppermute(p_d, "ctx", inverse(pairs_d)).astype(jnp.float32)
    r_c = lax.ppermute(p_c, "ctx", inverse(pairs_c)).astype(jnp.float32)
    r_b = lax.ppermute(p_b, "ctx", inverse(pairs_b)).astype(jnp.float32)
    r_a = lax.ppermute(p_a, "ctx", swap).astype(jnp.float32)
    back = lax.ppermute(out_far, "ctx", swap)

    own_sum = p_own + jnp.where(wrap_b, 0.0, r_b)
    far_sum = r_a + jnp.where(wrap_c, 0.0, r_c) + jnp.where(wrap_d, 0.0, r_d)
    edge_sum = (
        jnp.where(wrap_b, r_b, 0.0) + jnp.where(wrap_c, r_c, 0.0) + jnp.where(wrap_d, r_d, 0.0)
    )
    sums = jnp.stack(
        [jnp.where(even, own_sum, far_sum), jnp.where(even, far_sum, own_sum), edge_sum]
    ).astype(jnp.bfloat16)
    sums = sums.reshape(3, 2, heads, shard, head_dim).transpose(2, 0, 1, 3, 4)
    spread = lax.all_to_all(sums, "head", 0, 0, tiled=False)
    total = jnp.sum(spread.astype(jnp.float32), axis=0)
    returned = lax.ppermute(total[2].astype(jnp.bfloat16), "ctx", inverse(halo)).astype(jnp.float32)
    late = ring_place >= GROUP - REACH
    lower = total[0] + jnp.where(late, returned, 0.0)
    upper = total[1] + jnp.where(late, 0.0, returned)
    grads = jnp.stack([lower, upper]).astype(jnp.bfloat16)

    results = []
    for k in range(2):
        results.append(
            jnp.where(
                even, jnp.stack([out_own[k], back[k]]), jnp.stack([back[k], out_own[k]])
            )[None]
        )
    return results[0], results[1], grads[:, 0][None], grads[:, 1][None]


def solution(mesh):
    return jax.shard_map(
        body,
        mesh=mesh,
        in_specs=(
            P("ctx", None, None, "head"),
            P("ctx", None, "head", None),
            P("ctx", None, "head", None),
            P("ctx", None, None, "head"),
            P(),
        ),
        out_specs=(
            P("ctx", None, None, "head"),
            P("ctx", None, None, "head"),
            P("ctx", None, "head", None),
            P("ctx", None, "head", None),
        ),
        check_vma=False,
    )
```

```python
import math

import jax
import jax.numpy as jnp
from jax import lax
from jax.experimental import pallas as pl
from jax.experimental.pallas import tpu as pltpu
from jax.sharding import Mesh
from jax.sharding import PartitionSpec as P

REACH = 3
GROUP = 8
NEG_FILL = -1e30
CTX = ("pair", "core")


def within(ctx, moves):
    return [(base + a, base + b) for base in range(0, ctx, GROUP) for a, b in moves]


def swap_pairs(ctx):
    return within(ctx, [(r, r ^ 1) for r in range(GROUP)])


def near_pairs(ctx):
    forth = [(r, r + 2) for r in range(0, GROUP - 2, 2)]
    return within(ctx, forth + [(r, r - 2) for r in range(3, GROUP, 2)])


def next_pairs(ctx):
    forth = [(r, r + 4) for r in range(0, GROUP - 4, 2)]
    return within(ctx, forth + [(r, r - 4) for r in range(5, GROUP, 2)])


def edge_pairs(ctx, heads):
    moves = []
    for base in range(0, ctx, GROUP):
        for k in range(REACH):
            top = base + GROUP - 1 - k
            if base + GROUP < ctx:
                moves.append((top, base + GROUP + REACH - 1 - k))
            else:
                moves.append((top, base + GROUP - REACH + k))
            if base > 0:
                moves.append((base + k, base - REACH + k))
    return [
        (a * heads + h, b * heads + heads - 1 - h) for a, b in moves for h in range(heads)
    ]


def inverse(pairs):
    return [(b, a) for a, b in pairs]


def attention_kernel(
    lo_ref, place_ref, start_row, q_own, g_own, qg_far, kv_own, kv_near, kv_next, kv_edge,
    kv_edge1, kv_edge2, out_own, out_far, p_own, p_near, p_next,
    keys, values, keys_t, values_t, scores, key_acc, value_acc, sems,
):
    tile = scores.shape[1]
    width = q_own.shape[1]
    shard = kv_own.shape[3]
    head_dim = q_own.shape[2]
    per_span = width // tile
    shards = kv_own.shape[1]
    scale = head_dim ** -0.5
    core = place_ref[0]
    f32, bf16 = jnp.float32, jnp.bfloat16

    def copies(slot, source):
        return [
            pltpu.make_async_copy(
                source.at[:, which], target.at[pl.ds(slot * shards, shards)], sems.at[slot, which]
            )
            for which, target in enumerate((keys, values))
        ]

    def fetch(slot, source):
        for copy in copies(slot, source):
            copy.start()

    fetch(3, kv_own.at[core])
    fetch(4, kv_own.at[1 - core])

    @pl.when(place_ref[1] == 1)
    def _():
        fetch(0, kv_edge)

    @pl.when(place_ref[1] == 0)
    def _():
        fetch(0, kv_next)

    @pl.when(place_ref[2] == 1)
    def _():
        fetch(1, kv_edge2)
        fetch(2, kv_edge1)

    @pl.when(place_ref[2] == 0)
    def _():
        fetch(1, kv_near.at[core])
        fetch(2, kv_near.at[1 - core])

    key_acc[...] = jnp.zeros_like(key_acc)
    value_acc[...] = jnp.zeros_like(value_acc)
    for slot in range(REACH + 2):
        for copy in copies(slot, kv_edge):
            copy.wait()

    tile_shards = tile // shard

    def tile_of(ref, j):
        return ref[pl.ds(j * tile_shards, tile_shards)].reshape(tile, head_dim)

    key_tiles = keys.shape[0] // tile_shards
    for j in range(key_tiles):
        keys_t[j] = tile_of(keys, j).T
        values_t[j] = tile_of(values, j).T

    nt = (((1,), (1,)), ((), ()))
    nn = (((1,), (0,)), ((), ()))
    for i in range(2 * per_span):
        span, part = divmod(i, per_span)
        rows = pl.ds(part * tile, tile)
        if span == 0:
            query = q_own[core, rows]
            grad = g_own[core, rows]
        else:
            query = qg_far[0, rows]
            grad = qg_far[1, rows]
        diagonal = REACH * per_span + i
        lo = lo_ref[i]
        start = start_row[:, pl.ds(i * tile, tile)]

        def score_tile(j, causal):
            raw = lax.dot_general(
                tile_of(keys, j), query, nt, preferred_element_type=f32
            ) * (scale * math.log2(math.e))
            at_key = lax.broadcasted_iota(jnp.int32, (tile, tile), 0)
            allowed = at_key >= start - j * tile
            if causal:
                at_query = lax.broadcasted_iota(jnp.int32, (tile, tile), 1)
                allowed = allowed & (at_key <= at_query)
            raw = jnp.where(allowed, raw, NEG_FILL)
            scores[j] = raw
            return jnp.max(raw, axis=0, keepdims=True)

        top = score_tile(diagonal, True)
        top = lax.fori_loop(
            lo, diagonal, lambda j, m: jnp.maximum(m, score_tile(j, False)), top
        )

        def forward(j, carry):
            total, acc = carry
            prob = jnp.exp2(scores[j] - top)
            scores[j] = prob
            total = total + jnp.sum(prob, axis=0, keepdims=True)
            acc = acc + lax.dot_general(
                values_t[j], prob.astype(bf16), nn, preferred_element_type=f32
            )
            return total, acc

        total, acc = lax.fori_loop(
            lo,
            diagonal + 1,
            forward,
            (jnp.zeros((1, tile), f32), jnp.zeros((head_dim, tile), f32)),
        )
        inv = 1.0 / total
        attended_t = (acc * inv).astype(bf16).astype(f32)
        attended = attended_t.T.astype(bf16)
        delta = jnp.sum(grad.astype(f32).T * attended_t, axis=0, keepdims=True)

        def backward(j, acc):
            prob = scores[j] * inv
            here = pl.ds(pl.multiple_of(j * tile, tile), tile)
            value_acc[here] += lax.dot_general(
                prob.astype(bf16), grad, nn, preferred_element_type=f32
            )
            dot_grad = lax.dot_general(tile_of(values, j), grad, nt, preferred_element_type=f32)
            score_grad = (prob * (dot_grad - delta)).astype(bf16)
            key_acc[here] += lax.dot_general(score_grad, query, nn, preferred_element_type=f32)
            return acc + lax.dot_general(keys_t[j], score_grad, nn, preferred_element_type=f32)

        acc = lax.fori_loop(lo, diagonal + 1, backward, jnp.zeros((head_dim, tile), f32))
        query_grad = (acc.T * scale).astype(bf16)
        target = out_own if span == 0 else out_far
        target[0, rows] = attended
        target[1, rows] = query_grad

    targets = (p_next, p_near.at[0], p_near.at[1], p_own.at[0], p_own.at[1])
    for slot, target in enumerate(targets):
        here = pl.ds(slot * width, width)
        target[0] = (key_acc[here] * scale).astype(target.dtype)
        target[1] = value_acc[here].astype(target.dtype)


def attention(lo, place, start, queries, out_grad, far, kv_own, *kv_others):
    width, head_dim = queries.shape[1:]
    _, shards, _, shard, _ = kv_own.shape
    tile = max(min(256, width // 2), shard)
    window = (REACH + 2) * width
    part = (2, width, head_dim)
    vmem = pl.BlockSpec(memory_space=pltpu.VMEM)
    smem = pl.BlockSpec(memory_space=pltpu.SMEM)
    hbm = pl.BlockSpec(memory_space=pl.ANY)
    return pl.pallas_call(
        attention_kernel,
        out_shape=(
            jax.ShapeDtypeStruct(part, jnp.bfloat16),
            jax.ShapeDtypeStruct(part, jnp.bfloat16),
            jax.ShapeDtypeStruct((2,) + part, jnp.float32),
            jax.ShapeDtypeStruct((2,) + part, jnp.bfloat16),
            jax.ShapeDtypeStruct(part, jnp.bfloat16),
        ),
        in_specs=[smem, smem] + [vmem] * 4 + [hbm] * 6,
        out_specs=[vmem] * 5,
        scratch_shapes=[
            pltpu.VMEM(((REACH + 2) * shards, shard, head_dim), jnp.bfloat16),
            pltpu.VMEM(((REACH + 2) * shards, shard, head_dim), jnp.bfloat16),
            pltpu.VMEM((window // tile, head_dim, tile), jnp.bfloat16),
            pltpu.VMEM((window // tile, head_dim, tile), jnp.bfloat16),
            pltpu.VMEM((window // tile, tile, tile), jnp.float32),
            pltpu.VMEM((window, head_dim), jnp.float32),
            pltpu.VMEM((window, head_dim), jnp.float32),
            pltpu.SemaphoreType.DMA((REACH + 2, 2)),
        ],
        compiler_params=pltpu.CompilerParams(vmem_limit_bytes=40 * 1024 * 1024),
        cost_estimate=pl.CostEstimate(
            flops=6 * 2 * 8 * width * width * head_dim,
            bytes_accessed=8 * 1024 * 1024,
            transcendentals=8 * width * width,
        ),
        name="attention",
    )(lo, place, start[None, :], queries, out_grad, far, kv_own, *kv_others)


def body(queries, key_states, value_states, out_grad, segments):
    ctx = lax.axis_size("pair") * 2
    core = lax.axis_index("core")
    position = lax.axis_index("pair") * 2 + core
    place = position % GROUP
    width = queries.shape[2]
    heads = lax.axis_size("head")
    shard = key_states.shape[2]
    head_dim = key_states.shape[3]
    bf16, f32 = jnp.bfloat16, jnp.float32

    swap, near, far_chip = swap_pairs(ctx), near_pairs(ctx), next_pairs(ctx)
    edge1 = within(ctx, [(2, 0), (GROUP - 3, GROUP - 1)])
    edge2 = within(ctx, [(1, 0), (GROUP - 2, GROUP - 1)])
    edge = edge_pairs(ctx, heads)
    even = core == 0
    sends_lower = place >= GROUP - REACH

    own = jnp.stack([key_states[0], value_states[0]], axis=1)
    crossed = lax.ppermute(jnp.where(sends_lower, own[0], own[1]), CTX + ("head",), edge)

    spread = jnp.broadcast_to(own[:, None], (2, heads) + own.shape[1:])
    kv_own = lax.all_to_all(
        spread.reshape((2 * heads,) + own.shape[1:]), ("core", "head"), 0, 0, tiled=True
    ).reshape(spread.shape)
    crossed, kv_own = lax.optimization_barrier((crossed, kv_own))
    kv_edge = lax.all_to_all(
        jnp.broadcast_to(crossed[None], (heads,) + crossed.shape), "head", 0, 0, tiled=True
    )[::-1]

    queries, out_grad = queries[0], out_grad[0]
    far = lax.ppermute(
        jnp.where(
            even,
            jnp.stack([queries[1], out_grad[1]]),
            jnp.stack([queries[0], out_grad[0]]),
        ),
        CTX,
        swap,
    )

    kv_next = lax.ppermute(jnp.where(even, kv_own[1], kv_own[0]), CTX, far_chip)
    kv_near = lax.ppermute(kv_own, CTX, near)
    kv_edge1 = lax.ppermute(kv_edge, CTX, edge1)
    kv_edge2 = lax.ppermute(kv_edge, CTX, edge2)

    first = jnp.where(even, position, 2 * ctx - 1 - position)
    window = (REACH + 2) * width
    padded = jnp.concatenate([jnp.full((REACH * width,), -1, jnp.int32), segments])
    seg_window = lax.dynamic_slice_in_dim(padded, first * width, window)
    start = jnp.sum(
        seg_window[:, None] < seg_window[None, REACH * width :], axis=0, dtype=jnp.int32
    )
    tile = max(min(256, width // 2), shard)
    lo = start[::tile] // tile
    edge_next = jnp.where(even, place <= 2, place >= GROUP - 3)
    edge_near = jnp.where(even, place == 0, place == GROUP - 1)
    places = jnp.stack([core, edge_next, edge_near]).astype(jnp.int32)

    out_own, out_far, p_own, p_near, p_next = attention(
        lo, places, start, queries, out_grad, far,
        kv_own, kv_near, kv_next, kv_edge, kv_edge1, kv_edge2,
    )

    r_edge1 = lax.ppermute(p_near[1], CTX, inverse(edge1)).astype(f32)
    r_edge2 = lax.ppermute(p_near[0], CTX, inverse(edge2)).astype(f32)
    r_next = lax.ppermute(p_next, CTX, inverse(far_chip)).astype(f32)
    r_near = lax.ppermute(p_near, CTX, inverse(near)).astype(f32)

    edge_sum = jnp.where(edge_next, p_next.astype(f32), 0.0) + r_edge1 + r_edge2
    edge_sum = edge_sum.astype(bf16).reshape(2, heads, shard, head_dim)
    edge_heads = lax.all_to_all(
        edge_sum.transpose(1, 0, 2, 3)[::-1], "head", 0, 0, tiled=True
    )
    edge_total = jnp.sum(edge_heads.astype(f32), axis=0).astype(bf16)
    returned = lax.ppermute(edge_total, CTX + ("head",), inverse(edge)).astype(f32)

    sums = p_own + r_near
    sums = jnp.stack([sums[0], sums[1] + r_next])
    sums = jnp.where(even, sums, sums[::-1]).astype(bf16)
    sums = sums.reshape(2, 2, heads, shard, head_dim).transpose(0, 2, 1, 3, 4)
    by_head = lax.all_to_all(
        sums.reshape((2 * heads,) + own.shape[1:]), ("core", "head"), 0, 0, tiled=True
    ).reshape(spread.shape)
    total = jnp.sum(by_head.astype(f32), axis=1)
    lower = total[0] + jnp.where(sends_lower, returned, 0.0)
    upper = total[1] + jnp.where(sends_lower, 0.0, returned)
    grads = jnp.stack([lower, upper]).astype(bf16)

    back = lax.ppermute(out_far, CTX, swap)
    results = []
    for k in range(2):
        results.append(
            jnp.where(
                even, jnp.stack([out_own[k], back[k]]), jnp.stack([back[k], out_own[k]])
            )[None]
        )
    return results[0], results[1], grads[:, 0][None], grads[:, 1][None]


def solution(mesh):
    ctx, heads = mesh.devices.shape
    mesh = Mesh(mesh.devices.reshape(ctx // 2, 2, heads), CTX + ("head",))
    by_head = P(CTX, None, None, "head")
    by_row = P(CTX, None, "head", None)
    return jax.shard_map(
        body,
        mesh=mesh,
        in_specs=(by_head, by_row, by_row, by_head, P()),
        out_specs=(by_head, by_head, by_row, by_row),
        check_vma=False,
    )
```

```python
import math

import jax
import jax.numpy as jnp
from jax import lax
from jax.experimental import pallas as pl
from jax.experimental.pallas import tpu as pltpu
from jax.sharding import Mesh
from jax.sharding import PartitionSpec as P

REACH = 3
GROUP = 8
NEG_FILL = -1e30
CTX = ("pair", "core")


def within(ctx, moves):
    return [(base + a, base + b) for base in range(0, ctx, GROUP) for a, b in moves]


def swap_pairs(ctx):
    return within(ctx, [(r, r ^ 1) for r in range(GROUP)])


def near_pairs(ctx):
    forth = [(r, r + 2) for r in range(0, GROUP - 2, 2)]
    return within(ctx, forth + [(r, r - 2) for r in range(3, GROUP, 2)])


def next_pairs(ctx):
    forth = [(r, r + 4) for r in range(0, GROUP - 4, 2)]
    return within(ctx, forth + [(r, r - 4) for r in range(5, GROUP, 2)])


def edge_pairs(ctx, heads):
    moves = []
    for base in range(0, ctx, GROUP):
        for k in range(REACH):
            top = base + GROUP - 1 - k
            if base + GROUP < ctx:
                moves.append((top, base + GROUP + REACH - 1 - k))
            else:
                moves.append((top, base + GROUP - REACH + k))
            if base > 0:
                moves.append((base + k, base - REACH + k))
    return [
        (a * heads + h, b * heads + heads - 1 - h) for a, b in moves for h in range(heads)
    ]


def partners(ctx, heads, places, bit):
    return [
        ((base + r) * heads + h, (base + r) * heads + (h ^ bit))
        for base in range(0, ctx, GROUP)
        for r in places
        for h in range(heads)
    ]


def folds(heads):
    return [1 << k for k in reversed(range(heads.bit_length() - 1))]


def edge_order(heads):
    order = [0]
    for bit in folds(heads):
        order = order + [k | bit for k in order]
    return [heads - 1 - k for k in order]


def inverse(pairs):
    return [(b, a) for a, b in pairs]


def attention_kernel(
    lo_ref, place_ref, start_row, q_own, g_own, qg_far, kv_own, kv_near, kv_next, kv_edge,
    kv_edge1, kv_edge2, out_own, out_far, p_own, p_near, p_next,
    keys, values, keys_t, values_t, scores, key_acc, value_acc, sems,
):
    tile = scores.shape[1]
    width = q_own.shape[1]
    shard = kv_own.shape[3]
    head_dim = q_own.shape[2]
    per_span = width // tile
    shards = kv_own.shape[1]
    scale = head_dim ** -0.5
    core = place_ref[0]
    f32, bf16 = jnp.float32, jnp.bfloat16

    def copies(slot, source):
        return [
            pltpu.make_async_copy(
                source.at[:, which], target.at[pl.ds(slot * shards, shards)], sems.at[slot, which]
            )
            for which, target in enumerate((keys, values))
        ]

    def fetch(slot, source):
        for copy in copies(slot, source):
            copy.start()

    def fetch_edge(slot, source):
        for place, row in enumerate(edge_order(shards)):
            for which, target in enumerate((keys, values)):
                pltpu.make_async_copy(
                    source.at[place, which], target.at[slot * shards + row], sems.at[slot, which]
                ).start()

    fetch(3, kv_own.at[core])
    fetch(4, kv_own.at[1 - core])

    @pl.when(place_ref[1] == 1)
    def _():
        fetch_edge(0, kv_edge)

    @pl.when(place_ref[1] == 0)
    def _():
        fetch(0, kv_next)

    @pl.when(place_ref[2] == 1)
    def _():
        fetch_edge(1, kv_edge2)
        fetch_edge(2, kv_edge1)

    @pl.when(place_ref[2] == 0)
    def _():
        fetch(1, kv_near.at[core])
        fetch(2, kv_near.at[1 - core])

    key_acc[...] = jnp.zeros_like(key_acc)
    value_acc[...] = jnp.zeros_like(value_acc)
    for slot in range(REACH + 2):
        for copy in copies(slot, kv_edge):
            copy.wait()

    tile_shards = tile // shard

    def tile_of(ref, j):
        return ref[pl.ds(j * tile_shards, tile_shards)].reshape(tile, head_dim)

    key_tiles = keys.shape[0] // tile_shards
    for j in range(key_tiles):
        keys_t[j] = tile_of(keys, j).T
        values_t[j] = tile_of(values, j).T

    nt = (((1,), (1,)), ((), ()))
    nn = (((1,), (0,)), ((), ()))
    for i in range(2 * per_span):
        span, part = divmod(i, per_span)
        rows = pl.ds(part * tile, tile)
        if span == 0:
            query = q_own[core, rows]
            grad = g_own[core, rows]
        else:
            query = qg_far[0, rows]
            grad = qg_far[1, rows]
        diagonal = REACH * per_span + i
        lo = lo_ref[i]
        start = start_row[:, pl.ds(i * tile, tile)]

        def score_tile(j, causal):
            raw = lax.dot_general(
                tile_of(keys, j), query, nt, preferred_element_type=f32
            ) * (scale * math.log2(math.e))
            at_key = lax.broadcasted_iota(jnp.int32, (tile, tile), 0)
            allowed = at_key >= start - j * tile
            if causal:
                at_query = lax.broadcasted_iota(jnp.int32, (tile, tile), 1)
                allowed = allowed & (at_key <= at_query)
            raw = jnp.where(allowed, raw, NEG_FILL)
            scores[j] = raw
            return jnp.max(raw, axis=0, keepdims=True)

        top = score_tile(diagonal, True)
        top = lax.fori_loop(
            lo, diagonal, lambda j, m: jnp.maximum(m, score_tile(j, False)), top
        )

        def forward(j, carry):
            total, acc = carry
            prob = jnp.exp2(scores[j] - top)
            scores[j] = prob
            total = total + jnp.sum(prob, axis=0, keepdims=True)
            acc = acc + lax.dot_general(
                values_t[j], prob.astype(bf16), nn, preferred_element_type=f32
            )
            return total, acc

        total, acc = lax.fori_loop(
            lo,
            diagonal + 1,
            forward,
            (jnp.zeros((1, tile), f32), jnp.zeros((head_dim, tile), f32)),
        )
        inv = 1.0 / total
        attended_t = (acc * inv).astype(bf16).astype(f32)
        attended = attended_t.T.astype(bf16)
        delta = jnp.sum(grad.astype(f32).T * attended_t, axis=0, keepdims=True)

        def backward(j, acc):
            prob = scores[j] * inv
            here = pl.ds(pl.multiple_of(j * tile, tile), tile)
            value_acc[here] += lax.dot_general(
                prob.astype(bf16), grad, nn, preferred_element_type=f32
            )
            dot_grad = lax.dot_general(tile_of(values, j), grad, nt, preferred_element_type=f32)
            score_grad = (prob * (dot_grad - delta)).astype(bf16)
            key_acc[here] += lax.dot_general(score_grad, query, nn, preferred_element_type=f32)
            return acc + lax.dot_general(keys_t[j], score_grad, nn, preferred_element_type=f32)

        acc = lax.fori_loop(lo, diagonal + 1, backward, jnp.zeros((head_dim, tile), f32))
        query_grad = (acc.T * scale).astype(bf16)
        target = out_own if span == 0 else out_far
        target[0, rows] = attended
        target[1, rows] = query_grad

    targets = (p_next, p_near.at[0], p_near.at[1], p_own.at[0], p_own.at[1])
    for slot, target in enumerate(targets):
        here = pl.ds(slot * width, width)
        target[0] = (key_acc[here] * scale).astype(target.dtype)
        target[1] = value_acc[here].astype(target.dtype)


def attention(lo, place, start, queries, out_grad, far, kv_own, *kv_others):
    width, head_dim = queries.shape[1:]
    _, shards, _, shard, _ = kv_own.shape
    tile = max(min(256, width // 2), shard)
    window = (REACH + 2) * width
    part = (2, width, head_dim)
    vmem = pl.BlockSpec(memory_space=pltpu.VMEM)
    smem = pl.BlockSpec(memory_space=pltpu.SMEM)
    return pl.pallas_call(
        attention_kernel,
        out_shape=(
            jax.ShapeDtypeStruct(part, jnp.bfloat16),
            jax.ShapeDtypeStruct(part, jnp.bfloat16),
            jax.ShapeDtypeStruct((2,) + part, jnp.float32),
            jax.ShapeDtypeStruct((2,) + part, jnp.bfloat16),
            jax.ShapeDtypeStruct(part, jnp.bfloat16),
        ),
        in_specs=[smem, smem] + [vmem] * 10,
        out_specs=[vmem] * 5,
        scratch_shapes=[
            pltpu.VMEM(((REACH + 2) * shards, shard, head_dim), jnp.bfloat16),
            pltpu.VMEM(((REACH + 2) * shards, shard, head_dim), jnp.bfloat16),
            pltpu.VMEM((window // tile, head_dim, tile), jnp.bfloat16),
            pltpu.VMEM((window // tile, head_dim, tile), jnp.bfloat16),
            pltpu.VMEM((window // tile, tile, tile), jnp.float32),
            pltpu.VMEM((window, head_dim), jnp.float32),
            pltpu.VMEM((window, head_dim), jnp.float32),
            pltpu.SemaphoreType.DMA((REACH + 2, 2)),
        ],
        compiler_params=pltpu.CompilerParams(vmem_limit_bytes=24 * 1024 * 1024),
        cost_estimate=pl.CostEstimate(
            flops=6 * 2 * 8 * width * width * head_dim,
            bytes_accessed=8 * 1024 * 1024,
            transcendentals=8 * width * width,
        ),
        name="attention",
    )(lo, place, start[None, :], queries, out_grad, far, kv_own, *kv_others)


def body(queries, key_states, value_states, out_grad, segments):
    ctx = lax.axis_size("pair") * 2
    core = lax.axis_index("core")
    position = lax.axis_index("pair") * 2 + core
    place = position % GROUP
    width = queries.shape[2]
    heads = lax.axis_size("head")
    shard = key_states.shape[2]
    head_dim = key_states.shape[3]
    bf16, f32 = jnp.bfloat16, jnp.float32

    swap, near, far_chip = swap_pairs(ctx), near_pairs(ctx), next_pairs(ctx)
    edge1 = within(ctx, [(2, 0), (GROUP - 3, GROUP - 1)])
    edge2 = within(ctx, [(1, 0), (GROUP - 2, GROUP - 1)])
    edge = edge_pairs(ctx, heads)
    even = core == 0
    sends_lower = place >= GROUP - REACH

    own = jnp.stack([key_states[0], value_states[0]], axis=1)
    crossed = lax.ppermute(jnp.where(sends_lower, own[0], own[1]), CTX + ("head",), edge)

    spread = jnp.broadcast_to(own[:, None], (2, heads) + own.shape[1:])
    kv_own = lax.all_to_all(
        spread.reshape((2 * heads,) + own.shape[1:]), ("core", "head"), 0, 0, tiled=True
    ).reshape(spread.shape)
    head = lax.axis_index("head")
    holders = [r for r in range(GROUP) if r < REACH or r >= GROUP - REACH]
    kv_edge = crossed[None]
    for bit in folds(heads):
        other = lax.ppermute(kv_edge, CTX + ("head",), partners(ctx, heads, holders, bit))
        high = (head & bit) != 0
        kv_edge = jnp.concatenate(
            [jnp.where(high, other, kv_edge), jnp.where(high, kv_edge, other)]
        )

    queries, out_grad = queries[0], out_grad[0]
    far = lax.ppermute(
        jnp.where(
            even,
            jnp.stack([queries[1], out_grad[1]]),
            jnp.stack([queries[0], out_grad[0]]),
        ),
        CTX,
        swap,
    )

    kv_next = lax.ppermute(jnp.where(even, kv_own[1], kv_own[0]), CTX, far_chip)
    kv_near = lax.ppermute(kv_own, CTX, near)
    kv_edge1 = lax.ppermute(kv_edge, CTX, edge1)
    kv_edge2 = lax.ppermute(kv_edge, CTX, edge2)

    first = jnp.where(even, position, 2 * ctx - 1 - position)
    window = (REACH + 2) * width
    padded = jnp.concatenate([jnp.full((REACH * width,), -1, jnp.int32), segments])
    seg_window = lax.dynamic_slice_in_dim(padded, first * width, window)
    start = jnp.sum(
        seg_window[:, None] < seg_window[None, REACH * width :], axis=0, dtype=jnp.int32
    )
    tile = max(min(256, width // 2), shard)
    lo = start[::tile] // tile
    edge_next = jnp.where(even, place <= 2, place >= GROUP - 3)
    edge_near = jnp.where(even, place == 0, place == GROUP - 1)
    places = jnp.stack([core, edge_next, edge_near]).astype(jnp.int32)

    out_own, out_far, p_own, p_near, p_next = attention(
        lo, places, start, queries, out_grad, far,
        kv_own, kv_near, kv_next, kv_edge, kv_edge1, kv_edge2,
    )

    r_edge1 = lax.ppermute(p_near[1], CTX, inverse(edge1)).astype(f32)
    r_edge2 = lax.ppermute(p_near[0], CTX, inverse(edge2)).astype(f32)
    r_next = lax.ppermute(p_next, CTX, inverse(far_chip)).astype(f32)
    r_near = lax.ppermute(p_near, CTX, inverse(near)).astype(f32)

    edge_sum = jnp.where(edge_next, p_next.astype(f32), 0.0) + r_edge1 + r_edge2
    edge_sum = edge_sum.reshape(2, heads, shard, head_dim).transpose(1, 0, 2, 3)[::-1]
    for bit in reversed(folds(heads)):
        halves = edge_sum.reshape((-1, 2) + edge_sum.shape[1:])
        lower, upper = halves[:, 0], halves[:, 1]
        high = (head & bit) != 0
        away = jnp.where(high, lower, upper).astype(bf16)
        other = lax.ppermute(away, CTX + ("head",), partners(ctx, heads, holders, bit))
        edge_sum = jnp.where(high, upper, lower) + other.astype(f32)
    edge_total = edge_sum[0].astype(bf16)
    returned = lax.ppermute(edge_total, CTX + ("head",), inverse(edge)).astype(f32)

    sums = p_own + r_near
    sums = jnp.stack([sums[0], sums[1] + r_next])
    sums = jnp.where(even, sums, sums[::-1]).astype(bf16)
    sums = sums.reshape(2, 2, heads, shard, head_dim).transpose(0, 2, 1, 3, 4)
    by_head = lax.all_to_all(
        sums.reshape((2 * heads,) + own.shape[1:]), ("core", "head"), 0, 0, tiled=True
    ).reshape(spread.shape)
    total = jnp.sum(by_head.astype(f32), axis=1)
    lower = total[0] + jnp.where(sends_lower, returned, 0.0)
    upper = total[1] + jnp.where(sends_lower, 0.0, returned)
    grads = jnp.stack([lower, upper]).astype(bf16)

    back = lax.ppermute(out_far, CTX, swap)
    results = []
    for k in range(2):
        results.append(
            jnp.where(
                even, jnp.stack([out_own[k], back[k]]), jnp.stack([back[k], out_own[k]])
            )[None]
        )
    return results[0], results[1], grads[:, 0][None], grads[:, 1][None]


def solution(mesh):
    ctx, heads = mesh.devices.shape
    mesh = Mesh(mesh.devices.reshape(ctx // 2, 2, heads), CTX + ("head",))
    by_head = P(CTX, None, None, "head")
    by_row = P(CTX, None, "head", None)
    return jax.shard_map(
        body,
        mesh=mesh,
        in_specs=(by_head, by_row, by_row, by_head, P()),
        out_specs=(by_head, by_head, by_row, by_row),
        check_vma=False,
    )
```

```python
import math

import jax
import jax.numpy as jnp
from jax import lax
from jax.experimental import pallas as pl
from jax.experimental.pallas import tpu as pltpu
from jax.sharding import Mesh
from jax.sharding import PartitionSpec as P

REACH = 3
GROUP = 8
NEG_FILL = -1e30
CTX = ("pair", "core")


def within(ctx, moves):
    return [(base + a, base + b) for base in range(0, ctx, GROUP) for a, b in moves]


def swap_pairs(ctx):
    return within(ctx, [(r, r ^ 1) for r in range(GROUP)])


def near_pairs(ctx):
    forth = [(r, r + 2) for r in range(0, GROUP - 2, 2)]
    return within(ctx, forth + [(r, r - 2) for r in range(3, GROUP, 2)])


def next_pairs(ctx):
    forth = [(r, r + 4) for r in range(0, GROUP - 4, 2)]
    return within(ctx, forth + [(r, r - 4) for r in range(5, GROUP, 2)])


def edge_pairs(ctx, heads):
    moves = []
    for base in range(0, ctx, GROUP):
        for k in range(REACH):
            top = base + GROUP - 1 - k
            if base + GROUP < ctx:
                moves.append((top, base + GROUP + REACH - 1 - k))
            else:
                moves.append((top, base + GROUP - REACH + k))
            if base > 0:
                moves.append((base + k, base - REACH + k))
    return [
        (a * heads + h, b * heads + h) for a, b in moves for h in range(heads)
    ]


def inverse(pairs):
    return [(b, a) for a, b in pairs]


NT = (((1,), (1,)), ((), ()))
NN = (((1,), (0,)), ((), ()))


def matmul(a, b, dims=NN):
    return lax.dot_general(a, b, dims, preferred_element_type=jnp.float32)


def key_tile(ref, j, which, tile):
    _, shards, _, shard, head_dim = ref.shape
    per_span = shards * shard // tile
    rows = pl.ds((j % per_span) * (tile // shard), tile // shard)
    return ref[j // per_span, rows, which].reshape(tile, head_dim)


def query_tile(own_ref, far_ref, far_index, core, i, tile):
    width = far_ref.shape[1]
    span, part = divmod(i, width // tile)
    rows = pl.ds(part * tile, tile)
    return own_ref[core, rows] if span == 0 else far_ref[far_index, rows]


def masked_scores(keys, query, start, j, tile, causal):
    raw = matmul(keys, query, NT) * (query.shape[1] ** -0.5 * math.log2(math.e))
    at_key = lax.broadcasted_iota(jnp.int32, raw.shape, 0)
    allowed = at_key >= start - j * tile
    if causal:
        allowed = allowed & (at_key <= lax.broadcasted_iota(jnp.int32, raw.shape, 1))
    return jnp.where(allowed, raw, NEG_FILL)


def column_max(a):
    return jnp.max(a, axis=0, keepdims=True)


def column_sum(a):
    return jnp.sum(a, axis=0, keepdims=True)


def own_forward_kernel(
    lo_ref, place_ref, start_row, queries, far, kv_own, top_row, total_row, acc_out,
    keys, values, values_t, scores,
):
    tile, tiles = scores.shape[1], scores.shape[0]
    core = place_ref[0]
    before = REACH * tiles // 2
    for j in range(tiles):
        span = core if j < tiles // 2 else 1 - core
        rows = pl.ds(j % (tiles // 2) * (tile // kv_own.shape[3]), tile // kv_own.shape[3])
        keys[j] = kv_own[span, rows, 0].reshape(keys.shape[1:])
        values_t[j] = kv_own[span, rows, 1].reshape(keys.shape[1:]).T
    for i in range(tiles):
        columns = pl.ds(i * tile, tile)
        query = query_tile(queries, far, 0, core, i, tile)
        start = start_row[:, columns]
        lo = jnp.maximum(lo_ref[i] - before, 0)

        def score_tile(j, causal):
            raw = masked_scores(keys[j], query, start, j + before, tile, causal)
            scores[j] = raw
            return column_max(raw)

        top = lax.fori_loop(
            lo, i, lambda j, m: jnp.maximum(m, score_tile(j, False)), score_tile(i, True)
        )

        def forward(j, carry):
            total, acc = carry
            prob = jnp.exp2(scores[j] - top)
            return total + column_sum(prob), acc + matmul(values_t[j], prob.astype(jnp.bfloat16))

        total, acc = lax.fori_loop(
            lo, i + 1, forward, (jnp.zeros_like(top), jnp.zeros(acc_out.shape[1:], jnp.float32))
        )
        top_row[:, columns] = top
        total_row[:, columns] = total
        acc_out[i] = acc


def earlier_kernel(
    lo_ref, place_ref, start_row, queries, out_grad, far, top_row, total_row, acc_in, kv_prev,
    attended_out, lse_row, delta_row, acc_out, p_near, p_next,
    keys_t, values_t, scores, key_acc, value_acc,
):
    tile, before = scores.shape[1], scores.shape[0]
    tiles = acc_in.shape[0]
    scale = queries.shape[2] ** -0.5
    core = place_ref[0]
    bf16, f32 = jnp.bfloat16, jnp.float32
    first = lo_ref[0]

    @pl.when(first < before)
    def _():
        key_acc[...] = jnp.zeros_like(key_acc)
        value_acc[...] = jnp.zeros_like(value_acc)

        def turn(j, carry):
            keys_t[j] = key_tile(kv_prev, j, 0, tile).T
            values_t[j] = key_tile(kv_prev, j, 1, tile).T
            return carry

        lax.fori_loop(first, before, turn, 0)

    for i in range(tiles):
        columns = pl.ds(i * tile, tile)
        query = query_tile(queries, far, 0, core, i, tile)
        grad = query_tile(out_grad, far, 1, core, i, tile)
        start = start_row[:, columns]
        lo = jnp.minimum(lo_ref[i], before)
        own_top = top_row[:, columns]

        def score_tile(j, top):
            raw = masked_scores(key_tile(kv_prev, j, 0, tile), query, start, j, tile, False)
            scores[j] = raw
            return jnp.maximum(top, column_max(raw))

        top = lax.fori_loop(lo, before, score_tile, own_top)
        shrink = jnp.exp2(own_top - top)

        def forward(j, carry):
            total, acc = carry
            prob = jnp.exp2(scores[j] - top)
            scores[j] = prob
            return total + column_sum(prob), acc + matmul(values_t[j], prob.astype(bf16))

        total, acc = lax.fori_loop(
            lo, before, forward, (total_row[:, columns] * shrink, acc_in[i] * shrink)
        )
        inv = 1.0 / total
        attended_t = (acc * inv).astype(bf16).astype(f32)
        delta = column_sum(grad.astype(f32).T * attended_t)
        half, part = divmod(i, tiles // 2)
        attended_out[half, pl.ds(part * tile, tile)] = attended_t.T.astype(bf16)
        lse_row[:, columns] = top + jnp.log2(total)
        delta_row[:, columns] = delta

        def backward(j, acc):
            prob = scores[j] * inv
            here = pl.ds(pl.multiple_of(j * tile, tile), tile)
            value_acc[here] += matmul(prob.astype(bf16), grad)
            dot_grad = matmul(key_tile(kv_prev, j, 1, tile), grad, NT)
            score_grad = (prob * (dot_grad - delta)).astype(bf16)
            key_acc[here] += matmul(score_grad, query)
            return acc + matmul(keys_t[j], score_grad)

        acc_out[i] = lax.fori_loop(lo, before, backward, jnp.zeros(acc_out.shape[1:], f32))

    shards, shard = kv_prev.shape[1], kv_prev.shape[3]

    @pl.when(first < before)
    def _():
        for slot, target in enumerate((p_next, p_near.at[0], p_near.at[1])):
            for row in range(shards):
                here = pl.ds((slot * shards + row) * shard, shard)
                target[row, 0] = (key_acc[here] * scale).astype(bf16)
                target[row, 1] = value_acc[here].astype(bf16)

    @pl.when(first >= before)
    def _():
        p_next[...] = jnp.zeros_like(p_next)
        p_near[...] = jnp.zeros_like(p_near)


def own_backward_kernel(
    lo_ref, place_ref, start_row, queries, out_grad, far, kv_own, attended, lse_row, delta_row,
    acc_in, out_own, out_far, p_own,
    keys, values, keys_t, key_acc, value_acc,
):
    tiles, tile = keys.shape[0], keys.shape[1]
    scale = queries.shape[2] ** -0.5
    core = place_ref[0]
    bf16, f32 = jnp.bfloat16, jnp.float32
    before = REACH * tiles // 2
    for j in range(tiles):
        span = core if j < tiles // 2 else 1 - core
        rows = pl.ds(j % (tiles // 2) * (tile // kv_own.shape[3]), tile // kv_own.shape[3])
        block = kv_own[span, rows, 0].reshape(keys.shape[1:])
        keys[j] = block
        keys_t[j] = block.T
        values[j] = kv_own[span, rows, 1].reshape(keys.shape[1:])
    key_acc[...] = jnp.zeros_like(key_acc)
    value_acc[...] = jnp.zeros_like(value_acc)
    for i in range(tiles):
        columns = pl.ds(i * tile, tile)
        query = query_tile(queries, far, 0, core, i, tile)
        grad = query_tile(out_grad, far, 1, core, i, tile)
        start = start_row[:, columns]
        lse, delta = lse_row[:, columns], delta_row[:, columns]

        def backward(j, acc, causal):
            raw = masked_scores(keys[j], query, start, j + before, tile, causal)
            prob = jnp.exp2(raw - lse)
            value_acc[j] += matmul(prob.astype(bf16), grad)
            score_grad = (prob * (matmul(values[j], grad, NT) - delta)).astype(bf16)
            key_acc[j] += matmul(score_grad, query)
            return acc + matmul(keys_t[j], score_grad)

        acc = backward(i, acc_in[i], True)
        acc = lax.fori_loop(
            jnp.maximum(lo_ref[i] - before, 0), i, lambda j, acc: backward(j, acc, False), acc
        )
        half, part = divmod(i, tiles // 2)
        rows = pl.ds(part * tile, tile)
        (out_own, out_far)[half][1, rows] = (acc.T * scale).astype(bf16)
    out_own[0] = attended[0]
    out_far[0] = attended[1]
    shards, shard = kv_own.shape[1], kv_own.shape[3]
    for span in range(2):
        for row in range(shards):
            j, part = divmod((span * shards + row) * shard, tile)
            here = pl.ds(part, shard)
            p_own[span, row, 0] = key_acc[j, here] * scale
            p_own[span, row, 1] = value_acc[j, here]


def vmem_kernel(kernel, name, outputs, scratch, tiles, tile, head_dim, matmuls):
    def call(*operands):
        rest = [pl.BlockSpec(memory_space=pltpu.VMEM)] * (len(operands) - 2)
        return pl.pallas_call(
            kernel,
            out_shape=outputs,
            in_specs=[pl.BlockSpec(memory_space=pltpu.SMEM)] * 2 + rest,
            out_specs=[pl.BlockSpec(memory_space=pltpu.VMEM)] * len(outputs),
            scratch_shapes=[pltpu.VMEM(shape, dtype) for shape, dtype in scratch],
            compiler_params=pltpu.CompilerParams(vmem_limit_bytes=24 * 1024 * 1024),
            cost_estimate=pl.CostEstimate(
                flops=2 * matmuls * tiles * tile * tile * head_dim,
                bytes_accessed=4 * 1024 * 1024,
                transcendentals=tiles * tile * tile,
            ),
            name=name,
        )(*operands)

    return call


def body(queries, key_states, value_states, out_grad, segments):
    ctx = lax.axis_size("pair") * 2
    core = lax.axis_index("core")
    position = lax.axis_index("pair") * 2 + core
    place = position % GROUP
    width = queries.shape[2]
    heads = lax.axis_size("head")
    shard = key_states.shape[2]
    head_dim = key_states.shape[3]
    bf16, f32 = jnp.bfloat16, jnp.float32

    swap, near, far_chip = swap_pairs(ctx), near_pairs(ctx), next_pairs(ctx)
    edge1 = within(ctx, [(2, 0), (GROUP - 3, GROUP - 1)])
    edge2 = within(ctx, [(1, 0), (GROUP - 2, GROUP - 1)])
    edge = edge_pairs(ctx, heads)
    even = core == 0
    sends_lower = place >= GROUP - REACH

    own = jnp.stack([key_states[0], value_states[0]], axis=1)
    crossed = lax.ppermute(jnp.where(sends_lower, own[0], own[1]), CTX + ("head",), edge)

    spread = jnp.broadcast_to(own[:, None], (2, heads) + own.shape[1:])
    kv_own = lax.all_to_all(
        spread.reshape((2 * heads,) + own.shape[1:]), ("core", "head"), 0, 0, tiled=True
    ).reshape(spread.shape)
    crossed, kv_own = lax.optimization_barrier((crossed, kv_own))
    kv_edge = lax.all_to_all(
        jnp.broadcast_to(crossed[None], (heads,) + crossed.shape), "head", 0, 0, tiled=True
    )

    queries, out_grad = queries[0], out_grad[0]
    far = lax.ppermute(
        jnp.where(
            even,
            jnp.stack([queries[1], out_grad[1]]),
            jnp.stack([queries[0], out_grad[0]]),
        ),
        CTX,
        swap,
    )

    kv_next = lax.ppermute(jnp.where(even, kv_own[1], kv_own[0]), CTX, far_chip)
    kv_near = lax.ppermute(kv_own, CTX, near)
    kv_edge1 = lax.ppermute(kv_edge, CTX, edge1)
    kv_edge2 = lax.ppermute(kv_edge, CTX, edge2)

    first = jnp.where(even, position, 2 * ctx - 1 - position)
    window = (REACH + 2) * width
    padded = jnp.concatenate([jnp.full((REACH * width,), -1, jnp.int32), segments])
    seg_window = lax.dynamic_slice_in_dim(padded, first * width, window)
    start = jnp.sum(
        seg_window[:, None] < seg_window[None, REACH * width :], axis=0, dtype=jnp.int32
    )
    tile = max(min(256, width // 2), shard)
    tiles, earlier = 2 * width // tile, REACH * width // tile
    lo = start[::tile] // tile
    edge_next = jnp.where(even, place <= 2, place >= GROUP - 3)
    edge_near = jnp.where(even, place == 0, place == GROUP - 1)
    places = core[None].astype(jnp.int32)
    start = start[None, :]

    near_ordered = jnp.where(even, kv_near, kv_near[::-1])
    kv_prev = jnp.stack(
        [
            jnp.where(edge_next, kv_edge, kv_next),
            jnp.where(edge_near, kv_edge2, near_ordered[0]),
            jnp.where(edge_near, kv_edge1, near_ordered[1]),
        ]
    )

    row = jax.ShapeDtypeStruct((1, 2 * width), f32)
    turned = jax.ShapeDtypeStruct((tiles, head_dim, tile), f32)
    part = jax.ShapeDtypeStruct((2, width, head_dim), bf16)
    span_like = kv_next.shape
    natural = ((tiles, tile, head_dim), bf16)
    top, total, acc = vmem_kernel(
        own_forward_kernel, "own_forward", (row, row, turned),
        [natural, natural, ((tiles, head_dim, tile), bf16), ((tiles, tile, tile), f32)],
        6, tile, head_dim, 2,
    )(lo, places, start, queries, far, kv_own)
    attended, lse, delta, acc, p_near, p_next = vmem_kernel(
        earlier_kernel, "earlier",
        (
            part, row, row, turned,
            jax.ShapeDtypeStruct((2,) + span_like, bf16),
            jax.ShapeDtypeStruct(span_like, bf16),
        ),
        [
            ((earlier, head_dim, tile), bf16),
            ((earlier, head_dim, tile), bf16),
            ((earlier, tile, tile), f32),
            ((earlier * tile, head_dim), f32),
            ((earlier * tile, head_dim), f32),
        ],
        6, tile, head_dim, 6,
    )(lo, places, start, queries, out_grad, far, top, total, acc, kv_prev)

    r_edge1 = lax.ppermute(p_near[1], CTX, inverse(edge1)).astype(f32)
    r_edge2 = lax.ppermute(p_near[0], CTX, inverse(edge2)).astype(f32)
    r_next = lax.ppermute(p_next, CTX, inverse(far_chip)).astype(f32)
    r_near = lax.ppermute(p_near, CTX, inverse(near)).astype(f32)

    out_own, out_far, p_own = vmem_kernel(
        own_backward_kernel, "own_backward",
        (part, part, jax.ShapeDtypeStruct((2,) + span_like, f32)),
        [natural, natural, ((tiles, head_dim, tile), bf16)]
        + [((tiles, tile, head_dim), f32)] * 2,
        6, tile, head_dim, 5,
    )(lo, places, start, queries, out_grad, far, kv_own, attended, lse, delta, acc)

    edge_sum = jnp.where(edge_next, p_next.astype(f32), 0.0) + r_edge1 + r_edge2
    edge_heads = lax.all_to_all(edge_sum.astype(bf16), "head", 0, 0, tiled=True)
    edge_total = jnp.sum(edge_heads.astype(f32), axis=0).astype(bf16)
    returned = lax.ppermute(edge_total, CTX + ("head",), inverse(edge)).astype(f32)

    sums = p_own + r_near
    sums = jnp.stack([sums[0], sums[1] + r_next])
    sums = jnp.where(even, sums, sums[::-1]).astype(bf16)
    by_head = lax.all_to_all(
        sums.reshape((2 * heads,) + own.shape[1:]), ("core", "head"), 0, 0, tiled=True
    ).reshape(spread.shape)
    total = jnp.sum(by_head.astype(f32), axis=1)
    lower = total[0] + jnp.where(sends_lower, returned, 0.0)
    upper = total[1] + jnp.where(sends_lower, 0.0, returned)
    grads = jnp.stack([lower, upper]).astype(bf16)

    back = lax.ppermute(out_far, CTX, swap)
    results = []
    for k in range(2):
        results.append(
            jnp.where(
                even, jnp.stack([out_own[k], back[k]]), jnp.stack([back[k], out_own[k]])
            )[None]
        )
    return results[0], results[1], grads[:, 0][None], grads[:, 1][None]


def solution(mesh):
    ctx, heads = mesh.devices.shape
    mesh = Mesh(mesh.devices.reshape(ctx // 2, 2, heads), CTX + ("head",))
    by_head = P(CTX, None, None, "head")
    by_row = P(CTX, None, "head", None)
    return jax.shard_map(
        body,
        mesh=mesh,
        in_specs=(by_head, by_row, by_row, by_head, P()),
        out_specs=(by_head, by_head, by_row, by_row),
        check_vma=False,
    )
```

```python
import math

import jax
import jax.numpy as jnp
from jax import lax
from jax.experimental import pallas as pl
from jax.experimental.pallas import tpu as pltpu
from jax.sharding import Mesh
from jax.sharding import PartitionSpec as P

REACH = 3
GROUP = 8
NEG_FILL = -1e30
CTX = ("pair", "core")


def within(ctx, moves):
    return [(base + a, base + b) for base in range(0, ctx, GROUP) for a, b in moves]


def swap_pairs(ctx):
    return within(ctx, [(r, r ^ 1) for r in range(GROUP)])


def near_pairs(ctx):
    forth = [(r, r + 2) for r in range(0, GROUP - 2, 2)]
    return within(ctx, forth + [(r, r - 2) for r in range(3, GROUP, 2)])


def next_pairs(ctx):
    forth = [(r, r + 4) for r in range(0, GROUP - 4, 2)]
    return within(ctx, forth + [(r, r - 4) for r in range(5, GROUP, 2)])


def head_pairs(ctx, heads, bit):
    return [(d, d ^ bit) for d in range(ctx * heads)]


def edge_pairs(ctx, heads, flip):
    moves = []
    for base in range(0, ctx, GROUP):
        for k in range(REACH):
            top = base + GROUP - 1 - k
            if base + GROUP < ctx:
                moves.append((top, base + GROUP + REACH - 1 - k))
            else:
                moves.append((top, base + GROUP - REACH + k))
            if base > 0:
                moves.append((base + k, base - REACH + k))
    return [
        (a * heads + h, b * heads + (h ^ flip)) for a, b in moves for h in range(heads)
    ]


def folds(heads):
    return [1 << k for k in reversed(range(heads.bit_length() - 1))]


def pick(bit, low, high):
    return jnp.where(bit, high, low)


def by_bit(bit, mine, other, axis):
    mine, other = jnp.expand_dims(mine, axis), jnp.expand_dims(other, axis)
    place = lax.broadcasted_iota(jnp.int32, (2,) + (1,) * (mine.ndim - axis - 1), 0)
    return jnp.where(place == bit.astype(jnp.int32), mine, other)


def inverse(pairs):
    return [(b, a) for a, b in pairs]


NT = (((1,), (1,)), ((), ()))
NN = (((1,), (0,)), ((), ()))


def matmul(a, b, dims=NN):
    return lax.dot_general(a, b, dims, preferred_element_type=jnp.float32)


def key_tile(ref, j, which, tile):
    _, shards, _, shard, head_dim = ref.shape
    per_span = shards * shard // tile
    rows = pl.ds((j % per_span) * (tile // shard), tile // shard)
    return ref[j // per_span, rows, which].reshape(tile, head_dim)


def query_tile(own_ref, far_ref, far_index, core, i, tile):
    width = far_ref.shape[1]
    span, part = divmod(i, width // tile)
    rows = pl.ds(part * tile, tile)
    return own_ref[core, rows] if span == 0 else far_ref[far_index, rows]


def masked_scores(keys, query, start, j, tile, causal):
    raw = matmul(keys, query, NT) * (query.shape[1] ** -0.5 * math.log2(math.e))
    at_key = lax.broadcasted_iota(jnp.int32, raw.shape, 0)
    allowed = at_key >= start - j * tile
    if causal:
        allowed = allowed & (at_key <= lax.broadcasted_iota(jnp.int32, raw.shape, 1))
    return jnp.where(allowed, raw, NEG_FILL)


def column_max(a):
    return jnp.max(a, axis=0, keepdims=True)


def column_sum(a):
    return jnp.sum(a, axis=0, keepdims=True)


def own_forward_kernel(
    lo_ref, place_ref, start_row, queries, far, kv_own, top_row, total_row, acc_out,
    keys, values, values_t, scores,
):
    tile, tiles = scores.shape[1], scores.shape[0]
    core = place_ref[0]
    before = REACH * tiles // 2
    for j in range(tiles):
        span = core if j < tiles // 2 else 1 - core
        rows = pl.ds(j % (tiles // 2) * (tile // kv_own.shape[3]), tile // kv_own.shape[3])
        keys[j] = kv_own[span, rows, 0].reshape(keys.shape[1:])
        values_t[j] = kv_own[span, rows, 1].reshape(keys.shape[1:]).T
    for i in range(tiles):
        columns = pl.ds(i * tile, tile)
        query = query_tile(queries, far, 0, core, i, tile)
        start = start_row[:, columns]
        lo = jnp.maximum(lo_ref[i] - before, 0)

        def score_tile(j, causal):
            raw = masked_scores(keys[j], query, start, j + before, tile, causal)
            scores[j] = raw
            return column_max(raw)

        top = lax.fori_loop(
            lo, i, lambda j, m: jnp.maximum(m, score_tile(j, False)), score_tile(i, True)
        )

        def forward(j, carry):
            total, acc = carry
            prob = jnp.exp2(scores[j] - top)
            return total + column_sum(prob), acc + matmul(values_t[j], prob.astype(jnp.bfloat16))

        total, acc = lax.fori_loop(
            lo, i + 1, forward, (jnp.zeros_like(top), jnp.zeros(acc_out.shape[1:], jnp.float32))
        )
        top_row[:, columns] = top
        total_row[:, columns] = total
        acc_out[i] = acc


def earlier_kernel(
    lo_ref, place_ref, start_row, queries, out_grad, far, top_row, total_row, acc_in, kv_prev,
    attended_out, lse_row, delta_row, acc_out, p_near, p_next,
    keys_t, values_t, scores, key_acc, value_acc,
):
    tile, before = scores.shape[1], scores.shape[0]
    tiles = acc_in.shape[0]
    scale = queries.shape[2] ** -0.5
    core = place_ref[0]
    bf16, f32 = jnp.bfloat16, jnp.float32
    first = lo_ref[0]

    @pl.when(first < before)
    def _():
        key_acc[...] = jnp.zeros_like(key_acc)
        value_acc[...] = jnp.zeros_like(value_acc)

        def turn(j, carry):
            keys_t[j] = key_tile(kv_prev, j, 0, tile).T
            values_t[j] = key_tile(kv_prev, j, 1, tile).T
            return carry

        lax.fori_loop(first, before, turn, 0)

    for i in range(tiles):
        columns = pl.ds(i * tile, tile)
        query = query_tile(queries, far, 0, core, i, tile)
        grad = query_tile(out_grad, far, 1, core, i, tile)
        start = start_row[:, columns]
        lo = jnp.minimum(lo_ref[i], before)
        own_top = top_row[:, columns]

        def score_tile(j, top):
            raw = masked_scores(key_tile(kv_prev, j, 0, tile), query, start, j, tile, False)
            scores[j] = raw
            return jnp.maximum(top, column_max(raw))

        top = lax.fori_loop(lo, before, score_tile, own_top)
        shrink = jnp.exp2(own_top - top)

        def forward(j, carry):
            total, acc = carry
            prob = jnp.exp2(scores[j] - top)
            scores[j] = prob
            return total + column_sum(prob), acc + matmul(values_t[j], prob.astype(bf16))

        total, acc = lax.fori_loop(
            lo, before, forward, (total_row[:, columns] * shrink, acc_in[i] * shrink)
        )
        inv = 1.0 / total
        attended_t = (acc * inv).astype(bf16).astype(f32)
        delta = column_sum(grad.astype(f32).T * attended_t)
        half, part = divmod(i, tiles // 2)
        attended_out[half, pl.ds(part * tile, tile)] = attended_t.T.astype(bf16)
        lse_row[:, columns] = top + jnp.log2(total)
        delta_row[:, columns] = delta

        def backward(j, acc):
            prob = scores[j] * inv
            here = pl.ds(pl.multiple_of(j * tile, tile), tile)
            value_acc[here] += matmul(prob.astype(bf16), grad)
            dot_grad = matmul(key_tile(kv_prev, j, 1, tile), grad, NT)
            score_grad = (prob * (dot_grad - delta)).astype(bf16)
            key_acc[here] += matmul(score_grad, query)
            return acc + matmul(keys_t[j], score_grad)

        acc_out[i] = lax.fori_loop(lo, before, backward, jnp.zeros(acc_out.shape[1:], f32))

    shards, shard = kv_prev.shape[1], kv_prev.shape[3]

    @pl.when(first < before)
    def _():
        for slot, target in enumerate((p_next, p_near.at[0], p_near.at[1])):
            for row in range(shards):
                here = pl.ds((slot * shards + row) * shard, shard)
                target[row, 0] = (key_acc[here] * scale).astype(bf16)
                target[row, 1] = value_acc[here].astype(bf16)

    @pl.when(first >= before)
    def _():
        p_next[...] = jnp.zeros_like(p_next)
        p_near[...] = jnp.zeros_like(p_near)


def own_backward_kernel(
    lo_ref, place_ref, start_row, queries, out_grad, far, kv_own, attended, lse_row, delta_row,
    acc_in, out_own, out_far, p_own,
    keys, values, keys_t, key_acc, value_acc,
):
    tiles, tile = keys.shape[0], keys.shape[1]
    scale = queries.shape[2] ** -0.5
    core = place_ref[0]
    bf16, f32 = jnp.bfloat16, jnp.float32
    before = REACH * tiles // 2
    for j in range(tiles):
        span = core if j < tiles // 2 else 1 - core
        rows = pl.ds(j % (tiles // 2) * (tile // kv_own.shape[3]), tile // kv_own.shape[3])
        block = kv_own[span, rows, 0].reshape(keys.shape[1:])
        keys[j] = block
        keys_t[j] = block.T
        values[j] = kv_own[span, rows, 1].reshape(keys.shape[1:])
    key_acc[...] = jnp.zeros_like(key_acc)
    value_acc[...] = jnp.zeros_like(value_acc)
    for i in range(tiles):
        columns = pl.ds(i * tile, tile)
        query = query_tile(queries, far, 0, core, i, tile)
        grad = query_tile(out_grad, far, 1, core, i, tile)
        start = start_row[:, columns]
        lse, delta = lse_row[:, columns], delta_row[:, columns]

        def backward(j, acc, causal):
            raw = masked_scores(keys[j], query, start, j + before, tile, causal)
            prob = jnp.exp2(raw - lse)
            value_acc[j] += matmul(prob.astype(bf16), grad)
            score_grad = (prob * (matmul(values[j], grad, NT) - delta)).astype(bf16)
            key_acc[j] += matmul(score_grad, query)
            return acc + matmul(keys_t[j], score_grad)

        acc = backward(i, acc_in[i], True)
        acc = lax.fori_loop(
            jnp.maximum(lo_ref[i] - before, 0), i, lambda j, acc: backward(j, acc, False), acc
        )
        half, part = divmod(i, tiles // 2)
        rows = pl.ds(part * tile, tile)
        (out_own, out_far)[half][1, rows] = (acc.T * scale).astype(bf16)
    out_own[0] = attended[0]
    out_far[0] = attended[1]
    shards, shard = kv_own.shape[1], kv_own.shape[3]
    for span in range(2):
        for row in range(shards):
            j, part = divmod((span * shards + row) * shard, tile)
            here = pl.ds(part, shard)
            p_own[span, row, 0] = key_acc[j, here] * scale
            p_own[span, row, 1] = value_acc[j, here]


def vmem_kernel(kernel, name, outputs, scratch, tiles, tile, head_dim, matmuls):
    def call(*operands):
        rest = [pl.BlockSpec(memory_space=pltpu.VMEM)] * (len(operands) - 2)
        return pl.pallas_call(
            kernel,
            out_shape=outputs,
            in_specs=[pl.BlockSpec(memory_space=pltpu.SMEM)] * 2 + rest,
            out_specs=[pl.BlockSpec(memory_space=pltpu.VMEM)] * len(outputs),
            scratch_shapes=[pltpu.VMEM(shape, dtype) for shape, dtype in scratch],
            compiler_params=pltpu.CompilerParams(vmem_limit_bytes=24 * 1024 * 1024),
            cost_estimate=pl.CostEstimate(
                flops=2 * matmuls * tiles * tile * tile * head_dim,
                bytes_accessed=4 * 1024 * 1024,
                transcendentals=tiles * tile * tile,
            ),
            name=name,
        )(*operands)

    return call


def body(queries, key_states, value_states, out_grad, segments):
    ctx = lax.axis_size("pair") * 2
    core = lax.axis_index("core")
    position = lax.axis_index("pair") * 2 + core
    place = position % GROUP
    width = queries.shape[2]
    heads = lax.axis_size("head")
    shard = key_states.shape[2]
    head_dim = key_states.shape[3]
    bf16, f32 = jnp.bfloat16, jnp.float32

    swap, near, far_chip = swap_pairs(ctx), near_pairs(ctx), next_pairs(ctx)
    edge1 = within(ctx, [(2, 0), (GROUP - 3, GROUP - 1)])
    edge2 = within(ctx, [(1, 0), (GROUP - 2, GROUP - 1)])
    everywhere = CTX + ("head",)
    even = core == 0
    sends_lower = place >= GROUP - REACH
    head = lax.axis_index("head")
    bits = folds(heads)
    far_bit = bits[0]
    high = {bit: (head & bit) != 0 for bit in bits}
    straight, crossing = edge_pairs(ctx, heads, 0), edge_pairs(ctx, heads, far_bit)

    lower = jnp.stack([key_states[0, 0], value_states[0, 0]])
    upper = jnp.stack([key_states[0, 1], value_states[0, 1]])
    leaving = pick(sends_lower, upper, lower)
    half = by_bit(core, pick(even, upper, lower), lax.ppermute(pick(even, lower, upper), CTX, swap), 0)
    kv_own = by_bit(high[far_bit], half, lax.ppermute(half, everywhere, head_pairs(ctx, heads, far_bit)), 1)
    kv_edge = by_bit(
        high[far_bit],
        lax.ppermute(leaving, everywhere, straight),
        lax.ppermute(leaving, everywhere, crossing),
        0,
    )
    kv_all = jnp.concatenate([kv_own, kv_edge[None]])
    for k, bit in enumerate(bits[1:]):
        other = lax.ppermute(kv_all, everywhere, head_pairs(ctx, heads, bit))
        kv_all = by_bit(high[bit], kv_all, other, 2 + k)
    kv_all = kv_all.reshape((3, heads) + half.shape[1:])
    kv_own, kv_edge = kv_all[:2], kv_all[2]

    queries, out_grad = queries[0], out_grad[0]
    far = lax.ppermute(
        jnp.where(
            even,
            jnp.stack([queries[1], out_grad[1]]),
            jnp.stack([queries[0], out_grad[0]]),
        ),
        CTX,
        swap,
    )

    kv_next = lax.ppermute(jnp.where(even, kv_own[1], kv_own[0]), CTX, far_chip)
    kv_near = lax.ppermute(kv_own, CTX, near)
    kv_edge1 = lax.ppermute(kv_edge, CTX, edge1)
    kv_edge2 = lax.ppermute(kv_edge, CTX, edge2)

    first = jnp.where(even, position, 2 * ctx - 1 - position)
    window = (REACH + 2) * width
    padded = jnp.concatenate([jnp.full((REACH * width,), -1, jnp.int32), segments])
    seg_window = lax.dynamic_slice_in_dim(padded, first * width, window)
    start = jnp.sum(
        seg_window[:, None] < seg_window[None, REACH * width :], axis=0, dtype=jnp.int32
    )
    tile = max(min(256, width // 2), shard)
    tiles, earlier = 2 * width // tile, REACH * width // tile
    lo = start[::tile] // tile
    edge_next = jnp.where(even, place <= 2, place >= GROUP - 3)
    edge_near = jnp.where(even, place == 0, place == GROUP - 1)
    places = core[None].astype(jnp.int32)
    start = start[None, :]

    near_ordered = jnp.where(even, kv_near, kv_near[::-1])
    kv_prev = jnp.stack(
        [
            jnp.where(edge_next, kv_edge, kv_next),
            jnp.where(edge_near, kv_edge2, near_ordered[0]),
            jnp.where(edge_near, kv_edge1, near_ordered[1]),
        ]
    )

    row = jax.ShapeDtypeStruct((1, 2 * width), f32)
    turned = jax.ShapeDtypeStruct((tiles, head_dim, tile), f32)
    part = jax.ShapeDtypeStruct((2, width, head_dim), bf16)
    span_like = kv_next.shape
    natural = ((tiles, tile, head_dim), bf16)
    top, total, acc = vmem_kernel(
        own_forward_kernel, "own_forward", (row, row, turned),
        [natural, natural, ((tiles, head_dim, tile), bf16), ((tiles, tile, tile), f32)],
        6, tile, head_dim, 2,
    )(lo, places, start, queries, far, kv_own)
    attended, lse, delta, acc, p_near, p_next = vmem_kernel(
        earlier_kernel, "earlier",
        (
            part, row, row, turned,
            jax.ShapeDtypeStruct((2,) + span_like, bf16),
            jax.ShapeDtypeStruct(span_like, bf16),
        ),
        [
            ((earlier, head_dim, tile), bf16),
            ((earlier, head_dim, tile), bf16),
            ((earlier, tile, tile), f32),
            ((earlier * tile, head_dim), f32),
            ((earlier * tile, head_dim), f32),
        ],
        6, tile, head_dim, 6,
    )(lo, places, start, queries, out_grad, far, top, total, acc, kv_prev)

    r_edge1 = lax.ppermute(p_near[1], CTX, inverse(edge1)).astype(f32)
    r_edge2 = lax.ppermute(p_near[0], CTX, inverse(edge2)).astype(f32)
    r_next = lax.ppermute(p_next, CTX, inverse(far_chip)).astype(f32)
    r_near = lax.ppermute(p_near, CTX, inverse(near)).astype(f32)

    out_own, out_far, p_own = vmem_kernel(
        own_backward_kernel, "own_backward",
        (part, part, jax.ShapeDtypeStruct((2,) + span_like, f32)),
        [natural, natural, ((tiles, head_dim, tile), bf16)]
        + [((tiles, tile, head_dim), f32)] * 2,
        6, tile, head_dim, 5,
    )(lo, places, start, queries, out_grad, far, kv_own, attended, lse, delta, acc)

    edge_sum = jnp.where(edge_next, p_next.astype(f32), 0.0) + r_edge1 + r_edge2
    sums = p_own + r_near
    first_sum, second_sum = sums[0], sums[1] + r_next
    sums = jnp.stack(
        [pick(even, second_sum, first_sum), pick(even, first_sum, second_sum), edge_sum]
    )
    for bit in reversed(bits[1:]):
        halves = sums.reshape((3, -1, 2) + half.shape[1:])
        away = pick(high[bit], halves[:, :, 1], halves[:, :, 0]).astype(bf16)
        other = lax.ppermute(away, everywhere, head_pairs(ctx, heads, bit))
        sums = pick(high[bit], halves[:, :, 0], halves[:, :, 1]) + other.astype(f32)
    stays, away = pick(high[far_bit], sums[:, 0], sums[:, 1]), pick(high[far_bit], sums[:, 1], sums[:, 0])
    away = away.astype(bf16)
    other = lax.ppermute(away[:2], everywhere, head_pairs(ctx, heads, far_bit))
    returned = lax.ppermute(stays[2].astype(bf16), everywhere, inverse(straight)).astype(f32)
    returned += lax.ppermute(away[2], everywhere, inverse(crossing)).astype(f32)
    stays = stays[:2] + other.astype(f32)
    own_half = pick(even, stays[1], stays[0])
    far_half = lax.ppermute(
        pick(even, stays[0], stays[1]).astype(bf16), CTX, swap
    ).astype(f32)
    lower = pick(even, far_half, own_half) + jnp.where(sends_lower, returned, 0.0)
    upper = pick(even, own_half, far_half) + jnp.where(sends_lower, 0.0, returned)
    grads = jnp.stack([lower, upper]).astype(bf16)

    back = lax.ppermute(out_far, CTX, swap)
    results = []
    for k in range(2):
        results.append(
            jnp.where(
                even, jnp.stack([out_own[k], back[k]]), jnp.stack([back[k], out_own[k]])
            )[None]
        )
    return results[0], results[1], grads[:, 0][None], grads[:, 1][None]


def solution(mesh):
    ctx, heads = mesh.devices.shape
    mesh = Mesh(mesh.devices.reshape(ctx // 2, 2, heads), CTX + ("head",))
    by_head = P(CTX, None, None, "head")
    by_row = P(CTX, None, "head", None)
    return jax.shard_map(
        body,
        mesh=mesh,
        in_specs=(by_head, by_row, by_row, by_head, P()),
        out_specs=(by_head, by_head, by_row, by_row),
        check_vma=False,
    )
```

```python
import math

import jax
import jax.numpy as jnp
from jax import lax
from jax.experimental import pallas as pl
from jax.experimental.pallas import tpu as pltpu
from jax.sharding import Mesh
from jax.sharding import PartitionSpec as P

REACH = 3
GROUP = 8
NEG_FILL = -1e30
CTX = ("pair", "core")


def within(ctx, moves):
    return [(base + a, base + b) for base in range(0, ctx, GROUP) for a, b in moves]


def swap_pairs(ctx):
    return within(ctx, [(r, r ^ 1) for r in range(GROUP)])


def near_pairs(ctx):
    forth = [(r, r + 2) for r in range(0, GROUP - 2, 2)]
    return within(ctx, forth + [(r, r - 2) for r in range(3, GROUP, 2)])


def next_pairs(ctx):
    forth = [(r, r + 4) for r in range(0, GROUP - 4, 2)]
    return within(ctx, forth + [(r, r - 4) for r in range(5, GROUP, 2)])


def head_pairs(ctx, heads, bit):
    return [(d, d ^ bit) for d in range(ctx * heads)]


def holder_pairs(ctx, heads, bit):
    holders = [r for r in range(GROUP) if r < REACH or r >= GROUP - REACH]
    return [
        ((base + r) * heads + h, (base + r) * heads + (h ^ bit))
        for base in range(0, ctx, GROUP)
        for r in holders
        for h in range(heads)
    ]


def edge_pairs(ctx, heads):
    moves = []
    for base in range(0, ctx, GROUP):
        for k in range(REACH):
            top = base + GROUP - 1 - k
            if base + GROUP < ctx:
                moves.append((top, base + GROUP + REACH - 1 - k))
            else:
                moves.append((top, base + GROUP - REACH + k))
            if base > 0:
                moves.append((base + k, base - REACH + k))
    return [
        (a * heads + h, b * heads + heads - 1 - h) for a, b in moves for h in range(heads)
    ]


def folds(heads):
    return [1 << k for k in reversed(range(heads.bit_length() - 1))]


def pick(bit, low, high):
    return jnp.where(bit, high, low)


def by_bit(bit, mine, other, axis):
    mine, other = jnp.expand_dims(mine, axis), jnp.expand_dims(other, axis)
    place = lax.broadcasted_iota(jnp.int32, (2,) + (1,) * (mine.ndim - axis - 1), 0)
    return jnp.where(place == bit.astype(jnp.int32), mine, other)


def inverse(pairs):
    return [(b, a) for a, b in pairs]


NT = (((1,), (1,)), ((), ()))
NN = (((1,), (0,)), ((), ()))


def matmul(a, b, dims=NN):
    return lax.dot_general(a, b, dims, preferred_element_type=jnp.float32)


def key_tile(ref, j, which, tile):
    _, shards, _, shard, head_dim = ref.shape
    per_span = shards * shard // tile
    rows = pl.ds((j % per_span) * (tile // shard), tile // shard)
    return ref[j // per_span, rows, which].reshape(tile, head_dim)


def query_tile(own_ref, far_ref, far_index, core, i, tile):
    width = far_ref.shape[1]
    span, part = divmod(i, width // tile)
    rows = pl.ds(part * tile, tile)
    return own_ref[core, rows] if span == 0 else far_ref[far_index, rows]


def masked_scores(keys, query, start, j, tile, causal):
    raw = matmul(keys, query, NT) * (query.shape[1] ** -0.5 * math.log2(math.e))
    at_key = lax.broadcasted_iota(jnp.int32, raw.shape, 0)
    allowed = at_key >= start - j * tile
    if causal:
        allowed = allowed & (at_key <= lax.broadcasted_iota(jnp.int32, raw.shape, 1))
    return jnp.where(allowed, raw, NEG_FILL)


def column_max(a):
    return jnp.max(a, axis=0, keepdims=True)


def column_sum(a):
    return jnp.sum(a, axis=0, keepdims=True)


def own_forward_kernel(
    lo_ref, place_ref, start_row, queries, far, kv_own, top_row, total_row, acc_out,
    keys, values, values_t, scores,
):
    tile, tiles = scores.shape[1], scores.shape[0]
    core = place_ref[0]
    before = REACH * tiles // 2
    for j in range(tiles):
        span = core if j < tiles // 2 else 1 - core
        rows = pl.ds(j % (tiles // 2) * (tile // kv_own.shape[3]), tile // kv_own.shape[3])
        keys[j] = kv_own[span, rows, 0].reshape(keys.shape[1:])
        values_t[j] = kv_own[span, rows, 1].reshape(keys.shape[1:]).T
    for i in range(tiles):
        columns = pl.ds(i * tile, tile)
        query = query_tile(queries, far, 0, core, i, tile)
        start = start_row[:, columns]
        lo = jnp.maximum(lo_ref[i] - before, 0)

        def score_tile(j, causal):
            raw = masked_scores(keys[j], query, start, j + before, tile, causal)
            scores[j] = raw
            return column_max(raw)

        top = lax.fori_loop(
            lo, i, lambda j, m: jnp.maximum(m, score_tile(j, False)), score_tile(i, True)
        )

        def forward(j, carry):
            total, acc = carry
            prob = jnp.exp2(scores[j] - top)
            return total + column_sum(prob), acc + matmul(values_t[j], prob.astype(jnp.bfloat16))

        total, acc = lax.fori_loop(
            lo, i + 1, forward, (jnp.zeros_like(top), jnp.zeros(acc_out.shape[1:], jnp.float32))
        )
        top_row[:, columns] = top
        total_row[:, columns] = total
        acc_out[i] = acc


def earlier_kernel(
    lo_ref, place_ref, start_row, queries, out_grad, far, top_row, total_row, acc_in, kv_prev,
    attended_out, lse_row, delta_row, acc_out, p_near, p_next,
    keys_t, values_t, scores, key_acc, value_acc,
):
    tile, before = scores.shape[1], scores.shape[0]
    tiles = acc_in.shape[0]
    scale = queries.shape[2] ** -0.5
    core = place_ref[0]
    bf16, f32 = jnp.bfloat16, jnp.float32
    first = lo_ref[0]

    @pl.when(first < before)
    def _():
        key_acc[...] = jnp.zeros_like(key_acc)
        value_acc[...] = jnp.zeros_like(value_acc)

        def turn(j, carry):
            keys_t[j] = key_tile(kv_prev, j, 0, tile).T
            values_t[j] = key_tile(kv_prev, j, 1, tile).T
            return carry

        lax.fori_loop(first, before, turn, 0)

    for i in range(tiles):
        columns = pl.ds(i * tile, tile)
        query = query_tile(queries, far, 0, core, i, tile)
        grad = query_tile(out_grad, far, 1, core, i, tile)
        start = start_row[:, columns]
        lo = jnp.minimum(lo_ref[i], before)
        own_top = top_row[:, columns]

        def score_tile(j, top):
            raw = masked_scores(key_tile(kv_prev, j, 0, tile), query, start, j, tile, False)
            scores[j] = raw
            return jnp.maximum(top, column_max(raw))

        top = lax.fori_loop(lo, before, score_tile, own_top)
        shrink = jnp.exp2(own_top - top)

        def forward(j, carry):
            total, acc = carry
            prob = jnp.exp2(scores[j] - top)
            scores[j] = prob
            return total + column_sum(prob), acc + matmul(values_t[j], prob.astype(bf16))

        total, acc = lax.fori_loop(
            lo, before, forward, (total_row[:, columns] * shrink, acc_in[i] * shrink)
        )
        inv = 1.0 / total
        attended_t = (acc * inv).astype(bf16).astype(f32)
        delta = column_sum(grad.astype(f32).T * attended_t)
        half, part = divmod(i, tiles // 2)
        attended_out[half, pl.ds(part * tile, tile)] = attended_t.T.astype(bf16)
        lse_row[:, columns] = top + jnp.log2(total)
        delta_row[:, columns] = delta

        def backward(j, acc):
            prob = scores[j] * inv
            here = pl.ds(pl.multiple_of(j * tile, tile), tile)
            value_acc[here] += matmul(prob.astype(bf16), grad)
            dot_grad = matmul(key_tile(kv_prev, j, 1, tile), grad, NT)
            score_grad = (prob * (dot_grad - delta)).astype(bf16)
            key_acc[here] += matmul(score_grad, query)
            return acc + matmul(keys_t[j], score_grad)

        acc_out[i] = lax.fori_loop(lo, before, backward, jnp.zeros(acc_out.shape[1:], f32))

    shards, shard = kv_prev.shape[1], kv_prev.shape[3]

    @pl.when(first < before)
    def _():
        for slot, target in enumerate((p_next, p_near.at[0], p_near.at[1])):
            for row in range(shards):
                here = pl.ds((slot * shards + row) * shard, shard)
                target[row, 0] = (key_acc[here] * scale).astype(bf16)
                target[row, 1] = value_acc[here].astype(bf16)

    @pl.when(first >= before)
    def _():
        p_next[...] = jnp.zeros_like(p_next)
        p_near[...] = jnp.zeros_like(p_near)


def own_backward_kernel(
    lo_ref, place_ref, start_row, queries, out_grad, far, kv_own, attended, lse_row, delta_row,
    acc_in, out_own, out_far, p_own,
    keys, values, keys_t, key_acc, value_acc,
):
    tiles, tile = keys.shape[0], keys.shape[1]
    scale = queries.shape[2] ** -0.5
    core = place_ref[0]
    bf16, f32 = jnp.bfloat16, jnp.float32
    before = REACH * tiles // 2
    for j in range(tiles):
        span = core if j < tiles // 2 else 1 - core
        rows = pl.ds(j % (tiles // 2) * (tile // kv_own.shape[3]), tile // kv_own.shape[3])
        block = kv_own[span, rows, 0].reshape(keys.shape[1:])
        keys[j] = block
        keys_t[j] = block.T
        values[j] = kv_own[span, rows, 1].reshape(keys.shape[1:])
    key_acc[...] = jnp.zeros_like(key_acc)
    value_acc[...] = jnp.zeros_like(value_acc)
    for i in range(tiles):
        columns = pl.ds(i * tile, tile)
        query = query_tile(queries, far, 0, core, i, tile)
        grad = query_tile(out_grad, far, 1, core, i, tile)
        start = start_row[:, columns]
        lse, delta = lse_row[:, columns], delta_row[:, columns]

        def backward(j, acc, causal):
            raw = masked_scores(keys[j], query, start, j + before, tile, causal)
            prob = jnp.exp2(raw - lse)
            value_acc[j] += matmul(prob.astype(bf16), grad)
            score_grad = (prob * (matmul(values[j], grad, NT) - delta)).astype(bf16)
            key_acc[j] += matmul(score_grad, query)
            return acc + matmul(keys_t[j], score_grad)

        acc = backward(i, acc_in[i], True)
        acc = lax.fori_loop(
            jnp.maximum(lo_ref[i] - before, 0), i, lambda j, acc: backward(j, acc, False), acc
        )
        half, part = divmod(i, tiles // 2)
        rows = pl.ds(part * tile, tile)
        (out_own, out_far)[half][1, rows] = (acc.T * scale).astype(bf16)
    out_own[0] = attended[0]
    out_far[0] = attended[1]
    shards, shard = kv_own.shape[1], kv_own.shape[3]
    for span in range(2):
        for row in range(shards):
            j, part = divmod((span * shards + row) * shard, tile)
            here = pl.ds(part, shard)
            p_own[span, row, 0] = key_acc[j, here] * scale
            p_own[span, row, 1] = value_acc[j, here]


def vmem_kernel(kernel, name, outputs, scratch, tiles, tile, head_dim, matmuls):
    def call(*operands):
        rest = [pl.BlockSpec(memory_space=pltpu.VMEM)] * (len(operands) - 2)
        return pl.pallas_call(
            kernel,
            out_shape=outputs,
            in_specs=[pl.BlockSpec(memory_space=pltpu.SMEM)] * 2 + rest,
            out_specs=[pl.BlockSpec(memory_space=pltpu.VMEM)] * len(outputs),
            scratch_shapes=[pltpu.VMEM(shape, dtype) for shape, dtype in scratch],
            compiler_params=pltpu.CompilerParams(vmem_limit_bytes=24 * 1024 * 1024),
            cost_estimate=pl.CostEstimate(
                flops=2 * matmuls * tiles * tile * tile * head_dim,
                bytes_accessed=4 * 1024 * 1024,
                transcendentals=tiles * tile * tile,
            ),
            name=name,
        )(*operands)

    return call


def body(queries, key_states, value_states, out_grad, segments):
    ctx = lax.axis_size("pair") * 2
    core = lax.axis_index("core")
    position = lax.axis_index("pair") * 2 + core
    place = position % GROUP
    width = queries.shape[2]
    heads = lax.axis_size("head")
    shard = key_states.shape[2]
    head_dim = key_states.shape[3]
    bf16, f32 = jnp.bfloat16, jnp.float32

    swap, near, far_chip = swap_pairs(ctx), near_pairs(ctx), next_pairs(ctx)
    edge1 = within(ctx, [(2, 0), (GROUP - 3, GROUP - 1)])
    edge2 = within(ctx, [(1, 0), (GROUP - 2, GROUP - 1)])
    everywhere = CTX + ("head",)
    even = core == 0
    sends_lower = place >= GROUP - REACH
    head = lax.axis_index("head")
    bits = folds(heads)
    high = {bit: (head & bit) != 0 for bit in bits}
    edge = edge_pairs(ctx, heads)

    lower = jnp.stack([key_states[0, 0], value_states[0, 0]])
    upper = jnp.stack([key_states[0, 1], value_states[0, 1]])
    leaving = pick(sends_lower, upper, lower)
    half = by_bit(core, pick(even, upper, lower), lax.ppermute(pick(even, lower, upper), CTX, swap), 0)
    half, leaving = lax.optimization_barrier((half, leaving))
    kv_own, kv_edge = half, lax.ppermute(leaving, everywhere, edge)
    for k, bit in enumerate(bits):
        other = lax.ppermute(kv_own, everywhere, head_pairs(ctx, heads, bit))
        kv_own = by_bit(high[bit], kv_own, other, 1 + k)
    for k, bit in enumerate(bits):
        other = lax.ppermute(kv_edge, everywhere, holder_pairs(ctx, heads, bit))
        kv_edge = by_bit(~high[bit], kv_edge, other, k)
    kv_own = kv_own.reshape((2, heads) + half.shape[1:])
    kv_edge = kv_edge.reshape((heads,) + half.shape[1:])

    queries, out_grad = queries[0], out_grad[0]
    far = lax.ppermute(
        jnp.where(
            even,
            jnp.stack([queries[1], out_grad[1]]),
            jnp.stack([queries[0], out_grad[0]]),
        ),
        CTX,
        swap,
    )

    kv_next = lax.ppermute(jnp.where(even, kv_own[1], kv_own[0]), CTX, far_chip)
    kv_near = lax.ppermute(kv_own, CTX, near)
    kv_edge1 = lax.ppermute(kv_edge, CTX, edge1)
    kv_edge2 = lax.ppermute(kv_edge, CTX, edge2)

    first = jnp.where(even, position, 2 * ctx - 1 - position)
    window = (REACH + 2) * width
    padded = jnp.concatenate([jnp.full((REACH * width,), -1, jnp.int32), segments])
    seg_window = lax.dynamic_slice_in_dim(padded, first * width, window)
    start = jnp.sum(
        seg_window[:, None] < seg_window[None, REACH * width :], axis=0, dtype=jnp.int32
    )
    tile = max(min(256, width // 2), shard)
    tiles, earlier = 2 * width // tile, REACH * width // tile
    lo = start[::tile] // tile
    edge_next = jnp.where(even, place <= 2, place >= GROUP - 3)
    edge_near = jnp.where(even, place == 0, place == GROUP - 1)
    places = core[None].astype(jnp.int32)
    start = start[None, :]

    near_ordered = jnp.where(even, kv_near, kv_near[::-1])
    kv_prev = jnp.stack(
        [
            jnp.where(edge_next, kv_edge, kv_next),
            jnp.where(edge_near, kv_edge2, near_ordered[0]),
            jnp.where(edge_near, kv_edge1, near_ordered[1]),
        ]
    )

    row = jax.ShapeDtypeStruct((1, 2 * width), f32)
    turned = jax.ShapeDtypeStruct((tiles, head_dim, tile), f32)
    part = jax.ShapeDtypeStruct((2, width, head_dim), bf16)
    span_like = kv_next.shape
    natural = ((tiles, tile, head_dim), bf16)
    top, total, acc = vmem_kernel(
        own_forward_kernel, "own_forward", (row, row, turned),
        [natural, natural, ((tiles, head_dim, tile), bf16), ((tiles, tile, tile), f32)],
        6, tile, head_dim, 2,
    )(lo, places, start, queries, far, kv_own)
    attended, lse, delta, acc, p_near, p_next = vmem_kernel(
        earlier_kernel, "earlier",
        (
            part, row, row, turned,
            jax.ShapeDtypeStruct((2,) + span_like, bf16),
            jax.ShapeDtypeStruct(span_like, bf16),
        ),
        [
            ((earlier, head_dim, tile), bf16),
            ((earlier, head_dim, tile), bf16),
            ((earlier, tile, tile), f32),
            ((earlier * tile, head_dim), f32),
            ((earlier * tile, head_dim), f32),
        ],
        6, tile, head_dim, 6,
    )(lo, places, start, queries, out_grad, far, top, total, acc, kv_prev)

    r_edge1 = lax.ppermute(p_near[1], CTX, inverse(edge1)).astype(f32)
    r_edge2 = lax.ppermute(p_near[0], CTX, inverse(edge2)).astype(f32)
    r_next = lax.ppermute(p_next, CTX, inverse(far_chip)).astype(f32)
    r_near = lax.ppermute(p_near, CTX, inverse(near)).astype(f32)

    out_own, out_far, p_own = vmem_kernel(
        own_backward_kernel, "own_backward",
        (part, part, jax.ShapeDtypeStruct((2,) + span_like, f32)),
        [natural, natural, ((tiles, head_dim, tile), bf16)]
        + [((tiles, tile, head_dim), f32)] * 2,
        6, tile, head_dim, 5,
    )(lo, places, start, queries, out_grad, far, kv_own, attended, lse, delta, acc)

    edge_sum = jnp.where(edge_next, p_next.astype(f32), 0.0) + r_edge1 + r_edge2
    for bit in reversed(bits):
        halves = edge_sum.reshape((-1, 2) + half.shape[1:])
        away = pick(high[bit], halves[:, 0], halves[:, 1]).astype(bf16)
        other = lax.ppermute(away, everywhere, holder_pairs(ctx, heads, bit))
        edge_sum = pick(high[bit], halves[:, 1], halves[:, 0]) + other.astype(f32)
    returned = lax.ppermute(edge_sum[0].astype(bf16), everywhere, inverse(edge)).astype(f32)

    sums = p_own + r_near
    first_sum, second_sum = sums[0], sums[1] + r_next
    sums = jnp.stack([pick(even, second_sum, first_sum), pick(even, first_sum, second_sum)])
    for bit in reversed(bits):
        halves = sums.reshape((2, -1, 2) + half.shape[1:])
        away = pick(high[bit], halves[:, :, 1], halves[:, :, 0]).astype(bf16)
        other = lax.ppermute(away, everywhere, head_pairs(ctx, heads, bit))
        sums = pick(high[bit], halves[:, :, 0], halves[:, :, 1]) + other.astype(f32)
    stays = sums[:, 0]
    own_half = pick(even, stays[1], stays[0])
    far_half = lax.ppermute(
        pick(even, stays[0], stays[1]).astype(bf16), CTX, swap
    ).astype(f32)
    lower = pick(even, far_half, own_half) + jnp.where(sends_lower, returned, 0.0)
    upper = pick(even, own_half, far_half) + jnp.where(sends_lower, 0.0, returned)
    grads = jnp.stack([lower, upper]).astype(bf16)

    back = lax.ppermute(out_far, CTX, swap)
    results = []
    for k in range(2):
        results.append(
            jnp.where(
                even, jnp.stack([out_own[k], back[k]]), jnp.stack([back[k], out_own[k]])
            )[None]
        )
    return results[0], results[1], grads[:, 0][None], grads[:, 1][None]


def solution(mesh):
    ctx, heads = mesh.devices.shape
    mesh = Mesh(mesh.devices.reshape(ctx // 2, 2, heads), CTX + ("head",))
    by_head = P(CTX, None, None, "head")
    by_row = P(CTX, None, "head", None)
    return jax.shard_map(
        body,
        mesh=mesh,
        in_specs=(by_head, by_row, by_row, by_head, P()),
        out_specs=(by_head, by_head, by_row, by_row),
        check_vma=False,
    )
```

```python
import math

import jax
import jax.numpy as jnp
from jax import lax
from jax.experimental import pallas as pl
from jax.experimental.pallas import tpu as pltpu
from jax.sharding import Mesh
from jax.sharding import PartitionSpec as P

REACH = 3
GROUP = 8
NEG_FILL = -1e30
CTX = ("pair", "core")


def within(ctx, moves):
    return [(base + a, base + b) for base in range(0, ctx, GROUP) for a, b in moves]


def swap_pairs(ctx):
    return within(ctx, [(r, r ^ 1) for r in range(GROUP)])


def near_pairs(ctx):
    forth = [(r, r + 2) for r in range(0, GROUP - 2, 2)]
    return within(ctx, forth + [(r, r - 2) for r in range(3, GROUP, 2)])


def next_pairs(ctx):
    forth = [(r, r + 4) for r in range(0, GROUP - 4, 2)]
    return within(ctx, forth + [(r, r - 4) for r in range(5, GROUP, 2)])


def head_pairs(ctx, heads, bit):
    return [(d, d ^ bit) for d in range(ctx * heads)]


def holder_pairs(ctx, heads, bit):
    holders = [r for r in range(GROUP) if r < REACH or r >= GROUP - REACH]
    return [
        ((base + r) * heads + h, (base + r) * heads + (h ^ bit))
        for base in range(0, ctx, GROUP)
        for r in holders
        for h in range(heads)
    ]


def edge_pairs(ctx, heads):
    moves = []
    for base in range(0, ctx, GROUP):
        for k in range(REACH):
            top = base + GROUP - 1 - k
            if base + GROUP < ctx:
                moves.append((top, base + GROUP + REACH - 1 - k))
            else:
                moves.append((top, base + GROUP - REACH + k))
            if base > 0:
                moves.append((base + k, base - REACH + k))
    return [
        (a * heads + h, b * heads + heads - 1 - h) for a, b in moves for h in range(heads)
    ]


def folds(heads):
    return [1 << k for k in reversed(range(heads.bit_length() - 1))]


def pick(bit, low, high):
    return jnp.where(bit, high, low)


def by_bit(bit, mine, other, axis):
    mine, other = jnp.expand_dims(mine, axis), jnp.expand_dims(other, axis)
    place = lax.broadcasted_iota(jnp.int32, (2,) + (1,) * (mine.ndim - axis - 1), 0)
    return jnp.where(place == bit.astype(jnp.int32), mine, other)


def inverse(pairs):
    return [(b, a) for a, b in pairs]


NT = (((1,), (1,)), ((), ()))
NN = (((1,), (0,)), ((), ()))


def matmul(a, b, dims=NN):
    return lax.dot_general(a, b, dims, preferred_element_type=jnp.float32)


def key_tile(ref, j, which, tile):
    _, shards, _, shard, head_dim = ref.shape
    per_span = shards * shard // tile
    rows = pl.ds((j % per_span) * (tile // shard), tile // shard)
    return ref[j // per_span, rows, which].reshape(tile, head_dim)


def query_tile(own_ref, far_ref, far_index, core, i, tile):
    width = far_ref.shape[1]
    span, part = divmod(i, width // tile)
    rows = pl.ds(part * tile, tile)
    return own_ref[core, rows] if span == 0 else far_ref[far_index, rows]


def masked_scores(keys, query, start, j, tile, causal):
    raw = matmul(keys, query, NT) * (query.shape[1] ** -0.5 * math.log2(math.e))
    at_key = lax.broadcasted_iota(jnp.int32, raw.shape, 0)
    allowed = at_key >= start - j * tile
    if causal:
        allowed = allowed & (at_key <= lax.broadcasted_iota(jnp.int32, raw.shape, 1))
    return jnp.where(allowed, raw, NEG_FILL)


def column_max(a):
    return jnp.max(a, axis=0, keepdims=True)


def column_sum(a):
    return jnp.sum(a, axis=0, keepdims=True)


def own_forward_kernel(
    lo_ref, place_ref, start_row, queries, far, kv_own, top_row, total_row, acc_out,
    keys, values, values_t, scores,
):
    tile, tiles = scores.shape[1], scores.shape[0]
    core = place_ref[0]
    before = REACH * tiles // 2
    for j in range(tiles):
        span = core if j < tiles // 2 else 1 - core
        rows = pl.ds(j % (tiles // 2) * (tile // kv_own.shape[3]), tile // kv_own.shape[3])
        keys[j] = kv_own[span, rows, 0].reshape(keys.shape[1:])
        values_t[j] = kv_own[span, rows, 1].reshape(keys.shape[1:]).T
    for i in range(tiles):
        columns = pl.ds(i * tile, tile)
        query = query_tile(queries, far, 0, core, i, tile)
        start = start_row[:, columns]
        lo = jnp.maximum(lo_ref[i] - before, 0)

        def score_tile(j, causal):
            raw = masked_scores(keys[j], query, start, j + before, tile, causal)
            scores[j] = raw
            return column_max(raw)

        top = lax.fori_loop(
            lo, i, lambda j, m: jnp.maximum(m, score_tile(j, False)), score_tile(i, True)
        )

        def forward(j, carry):
            total, acc = carry
            prob = jnp.exp2(scores[j] - top)
            return total + column_sum(prob), acc + matmul(values_t[j], prob.astype(jnp.bfloat16))

        total, acc = lax.fori_loop(
            lo, i + 1, forward, (jnp.zeros_like(top), jnp.zeros(acc_out.shape[1:], jnp.float32))
        )
        top_row[:, columns] = top
        total_row[:, columns] = total
        acc_out[i] = acc


def earlier_kernel(
    lo_ref, place_ref, start_row, queries, out_grad, far, top_row, total_row, acc_in, kv_prev,
    attended_out, lse_row, delta_row, acc_out, p_near, p_next,
    keys_t, values_t, scores, key_acc, value_acc,
):
    tile, before = scores.shape[1], scores.shape[0]
    tiles = acc_in.shape[0]
    scale = queries.shape[2] ** -0.5
    core = place_ref[0]
    bf16, f32 = jnp.bfloat16, jnp.float32
    first = lo_ref[0]

    @pl.when(first < before)
    def _():
        key_acc[...] = jnp.zeros_like(key_acc)
        value_acc[...] = jnp.zeros_like(value_acc)

        def turn(j, carry):
            keys_t[j] = key_tile(kv_prev, j, 0, tile).T
            values_t[j] = key_tile(kv_prev, j, 1, tile).T
            return carry

        lax.fori_loop(first, before, turn, 0)

    for i in range(tiles):
        columns = pl.ds(i * tile, tile)
        query = query_tile(queries, far, 0, core, i, tile)
        grad = query_tile(out_grad, far, 1, core, i, tile)
        start = start_row[:, columns]
        lo = jnp.minimum(lo_ref[i], before)
        own_top = top_row[:, columns]

        def score_tile(j, top):
            raw = masked_scores(key_tile(kv_prev, j, 0, tile), query, start, j, tile, False)
            scores[j] = raw
            return jnp.maximum(top, column_max(raw))

        top = lax.fori_loop(lo, before, score_tile, own_top)
        shrink = jnp.exp2(own_top - top)

        def forward(j, carry):
            total, acc = carry
            prob = jnp.exp2(scores[j] - top)
            scores[j] = prob
            return total + column_sum(prob), acc + matmul(values_t[j], prob.astype(bf16))

        total, acc = lax.fori_loop(
            lo, before, forward, (total_row[:, columns] * shrink, acc_in[i] * shrink)
        )
        inv = 1.0 / total
        attended_t = (acc * inv).astype(bf16).astype(f32)
        delta = column_sum(grad.astype(f32).T * attended_t)
        half, part = divmod(i, tiles // 2)
        attended_out[half, pl.ds(part * tile, tile)] = attended_t.T.astype(bf16)
        lse_row[:, columns] = top + jnp.log2(total)
        delta_row[:, columns] = delta

        def backward(j, acc):
            prob = scores[j] * inv
            here = pl.ds(pl.multiple_of(j * tile, tile), tile)
            value_acc[here] += matmul(prob.astype(bf16), grad)
            dot_grad = matmul(key_tile(kv_prev, j, 1, tile), grad, NT)
            score_grad = (prob * (dot_grad - delta)).astype(bf16)
            key_acc[here] += matmul(score_grad, query)
            return acc + matmul(keys_t[j], score_grad)

        acc_out[i] = lax.fori_loop(lo, before, backward, jnp.zeros(acc_out.shape[1:], f32))

    shards, shard = kv_prev.shape[1], kv_prev.shape[3]

    @pl.when(first < before)
    def _():
        for slot, target in enumerate((p_next, p_near.at[0], p_near.at[1])):
            for row in range(shards):
                here = pl.ds((slot * shards + row) * shard, shard)
                target[row, 0] = (key_acc[here] * scale).astype(bf16)
                target[row, 1] = value_acc[here].astype(bf16)

    @pl.when(first >= before)
    def _():
        p_next[...] = jnp.zeros_like(p_next)
        p_near[...] = jnp.zeros_like(p_near)


def own_backward_kernel(
    lo_ref, place_ref, start_row, queries, out_grad, far, kv_own, attended, lse_row, delta_row,
    acc_in, out_own, out_far, p_own,
    keys, values, keys_t, key_acc, value_acc,
):
    tiles, tile = keys.shape[0], keys.shape[1]
    scale = queries.shape[2] ** -0.5
    core = place_ref[0]
    bf16, f32 = jnp.bfloat16, jnp.float32
    before = REACH * tiles // 2
    for j in range(tiles):
        span = core if j < tiles // 2 else 1 - core
        rows = pl.ds(j % (tiles // 2) * (tile // kv_own.shape[3]), tile // kv_own.shape[3])
        block = kv_own[span, rows, 0].reshape(keys.shape[1:])
        keys[j] = block
        keys_t[j] = block.T
        values[j] = kv_own[span, rows, 1].reshape(keys.shape[1:])
    key_acc[...] = jnp.zeros_like(key_acc)
    value_acc[...] = jnp.zeros_like(value_acc)
    for i in range(tiles):
        columns = pl.ds(i * tile, tile)
        query = query_tile(queries, far, 0, core, i, tile)
        grad = query_tile(out_grad, far, 1, core, i, tile)
        start = start_row[:, columns]
        lse, delta = lse_row[:, columns], delta_row[:, columns]

        def backward(j, acc, causal):
            raw = masked_scores(keys[j], query, start, j + before, tile, causal)
            prob = jnp.exp2(raw - lse)
            value_acc[j] += matmul(prob.astype(bf16), grad)
            score_grad = (prob * (matmul(values[j], grad, NT) - delta)).astype(bf16)
            key_acc[j] += matmul(score_grad, query)
            return acc + matmul(keys_t[j], score_grad)

        acc = backward(i, acc_in[i], True)
        acc = lax.fori_loop(
            jnp.maximum(lo_ref[i] - before, 0), i, lambda j, acc: backward(j, acc, False), acc
        )
        half, part = divmod(i, tiles // 2)
        rows = pl.ds(part * tile, tile)
        (out_own, out_far)[half][1, rows] = (acc.T * scale).astype(bf16)
    out_own[0] = attended[0]
    out_far[0] = attended[1]
    shards, shard = kv_own.shape[1], kv_own.shape[3]
    for span in range(2):
        for row in range(shards):
            j, part = divmod((span * shards + row) * shard, tile)
            here = pl.ds(part, shard)
            p_own[span, row, 0] = key_acc[j, here] * scale
            p_own[span, row, 1] = value_acc[j, here]


def vmem_kernel(kernel, name, outputs, scratch, tiles, tile, head_dim, matmuls):
    def call(*operands):
        rest = [pl.BlockSpec(memory_space=pltpu.VMEM)] * (len(operands) - 2)
        return pl.pallas_call(
            kernel,
            out_shape=outputs,
            in_specs=[pl.BlockSpec(memory_space=pltpu.SMEM)] * 2 + rest,
            out_specs=[pl.BlockSpec(memory_space=pltpu.VMEM)] * len(outputs),
            scratch_shapes=[pltpu.VMEM(shape, dtype) for shape, dtype in scratch],
            compiler_params=pltpu.CompilerParams(vmem_limit_bytes=24 * 1024 * 1024),
            cost_estimate=pl.CostEstimate(
                flops=2 * matmuls * tiles * tile * tile * head_dim,
                bytes_accessed=4 * 1024 * 1024,
                transcendentals=tiles * tile * tile,
            ),
            name=name,
        )(*operands)

    return call


def body(queries, key_states, value_states, out_grad, segments):
    ctx = lax.axis_size("pair") * 2
    core = lax.axis_index("core")
    position = lax.axis_index("pair") * 2 + core
    place = position % GROUP
    width = queries.shape[2]
    heads = lax.axis_size("head")
    shard = key_states.shape[2]
    head_dim = key_states.shape[3]
    bf16, f32 = jnp.bfloat16, jnp.float32

    swap, near, far_chip = swap_pairs(ctx), near_pairs(ctx), next_pairs(ctx)
    edge1 = within(ctx, [(2, 0), (GROUP - 3, GROUP - 1)])
    edge2 = within(ctx, [(1, 0), (GROUP - 2, GROUP - 1)])
    everywhere = CTX + ("head",)
    even = core == 0
    sends_lower = place >= GROUP - REACH
    head = lax.axis_index("head")
    bits = folds(heads)
    high = {bit: (head & bit) != 0 for bit in bits}
    edge = edge_pairs(ctx, heads)

    lower = jnp.stack([key_states[0, 0], value_states[0, 0]])
    upper = jnp.stack([key_states[0, 1], value_states[0, 1]])
    leaving = pick(sends_lower, upper, lower)
    half = by_bit(core, pick(even, upper, lower), lax.ppermute(pick(even, lower, upper), CTX, swap), 0)
    kv_own = half
    for k, bit in enumerate(bits):
        other = lax.ppermute(kv_own, everywhere, head_pairs(ctx, heads, bit))
        if k == 0:
            arrived = lax.ppermute(leaving, everywhere, edge)
        else:
            arrived = lax.ppermute(kv_edge, everywhere, holder_pairs(ctx, heads, bits[k - 1]))
        other, arrived = lax.optimization_barrier((other, arrived))
        kv_own = by_bit(high[bit], kv_own, other, 1 + k)
        kv_edge = arrived if k == 0 else by_bit(~high[bits[k - 1]], kv_edge, arrived, k - 1)
    arrived = lax.ppermute(kv_edge, everywhere, holder_pairs(ctx, heads, bits[-1]))
    kv_edge = by_bit(~high[bits[-1]], kv_edge, arrived, len(bits) - 1)
    kv_own = kv_own.reshape((2, heads) + half.shape[1:])
    kv_edge = kv_edge.reshape((heads,) + half.shape[1:])

    queries, out_grad = queries[0], out_grad[0]
    far = lax.ppermute(
        jnp.where(
            even,
            jnp.stack([queries[1], out_grad[1]]),
            jnp.stack([queries[0], out_grad[0]]),
        ),
        CTX,
        swap,
    )

    kv_next = lax.ppermute(jnp.where(even, kv_own[1], kv_own[0]), CTX, far_chip)
    kv_near = lax.ppermute(kv_own, CTX, near)
    kv_edge1 = lax.ppermute(kv_edge, CTX, edge1)
    kv_edge2 = lax.ppermute(kv_edge, CTX, edge2)

    first = jnp.where(even, position, 2 * ctx - 1 - position)
    window = (REACH + 2) * width
    padded = jnp.concatenate([jnp.full((REACH * width,), -1, jnp.int32), segments])
    seg_window = lax.dynamic_slice_in_dim(padded, first * width, window)
    start = jnp.sum(
        seg_window[:, None] < seg_window[None, REACH * width :], axis=0, dtype=jnp.int32
    )
    tile = max(min(256, width // 2), shard)
    tiles, earlier = 2 * width // tile, REACH * width // tile
    lo = start[::tile] // tile
    edge_next = jnp.where(even, place <= 2, place >= GROUP - 3)
    edge_near = jnp.where(even, place == 0, place == GROUP - 1)
    places = core[None].astype(jnp.int32)
    start = start[None, :]

    near_ordered = jnp.where(even, kv_near, kv_near[::-1])
    kv_prev = jnp.stack(
        [
            jnp.where(edge_next, kv_edge, kv_next),
            jnp.where(edge_near, kv_edge2, near_ordered[0]),
            jnp.where(edge_near, kv_edge1, near_ordered[1]),
        ]
    )

    row = jax.ShapeDtypeStruct((1, 2 * width), f32)
    turned = jax.ShapeDtypeStruct((tiles, head_dim, tile), f32)
    part = jax.ShapeDtypeStruct((2, width, head_dim), bf16)
    span_like = kv_next.shape
    natural = ((tiles, tile, head_dim), bf16)
    top, total, acc = vmem_kernel(
        own_forward_kernel, "own_forward", (row, row, turned),
        [natural, natural, ((tiles, head_dim, tile), bf16), ((tiles, tile, tile), f32)],
        6, tile, head_dim, 2,
    )(lo, places, start, queries, far, kv_own)
    attended, lse, delta, acc, p_near, p_next = vmem_kernel(
        earlier_kernel, "earlier",
        (
            part, row, row, turned,
            jax.ShapeDtypeStruct((2,) + span_like, bf16),
            jax.ShapeDtypeStruct(span_like, bf16),
        ),
        [
            ((earlier, head_dim, tile), bf16),
            ((earlier, head_dim, tile), bf16),
            ((earlier, tile, tile), f32),
            ((earlier * tile, head_dim), f32),
            ((earlier * tile, head_dim), f32),
        ],
        6, tile, head_dim, 6,
    )(lo, places, start, queries, out_grad, far, top, total, acc, kv_prev)

    r_edge1 = lax.ppermute(p_near[1], CTX, inverse(edge1)).astype(f32)
    r_edge2 = lax.ppermute(p_near[0], CTX, inverse(edge2)).astype(f32)
    r_next = lax.ppermute(p_next, CTX, inverse(far_chip)).astype(f32)
    r_near = lax.ppermute(p_near, CTX, inverse(near)).astype(f32)

    out_own, out_far, p_own = vmem_kernel(
        own_backward_kernel, "own_backward",
        (part, part, jax.ShapeDtypeStruct((2,) + span_like, f32)),
        [natural, natural, ((tiles, head_dim, tile), bf16)]
        + [((tiles, tile, head_dim), f32)] * 2,
        6, tile, head_dim, 5,
    )(lo, places, start, queries, out_grad, far, kv_own, attended, lse, delta, acc)

    edge_sum = jnp.where(edge_next, p_next.astype(f32), 0.0) + r_edge1 + r_edge2
    for bit in reversed(bits):
        halves = edge_sum.reshape((-1, 2) + half.shape[1:])
        away = pick(high[bit], halves[:, 0], halves[:, 1]).astype(bf16)
        other = lax.ppermute(away, everywhere, holder_pairs(ctx, heads, bit))
        edge_sum = pick(high[bit], halves[:, 1], halves[:, 0]) + other.astype(f32)
    returned = lax.ppermute(edge_sum[0].astype(bf16), everywhere, inverse(edge)).astype(f32)

    sums = p_own + r_near
    first_sum, second_sum = sums[0], sums[1] + r_next
    sums = jnp.stack([pick(even, second_sum, first_sum), pick(even, first_sum, second_sum)])
    for bit in reversed(bits):
        halves = sums.reshape((2, -1, 2) + half.shape[1:])
        away = pick(high[bit], halves[:, :, 1], halves[:, :, 0]).astype(bf16)
        other = lax.ppermute(away, everywhere, head_pairs(ctx, heads, bit))
        sums = pick(high[bit], halves[:, :, 0], halves[:, :, 1]) + other.astype(f32)
    stays = sums[:, 0]
    own_half = pick(even, stays[1], stays[0])
    far_half = lax.ppermute(
        pick(even, stays[0], stays[1]).astype(bf16), CTX, swap
    ).astype(f32)
    lower = pick(even, far_half, own_half) + jnp.where(sends_lower, returned, 0.0)
    upper = pick(even, own_half, far_half) + jnp.where(sends_lower, 0.0, returned)
    grads = jnp.stack([lower, upper]).astype(bf16)

    back = lax.ppermute(out_far, CTX, swap)
    results = []
    for k in range(2):
        results.append(
            jnp.where(
                even, jnp.stack([out_own[k], back[k]]), jnp.stack([back[k], out_own[k]])
            )[None]
        )
    return results[0], results[1], grads[:, 0][None], grads[:, 1][None]


def solution(mesh):
    ctx, heads = mesh.devices.shape
    mesh = Mesh(mesh.devices.reshape(ctx // 2, 2, heads), CTX + ("head",))
    by_head = P(CTX, None, None, "head")
    by_row = P(CTX, None, "head", None)
    return jax.shard_map(
        body,
        mesh=mesh,
        in_specs=(by_head, by_row, by_row, by_head, P()),
        out_specs=(by_head, by_head, by_row, by_row),
        check_vma=False,
    )
```

```python
import math

import jax
import jax.numpy as jnp
from jax import lax
from jax.experimental import pallas as pl
from jax.experimental.pallas import tpu as pltpu
from jax.sharding import Mesh
from jax.sharding import PartitionSpec as P

REACH = 3
GROUP = 8
NEG_FILL = -1e30
CTX = ("pair", "core")


def within(ctx, moves):
    return [(base + a, base + b) for base in range(0, ctx, GROUP) for a, b in moves]


def swap_pairs(ctx):
    return within(ctx, [(r, r ^ 1) for r in range(GROUP)])


def near_pairs(ctx):
    forth = [(r, r + 2) for r in range(0, GROUP - 2, 2)]
    return within(ctx, forth + [(r, r - 2) for r in range(3, GROUP, 2)])


def next_pairs(ctx):
    forth = [(r, r + 4) for r in range(0, GROUP - 4, 2)]
    return within(ctx, forth + [(r, r - 4) for r in range(5, GROUP, 2)])


def head_pairs(ctx, heads, bit):
    return [(d, d ^ bit) for d in range(ctx * heads)]


def cross_pairs(ctx, heads, bit):
    return [
        (c * heads + h, (c ^ 1) * heads + (h ^ bit)) for c in range(ctx) for h in range(heads)
    ]


def edge_pairs(ctx, heads, flip):
    moves = []
    for base in range(0, ctx, GROUP):
        for k in range(REACH):
            top = base + GROUP - 1 - k
            if base + GROUP < ctx:
                moves.append((top, base + GROUP + REACH - 1 - k))
            else:
                moves.append((top, base + GROUP - REACH + k))
            if base > 0:
                moves.append((base + k, base - REACH + k))
    return [
        (a * heads + h, b * heads + (h ^ flip)) for a, b in moves for h in range(heads)
    ]


def folds(heads):
    return [1 << k for k in reversed(range(heads.bit_length() - 1))]


def pick(bit, low, high):
    return jnp.where(bit, high, low)


def by_bit(bit, mine, other, axis):
    mine, other = jnp.expand_dims(mine, axis), jnp.expand_dims(other, axis)
    place = lax.broadcasted_iota(jnp.int32, (2,) + (1,) * (mine.ndim - axis - 1), 0)
    return jnp.where(place == bit.astype(jnp.int32), mine, other)


def inverse(pairs):
    return [(b, a) for a, b in pairs]


NT = (((1,), (1,)), ((), ()))
NN = (((1,), (0,)), ((), ()))


def matmul(a, b, dims=NN):
    return lax.dot_general(a, b, dims, preferred_element_type=jnp.float32)


def key_tile(ref, j, which, tile):
    _, shards, _, shard, head_dim = ref.shape
    per_span = shards * shard // tile
    rows = pl.ds((j % per_span) * (tile // shard), tile // shard)
    return ref[j // per_span, rows, which].reshape(tile, head_dim)


def query_tile(own_ref, far_ref, far_index, core, i, tile):
    width = far_ref.shape[1]
    span, part = divmod(i, width // tile)
    rows = pl.ds(part * tile, tile)
    return own_ref[core, rows] if span == 0 else far_ref[far_index, rows]


def masked_scores(keys, query, start, j, tile, causal):
    raw = matmul(keys, query, NT) * (query.shape[1] ** -0.5 * math.log2(math.e))
    at_key = lax.broadcasted_iota(jnp.int32, raw.shape, 0)
    allowed = at_key >= start - j * tile
    if causal:
        allowed = allowed & (at_key <= lax.broadcasted_iota(jnp.int32, raw.shape, 1))
    return jnp.where(allowed, raw, NEG_FILL)


def column_max(a):
    return jnp.max(a, axis=0, keepdims=True)


def column_sum(a):
    return jnp.sum(a, axis=0, keepdims=True)


def own_forward_kernel(
    lo_ref, place_ref, start_row, queries, far, kv_own, top_row, total_row, acc_out,
    keys, values, values_t, scores,
):
    tile, tiles = scores.shape[1], scores.shape[0]
    core = place_ref[0]
    before = REACH * tiles // 2
    for j in range(tiles):
        span = core if j < tiles // 2 else 1 - core
        rows = pl.ds(j % (tiles // 2) * (tile // kv_own.shape[3]), tile // kv_own.shape[3])
        keys[j] = kv_own[span, rows, 0].reshape(keys.shape[1:])
        values_t[j] = kv_own[span, rows, 1].reshape(keys.shape[1:]).T
    for i in range(tiles):
        columns = pl.ds(i * tile, tile)
        query = query_tile(queries, far, 0, core, i, tile)
        start = start_row[:, columns]
        lo = jnp.maximum(lo_ref[i] - before, 0)

        def score_tile(j, causal):
            raw = masked_scores(keys[j], query, start, j + before, tile, causal)
            scores[j] = raw
            return column_max(raw)

        top = lax.fori_loop(
            lo, i, lambda j, m: jnp.maximum(m, score_tile(j, False)), score_tile(i, True)
        )

        def forward(j, carry):
            total, acc = carry
            prob = jnp.exp2(scores[j] - top)
            return total + column_sum(prob), acc + matmul(values_t[j], prob.astype(jnp.bfloat16))

        total, acc = lax.fori_loop(
            lo, i + 1, forward, (jnp.zeros_like(top), jnp.zeros(acc_out.shape[1:], jnp.float32))
        )
        top_row[:, columns] = top
        total_row[:, columns] = total
        acc_out[i] = acc


def earlier_kernel(
    lo_ref, place_ref, start_row, queries, out_grad, far, top_row, total_row, acc_in, kv_prev,
    attended_out, lse_row, delta_row, acc_out, p_near, p_next,
    keys_t, values_t, scores, key_acc, value_acc,
):
    tile, before = scores.shape[1], scores.shape[0]
    tiles = acc_in.shape[0]
    scale = queries.shape[2] ** -0.5
    core = place_ref[0]
    bf16, f32 = jnp.bfloat16, jnp.float32
    first = lo_ref[0]

    @pl.when(first < before)
    def _():
        key_acc[...] = jnp.zeros_like(key_acc)
        value_acc[...] = jnp.zeros_like(value_acc)

        def turn(j, carry):
            keys_t[j] = key_tile(kv_prev, j, 0, tile).T
            values_t[j] = key_tile(kv_prev, j, 1, tile).T
            return carry

        lax.fori_loop(first, before, turn, 0)

    for i in range(tiles):
        columns = pl.ds(i * tile, tile)
        query = query_tile(queries, far, 0, core, i, tile)
        grad = query_tile(out_grad, far, 1, core, i, tile)
        start = start_row[:, columns]
        lo = jnp.minimum(lo_ref[i], before)
        own_top = top_row[:, columns]

        def score_tile(j, top):
            raw = masked_scores(key_tile(kv_prev, j, 0, tile), query, start, j, tile, False)
            scores[j] = raw
            return jnp.maximum(top, column_max(raw))

        top = lax.fori_loop(lo, before, score_tile, own_top)
        shrink = jnp.exp2(own_top - top)

        def forward(j, carry):
            total, acc = carry
            prob = jnp.exp2(scores[j] - top)
            scores[j] = prob
            return total + column_sum(prob), acc + matmul(values_t[j], prob.astype(bf16))

        total, acc = lax.fori_loop(
            lo, before, forward, (total_row[:, columns] * shrink, acc_in[i] * shrink)
        )
        inv = 1.0 / total
        attended_t = (acc * inv).astype(bf16).astype(f32)
        delta = column_sum(grad.astype(f32).T * attended_t)
        half, part = divmod(i, tiles // 2)
        attended_out[half, pl.ds(part * tile, tile)] = attended_t.T.astype(bf16)
        lse_row[:, columns] = top + jnp.log2(total)
        delta_row[:, columns] = delta

        def backward(j, acc):
            prob = scores[j] * inv
            here = pl.ds(pl.multiple_of(j * tile, tile), tile)
            value_acc[here] += matmul(prob.astype(bf16), grad)
            dot_grad = matmul(key_tile(kv_prev, j, 1, tile), grad, NT)
            score_grad = (prob * (dot_grad - delta)).astype(bf16)
            key_acc[here] += matmul(score_grad, query)
            return acc + matmul(keys_t[j], score_grad)

        acc_out[i] = lax.fori_loop(lo, before, backward, jnp.zeros(acc_out.shape[1:], f32))

    shards, shard = kv_prev.shape[1], kv_prev.shape[3]

    @pl.when(first < before)
    def _():
        for slot, target in enumerate((p_next, p_near.at[0], p_near.at[1])):
            for row in range(shards):
                here = pl.ds((slot * shards + row) * shard, shard)
                target[row, 0] = (key_acc[here] * scale).astype(bf16)
                target[row, 1] = value_acc[here].astype(bf16)

    @pl.when(first >= before)
    def _():
        p_next[...] = jnp.zeros_like(p_next)
        p_near[...] = jnp.zeros_like(p_near)


def own_backward_kernel(
    lo_ref, place_ref, start_row, queries, out_grad, far, kv_own, attended, lse_row, delta_row,
    acc_in, out_own, out_far, p_own,
    keys, values, keys_t, key_acc, value_acc,
):
    tiles, tile = keys.shape[0], keys.shape[1]
    scale = queries.shape[2] ** -0.5
    core = place_ref[0]
    bf16, f32 = jnp.bfloat16, jnp.float32
    before = REACH * tiles // 2
    for j in range(tiles):
        span = core if j < tiles // 2 else 1 - core
        rows = pl.ds(j % (tiles // 2) * (tile // kv_own.shape[3]), tile // kv_own.shape[3])
        block = kv_own[span, rows, 0].reshape(keys.shape[1:])
        keys[j] = block
        keys_t[j] = block.T
        values[j] = kv_own[span, rows, 1].reshape(keys.shape[1:])
    key_acc[...] = jnp.zeros_like(key_acc)
    value_acc[...] = jnp.zeros_like(value_acc)
    for i in range(tiles):
        columns = pl.ds(i * tile, tile)
        query = query_tile(queries, far, 0, core, i, tile)
        grad = query_tile(out_grad, far, 1, core, i, tile)
        start = start_row[:, columns]
        lse, delta = lse_row[:, columns], delta_row[:, columns]

        def backward(j, acc, causal):
            raw = masked_scores(keys[j], query, start, j + before, tile, causal)
            prob = jnp.exp2(raw - lse)
            value_acc[j] += matmul(prob.astype(bf16), grad)
            score_grad = (prob * (matmul(values[j], grad, NT) - delta)).astype(bf16)
            key_acc[j] += matmul(score_grad, query)
            return acc + matmul(keys_t[j], score_grad)

        acc = backward(i, acc_in[i], True)
        acc = lax.fori_loop(
            jnp.maximum(lo_ref[i] - before, 0), i, lambda j, acc: backward(j, acc, False), acc
        )
        half, part = divmod(i, tiles // 2)
        rows = pl.ds(part * tile, tile)
        (out_own, out_far)[half][1, rows] = (acc.T * scale).astype(bf16)
    out_own[0] = attended[0]
    out_far[0] = attended[1]
    shards, shard = kv_own.shape[1], kv_own.shape[3]
    for span in range(2):
        for row in range(shards):
            j, part = divmod((span * shards + row) * shard, tile)
            here = pl.ds(part, shard)
            p_own[span, row, 0] = key_acc[j, here] * scale
            p_own[span, row, 1] = value_acc[j, here]


def vmem_kernel(kernel, name, outputs, scratch, tiles, tile, head_dim, matmuls):
    def call(*operands):
        rest = [pl.BlockSpec(memory_space=pltpu.VMEM)] * (len(operands) - 2)
        return pl.pallas_call(
            kernel,
            out_shape=outputs,
            in_specs=[pl.BlockSpec(memory_space=pltpu.SMEM)] * 2 + rest,
            out_specs=[pl.BlockSpec(memory_space=pltpu.VMEM)] * len(outputs),
            scratch_shapes=[pltpu.VMEM(shape, dtype) for shape, dtype in scratch],
            compiler_params=pltpu.CompilerParams(vmem_limit_bytes=24 * 1024 * 1024),
            cost_estimate=pl.CostEstimate(
                flops=2 * matmuls * tiles * tile * tile * head_dim,
                bytes_accessed=4 * 1024 * 1024,
                transcendentals=tiles * tile * tile,
            ),
            name=name,
        )(*operands)

    return call


def body(queries, key_states, value_states, out_grad, segments):
    ctx = lax.axis_size("pair") * 2
    core = lax.axis_index("core")
    position = lax.axis_index("pair") * 2 + core
    place = position % GROUP
    width = queries.shape[2]
    heads = lax.axis_size("head")
    shard = key_states.shape[2]
    head_dim = key_states.shape[3]
    bf16, f32 = jnp.bfloat16, jnp.float32

    swap, near, far_chip = swap_pairs(ctx), near_pairs(ctx), next_pairs(ctx)
    edge1 = within(ctx, [(2, 0), (GROUP - 3, GROUP - 1)])
    edge2 = within(ctx, [(1, 0), (GROUP - 2, GROUP - 1)])
    everywhere = CTX + ("head",)
    even = core == 0
    sends_lower = place >= GROUP - REACH
    head = lax.axis_index("head")
    bits = folds(heads)
    far_bit = bits[0]
    high = {bit: (head & bit) != 0 for bit in bits}
    cross = cross_pairs(ctx, heads, far_bit)
    mirrored = edge_pairs(ctx, heads, heads - 1)
    folded = edge_pairs(ctx, heads, heads - 1 - far_bit)
    is_edge = lax.broadcasted_iota(jnp.int32, (3, 1, 1, 1, 1), 0) == 2

    lower = jnp.stack([key_states[0, 0], value_states[0, 0]])
    upper = jnp.stack([key_states[0, 1], value_states[0, 1]])
    leaving = pick(sends_lower, upper, lower)
    mine, theirs = pick(even, upper, lower), pick(even, lower, upper)
    edge_far = lax.ppermute(leaving, everywhere, mirrored)
    near_core = lax.ppermute(theirs, CTX, swap)
    near_head = lax.ppermute(mine, everywhere, head_pairs(ctx, heads, far_bit))
    far_core = lax.ppermute(theirs, everywhere, cross)
    leaving, near_core = lax.optimization_barrier((leaving, near_core))
    edge_near = lax.ppermute(leaving, everywhere, folded)
    kv_own = by_bit(
        core,
        by_bit(high[far_bit], mine, near_head, 0),
        by_bit(high[far_bit], near_core, far_core, 0),
        0,
    )
    kv_all = jnp.concatenate([kv_own, by_bit(high[far_bit], edge_near, edge_far, 0)[None]])
    for bit in bits[1:]:
        other = lax.ppermute(kv_all, everywhere, head_pairs(ctx, heads, bit))
        slot = lax.broadcasted_iota(jnp.int32, (2, 1, 1, 1), 0) == 1
        stays = slot == (high[bit] ^ is_edge)[:, None]
        kv_all = jnp.where(stays, kv_all[:, :, None], other[:, :, None])
        kv_all = kv_all.reshape((3, -1) + mine.shape)
    kv_own, kv_edge = kv_all[:2], kv_all[2]

    queries, out_grad = queries[0], out_grad[0]
    far = lax.ppermute(
        jnp.where(
            even,
            jnp.stack([queries[1], out_grad[1]]),
            jnp.stack([queries[0], out_grad[0]]),
        ),
        CTX,
        swap,
    )

    kv_next = lax.ppermute(jnp.where(even, kv_own[1], kv_own[0]), CTX, far_chip)
    kv_near = lax.ppermute(kv_own, CTX, near)
    kv_edge1 = lax.ppermute(kv_edge, CTX, edge1)
    kv_edge2 = lax.ppermute(kv_edge, CTX, edge2)

    first = jnp.where(even, position, 2 * ctx - 1 - position)
    window = (REACH + 2) * width
    padded = jnp.concatenate([jnp.full((REACH * width,), -1, jnp.int32), segments])
    seg_window = lax.dynamic_slice_in_dim(padded, first * width, window)
    start = jnp.sum(
        seg_window[:, None] < seg_window[None, REACH * width :], axis=0, dtype=jnp.int32
    )
    tile = max(min(256, width // 2), shard)
    tiles, earlier = 2 * width // tile, REACH * width // tile
    lo = start[::tile] // tile
    edge_next = jnp.where(even, place <= 2, place >= GROUP - 3)
    edge_near = jnp.where(even, place == 0, place == GROUP - 1)
    places = core[None].astype(jnp.int32)
    start = start[None, :]

    near_ordered = jnp.where(even, kv_near, kv_near[::-1])
    kv_prev = jnp.stack(
        [
            jnp.where(edge_next, kv_edge, kv_next),
            jnp.where(edge_near, kv_edge2, near_ordered[0]),
            jnp.where(edge_near, kv_edge1, near_ordered[1]),
        ]
    )

    row = jax.ShapeDtypeStruct((1, 2 * width), f32)
    turned = jax.ShapeDtypeStruct((tiles, head_dim, tile), f32)
    part = jax.ShapeDtypeStruct((2, width, head_dim), bf16)
    span_like = kv_next.shape
    natural = ((tiles, tile, head_dim), bf16)
    top, total, acc = vmem_kernel(
        own_forward_kernel, "own_forward", (row, row, turned),
        [natural, natural, ((tiles, head_dim, tile), bf16), ((tiles, tile, tile), f32)],
        6, tile, head_dim, 2,
    )(lo, places, start, queries, far, kv_own)
    attended, lse, delta, acc, p_near, p_next = vmem_kernel(
        earlier_kernel, "earlier",
        (
            part, row, row, turned,
            jax.ShapeDtypeStruct((2,) + span_like, bf16),
            jax.ShapeDtypeStruct(span_like, bf16),
        ),
        [
            ((earlier, head_dim, tile), bf16),
            ((earlier, head_dim, tile), bf16),
            ((earlier, tile, tile), f32),
            ((earlier * tile, head_dim), f32),
            ((earlier * tile, head_dim), f32),
        ],
        6, tile, head_dim, 6,
    )(lo, places, start, queries, out_grad, far, top, total, acc, kv_prev)

    r_edge1 = lax.ppermute(p_near[1], CTX, inverse(edge1)).astype(f32)
    r_edge2 = lax.ppermute(p_near[0], CTX, inverse(edge2)).astype(f32)
    r_next = lax.ppermute(p_next, CTX, inverse(far_chip)).astype(f32)
    r_near = lax.ppermute(p_near, CTX, inverse(near)).astype(f32)

    out_own, out_far, p_own = vmem_kernel(
        own_backward_kernel, "own_backward",
        (part, part, jax.ShapeDtypeStruct((2,) + span_like, f32)),
        [natural, natural, ((tiles, head_dim, tile), bf16)]
        + [((tiles, tile, head_dim), f32)] * 2,
        6, tile, head_dim, 5,
    )(lo, places, start, queries, out_grad, far, kv_own, attended, lse, delta, acc)

    edge_sum = jnp.where(edge_next, p_next.astype(f32), 0.0) + r_edge1 + r_edge2
    sums = p_own + r_near
    first_sum, second_sum = sums[0], sums[1] + r_next
    sums = jnp.stack(
        [pick(even, second_sum, first_sum), pick(even, first_sum, second_sum), edge_sum]
    )
    for bit in reversed(bits[1:]):
        halves = sums.reshape((3, -1, 2) + mine.shape)
        high_half = high[bit] ^ is_edge
        away = jnp.where(high_half, halves[:, :, 0], halves[:, :, 1]).astype(bf16)
        other = lax.ppermute(away, everywhere, head_pairs(ctx, heads, bit))
        sums = jnp.where(high_half, halves[:, :, 1], halves[:, :, 0]) + other.astype(f32)
    stays = pick(high[far_bit], sums[:, 0], sums[:, 1])
    away = pick(high[far_bit], sums[:, 1], sums[:, 0])
    own_half = pick(even, stays[1], stays[0])
    sent_head = pick(even, away[1], away[0]).astype(bf16)
    sent_core = pick(even, stays[0], stays[1]).astype(bf16)
    sent_cross = pick(even, away[0], away[1]).astype(bf16)
    from_far = lax.ppermute(away[2].astype(bf16), everywhere, inverse(mirrored))
    far_half = lax.ppermute(sent_core, CTX, swap)
    from_head = lax.ppermute(sent_head, everywhere, head_pairs(ctx, heads, far_bit))
    from_cross = lax.ppermute(sent_cross, everywhere, cross)
    folded_back, far_half = lax.optimization_barrier((stays[2].astype(bf16), far_half))
    from_near = lax.ppermute(folded_back, everywhere, inverse(folded))
    own_half = own_half + from_head.astype(f32)
    far_half = far_half.astype(f32) + from_cross.astype(f32)
    returned = from_near.astype(f32) + from_far.astype(f32)
    lower = pick(even, far_half, own_half) + jnp.where(sends_lower, returned, 0.0)
    upper = pick(even, own_half, far_half) + jnp.where(sends_lower, 0.0, returned)
    grads = jnp.stack([lower, upper]).astype(bf16)

    back = lax.ppermute(out_far, CTX, swap)
    results = []
    for k in range(2):
        results.append(
            jnp.where(
                even, jnp.stack([out_own[k], back[k]]), jnp.stack([back[k], out_own[k]])
            )[None]
        )
    return results[0], results[1], grads[:, 0][None], grads[:, 1][None]


def solution(mesh):
    ctx, heads = mesh.devices.shape
    mesh = Mesh(mesh.devices.reshape(ctx // 2, 2, heads), CTX + ("head",))
    by_head = P(CTX, None, None, "head")
    by_row = P(CTX, None, "head", None)
    return jax.shard_map(
        body,
        mesh=mesh,
        in_specs=(by_head, by_row, by_row, by_head, P()),
        out_specs=(by_head, by_head, by_row, by_row),
        check_vma=False,
    )
```

```python
import math

import jax
import jax.numpy as jnp
from jax import lax
from jax.experimental import pallas as pl
from jax.experimental.pallas import tpu as pltpu
from jax.sharding import Mesh
from jax.sharding import PartitionSpec as P

REACH = 3
GROUP = 8
NEG_FILL = -1e30
CTX = ("pair", "core")


def within(ctx, moves):
    return [(base + a, base + b) for base in range(0, ctx, GROUP) for a, b in moves]


def swap_pairs(ctx):
    return within(ctx, [(r, r ^ 1) for r in range(GROUP)])


def near_pairs(ctx):
    forth = [(r, r + 2) for r in range(0, GROUP - 2, 2)]
    return within(ctx, forth + [(r, r - 2) for r in range(3, GROUP, 2)])


def next_pairs(ctx):
    forth = [(r, r + 4) for r in range(0, GROUP - 4, 2)]
    return within(ctx, forth + [(r, r - 4) for r in range(5, GROUP, 2)])


def head_pairs(ctx, heads, bit):
    return [(d, d ^ bit) for d in range(ctx * heads)]


def holder_pairs(ctx, heads, bit):
    holders = [r for r in range(GROUP) if r < REACH or r >= GROUP - REACH]
    return [
        ((base + r) * heads + h, (base + r) * heads + (h ^ bit))
        for base in range(0, ctx, GROUP)
        for r in holders
        for h in range(heads)
    ]


def edge_pairs(ctx, heads):
    moves = []
    for base in range(0, ctx, GROUP):
        for k in range(REACH):
            top = base + GROUP - 1 - k
            if base + GROUP < ctx:
                moves.append((top, base + GROUP + REACH - 1 - k))
            else:
                moves.append((top, base + GROUP - REACH + k))
            if base > 0:
                moves.append((base + k, base - REACH + k))
    return [
        (a * heads + h, b * heads + heads - 1 - h) for a, b in moves for h in range(heads)
    ]


def folds(heads):
    return [1 << k for k in reversed(range(heads.bit_length() - 1))]


def pick(bit, low, high):
    return jnp.where(bit, high, low)


def by_bit(bit, mine, other, axis):
    mine, other = jnp.expand_dims(mine, axis), jnp.expand_dims(other, axis)
    place = lax.broadcasted_iota(jnp.int32, (2,) + (1,) * (mine.ndim - axis - 1), 0)
    return jnp.where(place == bit.astype(jnp.int32), mine, other)


def inverse(pairs):
    return [(b, a) for a, b in pairs]


NT = (((1,), (1,)), ((), ()))
NN = (((1,), (0,)), ((), ()))


def matmul(a, b, dims=NN):
    return lax.dot_general(a, b, dims, preferred_element_type=jnp.float32)


def key_tile(ref, j, which, tile):
    _, shards, _, shard, head_dim = ref.shape
    per_span = shards * shard // tile
    rows = pl.ds((j % per_span) * (tile // shard), tile // shard)
    return ref[j // per_span, rows, which].reshape(tile, head_dim)


def query_tile(own_ref, far_ref, far_index, core, i, tile):
    width = far_ref.shape[1]
    span, part = divmod(i, width // tile)
    rows = pl.ds(part * tile, tile)
    return own_ref[core, rows] if span == 0 else far_ref[far_index, rows]


def masked_scores(keys, query, start, j, tile, causal):
    raw = matmul(keys, query, NT) * (query.shape[1] ** -0.5 * math.log2(math.e))
    at_key = lax.broadcasted_iota(jnp.int32, raw.shape, 0)
    allowed = at_key >= start - j * tile
    if causal:
        allowed = allowed & (at_key <= lax.broadcasted_iota(jnp.int32, raw.shape, 1))
    return jnp.where(allowed, raw, NEG_FILL)


def column_max(a):
    return jnp.max(a, axis=0, keepdims=True)


def column_sum(a):
    return jnp.sum(a, axis=0, keepdims=True)


def own_forward_kernel(
    lo_ref, place_ref, start_row, queries, far, kv_own, top_row, total_row, acc_out,
    keys, values, values_t, scores,
):
    tile, tiles = scores.shape[1], scores.shape[0]
    core = place_ref[0]
    before = REACH * tiles // 2
    for j in range(tiles):
        span = core if j < tiles // 2 else 1 - core
        rows = pl.ds(j % (tiles // 2) * (tile // kv_own.shape[3]), tile // kv_own.shape[3])
        keys[j] = kv_own[span, rows, 0].reshape(keys.shape[1:])
        values_t[j] = kv_own[span, rows, 1].reshape(keys.shape[1:]).T
    for i in range(tiles):
        columns = pl.ds(i * tile, tile)
        query = query_tile(queries, far, 0, core, i, tile)
        start = start_row[:, columns]
        lo = jnp.maximum(lo_ref[i] - before, 0)

        def score_tile(j, causal):
            raw = masked_scores(keys[j], query, start, j + before, tile, causal)
            scores[j] = raw
            return column_max(raw)

        top = lax.fori_loop(
            lo, i, lambda j, m: jnp.maximum(m, score_tile(j, False)), score_tile(i, True)
        )

        def forward(j, carry):
            total, acc = carry
            prob = jnp.exp2(scores[j] - top)
            return total + column_sum(prob), acc + matmul(values_t[j], prob.astype(jnp.bfloat16))

        total, acc = lax.fori_loop(
            lo, i + 1, forward, (jnp.zeros_like(top), jnp.zeros(acc_out.shape[1:], jnp.float32))
        )
        top_row[:, columns] = top
        total_row[:, columns] = total
        acc_out[i] = acc


def earlier_kernel(
    lo_ref, place_ref, start_row, queries, out_grad, far, top_row, total_row, acc_in, kv_prev,
    attended_out, lse_row, delta_row, acc_out, p_near, p_next,
    keys_t, values_t, scores, key_acc, value_acc,
):
    tile, before = scores.shape[1], scores.shape[0]
    tiles = acc_in.shape[0]
    scale = queries.shape[2] ** -0.5
    core = place_ref[0]
    bf16, f32 = jnp.bfloat16, jnp.float32
    first = lo_ref[0]

    @pl.when(first < before)
    def _():
        key_acc[...] = jnp.zeros_like(key_acc)
        value_acc[...] = jnp.zeros_like(value_acc)

        def turn(j, carry):
            keys_t[j] = key_tile(kv_prev, j, 0, tile).T
            values_t[j] = key_tile(kv_prev, j, 1, tile).T
            return carry

        lax.fori_loop(first, before, turn, 0)

    for i in range(tiles):
        columns = pl.ds(i * tile, tile)
        query = query_tile(queries, far, 0, core, i, tile)
        grad = query_tile(out_grad, far, 1, core, i, tile)
        start = start_row[:, columns]
        lo = jnp.minimum(lo_ref[i], before)
        own_top = top_row[:, columns]

        def score_tile(j, top):
            raw = masked_scores(key_tile(kv_prev, j, 0, tile), query, start, j, tile, False)
            scores[j] = raw
            return jnp.maximum(top, column_max(raw))

        top = lax.fori_loop(lo, before, score_tile, own_top)
        shrink = jnp.exp2(own_top - top)

        def forward(j, carry):
            total, acc = carry
            prob = jnp.exp2(scores[j] - top)
            scores[j] = prob
            return total + column_sum(prob), acc + matmul(values_t[j], prob.astype(bf16))

        total, acc = lax.fori_loop(
            lo, before, forward, (total_row[:, columns] * shrink, acc_in[i] * shrink)
        )
        inv = 1.0 / total
        attended_t = (acc * inv).astype(bf16).astype(f32)
        delta = column_sum(grad.astype(f32).T * attended_t)
        half, part = divmod(i, tiles // 2)
        attended_out[half, pl.ds(part * tile, tile)] = attended_t.T.astype(bf16)
        lse_row[:, columns] = top + jnp.log2(total)
        delta_row[:, columns] = delta

        def backward(j, acc):
            prob = scores[j] * inv
            here = pl.ds(pl.multiple_of(j * tile, tile), tile)
            value_acc[here] += matmul(prob.astype(bf16), grad)
            dot_grad = matmul(key_tile(kv_prev, j, 1, tile), grad, NT)
            score_grad = (prob * (dot_grad - delta)).astype(bf16)
            key_acc[here] += matmul(score_grad, query)
            return acc + matmul(keys_t[j], score_grad)

        acc_out[i] = lax.fori_loop(lo, before, backward, jnp.zeros(acc_out.shape[1:], f32))

    shards, shard = kv_prev.shape[1], kv_prev.shape[3]

    @pl.when(first < before)
    def _():
        for slot, target in enumerate((p_next, p_near.at[0], p_near.at[1])):
            for row in range(shards):
                here = pl.ds((slot * shards + row) * shard, shard)
                target[row, 0] = (key_acc[here] * scale).astype(bf16)
                target[row, 1] = value_acc[here].astype(bf16)

    @pl.when(first >= before)
    def _():
        p_next[...] = jnp.zeros_like(p_next)
        p_near[...] = jnp.zeros_like(p_near)


def own_backward_kernel(
    lo_ref, place_ref, start_row, queries, out_grad, far, kv_own, attended, lse_row, delta_row,
    acc_in, out_own, out_far, p_own,
    keys, values, keys_t, key_acc, value_acc,
):
    tiles, tile = keys.shape[0], keys.shape[1]
    scale = queries.shape[2] ** -0.5
    core = place_ref[0]
    bf16, f32 = jnp.bfloat16, jnp.float32
    before = REACH * tiles // 2
    for j in range(tiles):
        span = core if j < tiles // 2 else 1 - core
        rows = pl.ds(j % (tiles // 2) * (tile // kv_own.shape[3]), tile // kv_own.shape[3])
        block = kv_own[span, rows, 0].reshape(keys.shape[1:])
        keys[j] = block
        keys_t[j] = block.T
        values[j] = kv_own[span, rows, 1].reshape(keys.shape[1:])
    key_acc[...] = jnp.zeros_like(key_acc)
    value_acc[...] = jnp.zeros_like(value_acc)
    for i in range(tiles):
        columns = pl.ds(i * tile, tile)
        query = query_tile(queries, far, 0, core, i, tile)
        grad = query_tile(out_grad, far, 1, core, i, tile)
        start = start_row[:, columns]
        lse, delta = lse_row[:, columns], delta_row[:, columns]

        def backward(j, acc, causal):
            raw = masked_scores(keys[j], query, start, j + before, tile, causal)
            prob = jnp.exp2(raw - lse)
            value_acc[j] += matmul(prob.astype(bf16), grad)
            score_grad = (prob * (matmul(values[j], grad, NT) - delta)).astype(bf16)
            key_acc[j] += matmul(score_grad, query)
            return acc + matmul(keys_t[j], score_grad)

        acc = backward(i, acc_in[i], True)
        acc = lax.fori_loop(
            jnp.maximum(lo_ref[i] - before, 0), i, lambda j, acc: backward(j, acc, False), acc
        )
        half, part = divmod(i, tiles // 2)
        rows = pl.ds(part * tile, tile)
        (out_own, out_far)[half][1, rows] = (acc.T * scale).astype(bf16)
    out_own[0] = attended[0]
    out_far[0] = attended[1]
    shards, shard = kv_own.shape[1], kv_own.shape[3]
    for span in range(2):
        for row in range(shards):
            j, part = divmod((span * shards + row) * shard, tile)
            here = pl.ds(part, shard)
            p_own[span, row, 0] = key_acc[j, here] * scale
            p_own[span, row, 1] = value_acc[j, here]


def vmem_kernel(kernel, name, outputs, scratch, tiles, tile, head_dim, matmuls):
    def call(*operands):
        rest = [pl.BlockSpec(memory_space=pltpu.VMEM)] * (len(operands) - 2)
        return pl.pallas_call(
            kernel,
            out_shape=outputs,
            in_specs=[pl.BlockSpec(memory_space=pltpu.SMEM)] * 2 + rest,
            out_specs=[pl.BlockSpec(memory_space=pltpu.VMEM)] * len(outputs),
            scratch_shapes=[pltpu.VMEM(shape, dtype) for shape, dtype in scratch],
            compiler_params=pltpu.CompilerParams(vmem_limit_bytes=24 * 1024 * 1024),
            cost_estimate=pl.CostEstimate(
                flops=2 * matmuls * tiles * tile * tile * head_dim,
                bytes_accessed=4 * 1024 * 1024,
                transcendentals=tiles * tile * tile,
            ),
            name=name,
        )(*operands)

    return call


def body(queries, key_states, value_states, out_grad, segments):
    ctx = lax.axis_size("pair") * 2
    core = lax.axis_index("core")
    position = lax.axis_index("pair") * 2 + core
    place = position % GROUP
    width = queries.shape[2]
    heads = lax.axis_size("head")
    shard = key_states.shape[2]
    head_dim = key_states.shape[3]
    bf16, f32 = jnp.bfloat16, jnp.float32

    swap, near, far_chip = swap_pairs(ctx), near_pairs(ctx), next_pairs(ctx)
    edge1 = within(ctx, [(2, 0), (GROUP - 3, GROUP - 1)])
    edge2 = within(ctx, [(1, 0), (GROUP - 2, GROUP - 1)])
    everywhere = CTX + ("head",)
    even = core == 0
    sends_lower = place >= GROUP - REACH
    head = lax.axis_index("head")
    bits = folds(heads)
    high = {bit: (head & bit) != 0 for bit in bits}
    edge = edge_pairs(ctx, heads)

    lower = jnp.stack([key_states[0, 0], value_states[0, 0]])
    upper = jnp.stack([key_states[0, 1], value_states[0, 1]])
    leaving = pick(sends_lower, upper, lower)
    half = by_bit(core, pick(even, upper, lower), lax.ppermute(pick(even, lower, upper), CTX, swap), 0)
    crossed = lax.ppermute(leaving, everywhere, edge)
    kv_all = jnp.concatenate([half, crossed[None]])[:, None]
    is_edge = lax.broadcasted_iota(jnp.int32, (3, 1, 1, 1, 1, 1), 0) == 2
    slot = lax.broadcasted_iota(jnp.int32, (1, 1, 2, 1, 1, 1), 2) == 1
    for bit in bits:
        other = lax.ppermute(kv_all, everywhere, head_pairs(ctx, heads, bit))
        stays = slot == (high[bit] ^ is_edge)
        kv_all = jnp.where(stays, kv_all[:, :, None], other[:, :, None])
        kv_all = kv_all.reshape((3, -1) + half.shape[1:])
    kv_own, kv_edge = kv_all[:2], kv_all[2]

    queries, out_grad = queries[0], out_grad[0]
    far = lax.ppermute(
        jnp.where(
            even,
            jnp.stack([queries[1], out_grad[1]]),
            jnp.stack([queries[0], out_grad[0]]),
        ),
        CTX,
        swap,
    )

    kv_next = lax.ppermute(jnp.where(even, kv_own[1], kv_own[0]), CTX, far_chip)
    kv_near = lax.ppermute(kv_own, CTX, near)
    kv_edge1 = lax.ppermute(kv_edge, CTX, edge1)
    kv_edge2 = lax.ppermute(kv_edge, CTX, edge2)

    first = jnp.where(even, position, 2 * ctx - 1 - position)
    window = (REACH + 2) * width
    padded = jnp.concatenate([jnp.full((REACH * width,), -1, jnp.int32), segments])
    seg_window = lax.dynamic_slice_in_dim(padded, first * width, window)
    start = jnp.sum(
        seg_window[:, None] < seg_window[None, REACH * width :], axis=0, dtype=jnp.int32
    )
    tile = max(min(256, width // 2), shard)
    tiles, earlier = 2 * width // tile, REACH * width // tile
    lo = start[::tile] // tile
    edge_next = jnp.where(even, place <= 2, place >= GROUP - 3)
    edge_near = jnp.where(even, place == 0, place == GROUP - 1)
    places = core[None].astype(jnp.int32)
    start = start[None, :]

    near_ordered = jnp.where(even, kv_near, kv_near[::-1])
    kv_prev = jnp.stack(
        [
            jnp.where(edge_next, kv_edge, kv_next),
            jnp.where(edge_near, kv_edge2, near_ordered[0]),
            jnp.where(edge_near, kv_edge1, near_ordered[1]),
        ]
    )

    row = jax.ShapeDtypeStruct((1, 2 * width), f32)
    turned = jax.ShapeDtypeStruct((tiles, head_dim, tile), f32)
    part = jax.ShapeDtypeStruct((2, width, head_dim), bf16)
    span_like = kv_next.shape
    natural = ((tiles, tile, head_dim), bf16)
    top, total, acc = vmem_kernel(
        own_forward_kernel, "own_forward", (row, row, turned),
        [natural, natural, ((tiles, head_dim, tile), bf16), ((tiles, tile, tile), f32)],
        6, tile, head_dim, 2,
    )(lo, places, start, queries, far, kv_own)
    attended, lse, delta, acc, p_near, p_next = vmem_kernel(
        earlier_kernel, "earlier",
        (
            part, row, row, turned,
            jax.ShapeDtypeStruct((2,) + span_like, bf16),
            jax.ShapeDtypeStruct(span_like, bf16),
        ),
        [
            ((earlier, head_dim, tile), bf16),
            ((earlier, head_dim, tile), bf16),
            ((earlier, tile, tile), f32),
            ((earlier * tile, head_dim), f32),
            ((earlier * tile, head_dim), f32),
        ],
        6, tile, head_dim, 6,
    )(lo, places, start, queries, out_grad, far, top, total, acc, kv_prev)

    r_edge1 = lax.ppermute(p_near[1], CTX, inverse(edge1)).astype(f32)
    r_edge2 = lax.ppermute(p_near[0], CTX, inverse(edge2)).astype(f32)
    r_next = lax.ppermute(p_next, CTX, inverse(far_chip)).astype(f32)
    r_near = lax.ppermute(p_near, CTX, inverse(near)).astype(f32)

    out_own, out_far, p_own = vmem_kernel(
        own_backward_kernel, "own_backward",
        (part, part, jax.ShapeDtypeStruct((2,) + span_like, f32)),
        [natural, natural, ((tiles, head_dim, tile), bf16)]
        + [((tiles, tile, head_dim), f32)] * 2,
        6, tile, head_dim, 5,
    )(lo, places, start, queries, out_grad, far, kv_own, attended, lse, delta, acc)

    edge_sum = jnp.where(edge_next, p_next.astype(f32), 0.0) + r_edge1 + r_edge2
    for bit in reversed(bits):
        halves = edge_sum.reshape((-1, 2) + half.shape[1:])
        away = pick(high[bit], halves[:, 0], halves[:, 1]).astype(bf16)
        other = lax.ppermute(away, everywhere, holder_pairs(ctx, heads, bit))
        edge_sum = pick(high[bit], halves[:, 1], halves[:, 0]) + other.astype(f32)
    returned = lax.ppermute(edge_sum[0].astype(bf16), everywhere, inverse(edge)).astype(f32)

    sums = p_own + r_near
    first_sum, second_sum = sums[0], sums[1] + r_next
    sums = jnp.stack([pick(even, second_sum, first_sum), pick(even, first_sum, second_sum)])
    for bit in reversed(bits):
        halves = sums.reshape((2, -1, 2) + half.shape[1:])
        away = pick(high[bit], halves[:, :, 1], halves[:, :, 0]).astype(bf16)
        other = lax.ppermute(away, everywhere, head_pairs(ctx, heads, bit))
        sums = pick(high[bit], halves[:, :, 0], halves[:, :, 1]) + other.astype(f32)
    stays = sums[:, 0]
    own_half = pick(even, stays[1], stays[0])
    far_half = lax.ppermute(
        pick(even, stays[0], stays[1]).astype(bf16), CTX, swap
    ).astype(f32)
    lower = pick(even, far_half, own_half) + jnp.where(sends_lower, returned, 0.0)
    upper = pick(even, own_half, far_half) + jnp.where(sends_lower, 0.0, returned)
    grads = jnp.stack([lower, upper]).astype(bf16)

    back = lax.ppermute(out_far, CTX, swap)
    results = []
    for k in range(2):
        results.append(
            jnp.where(
                even, jnp.stack([out_own[k], back[k]]), jnp.stack([back[k], out_own[k]])
            )[None]
        )
    return results[0], results[1], grads[:, 0][None], grads[:, 1][None]


def solution(mesh):
    ctx, heads = mesh.devices.shape
    mesh = Mesh(mesh.devices.reshape(ctx // 2, 2, heads), CTX + ("head",))
    by_head = P(CTX, None, None, "head")
    by_row = P(CTX, None, "head", None)
    return jax.shard_map(
        body,
        mesh=mesh,
        in_specs=(by_head, by_row, by_row, by_head, P()),
        out_specs=(by_head, by_head, by_row, by_row),
        check_vma=False,
    )
```

```python
import math

import jax
import jax.numpy as jnp
from jax import lax
from jax.experimental import pallas as pl
from jax.experimental.pallas import tpu as pltpu
from jax.sharding import Mesh
from jax.sharding import PartitionSpec as P

REACH = 3
GROUP = 8
NEG_FILL = -1e30
CTX = ("pair", "core")


def within(ctx, moves):
    return [(base + a, base + b) for base in range(0, ctx, GROUP) for a, b in moves]


def swap_pairs(ctx):
    return within(ctx, [(r, r ^ 1) for r in range(GROUP)])


def near_pairs(ctx):
    forth = [(r, r + 2) for r in range(0, GROUP - 2, 2)]
    return within(ctx, forth + [(r, r - 2) for r in range(3, GROUP, 2)])


def next_pairs(ctx):
    forth = [(r, r + 4) for r in range(0, GROUP - 4, 2)]
    return within(ctx, forth + [(r, r - 4) for r in range(5, GROUP, 2)])


def head_pairs(ctx, heads, bit):
    return [(d, d ^ bit) for d in range(ctx * heads)]


def holder_pairs(ctx, heads, bit):
    holders = [r for r in range(GROUP) if r < REACH or r >= GROUP - REACH]
    return [
        ((base + r) * heads + h, (base + r) * heads + (h ^ bit))
        for base in range(0, ctx, GROUP)
        for r in holders
        for h in range(heads)
    ]


def edge_pairs(ctx, heads):
    moves = []
    for base in range(0, ctx, GROUP):
        for k in range(REACH):
            top = base + GROUP - 1 - k
            if base + GROUP < ctx:
                moves.append((top, base + GROUP + REACH - 1 - k))
            else:
                moves.append((top, base + GROUP - REACH + k))
            if base > 0:
                moves.append((base + k, base - REACH + k))
    return [
        (a * heads + h, b * heads + heads - 1 - h) for a, b in moves for h in range(heads)
    ]


def folds(heads):
    return [1 << k for k in reversed(range(heads.bit_length() - 1))]


def pick(bit, low, high):
    return jnp.where(bit, high, low)


def by_bit(bit, mine, other, axis):
    mine, other = jnp.expand_dims(mine, axis), jnp.expand_dims(other, axis)
    place = lax.broadcasted_iota(jnp.int32, (2,) + (1,) * (mine.ndim - axis - 1), 0)
    return jnp.where(place == bit.astype(jnp.int32), mine, other)


def inverse(pairs):
    return [(b, a) for a, b in pairs]


NT = (((1,), (1,)), ((), ()))
NN = (((1,), (0,)), ((), ()))


def matmul(a, b, dims=NN):
    return lax.dot_general(a, b, dims, preferred_element_type=jnp.float32)


def key_tile(ref, j, which, tile):
    _, shards, _, shard, head_dim = ref.shape
    per_span = shards * shard // tile
    rows = pl.ds((j % per_span) * (tile // shard), tile // shard)
    return ref[j // per_span, rows, which].reshape(tile, head_dim)


def query_tile(own_ref, far_ref, far_index, core, i, tile):
    width = far_ref.shape[1]
    span, part = divmod(i, width // tile)
    rows = pl.ds(part * tile, tile)
    return own_ref[core, rows] if span == 0 else far_ref[far_index, rows]


def masked_scores(keys, query, start, j, tile, causal):
    raw = matmul(keys, query, NT) * (query.shape[1] ** -0.5 * math.log2(math.e))
    at_key = lax.broadcasted_iota(jnp.int32, raw.shape, 0)
    allowed = at_key >= start - j * tile
    if causal:
        allowed = allowed & (at_key <= lax.broadcasted_iota(jnp.int32, raw.shape, 1))
    return jnp.where(allowed, raw, NEG_FILL)


def column_max(a):
    return jnp.max(a, axis=0, keepdims=True)


def column_sum(a):
    return jnp.sum(a, axis=0, keepdims=True)


def own_forward_kernel(
    lo_ref, place_ref, start_row, queries, far, kv_own, top_row, total_row, acc_out,
    keys, values, values_t, scores,
):
    tile, tiles = scores.shape[1], scores.shape[0]
    core = place_ref[0]
    before = REACH * tiles // 2
    for j in range(tiles):
        span = core if j < tiles // 2 else 1 - core
        rows = pl.ds(j % (tiles // 2) * (tile // kv_own.shape[3]), tile // kv_own.shape[3])
        keys[j] = kv_own[span, rows, 0].reshape(keys.shape[1:])
        values_t[j] = kv_own[span, rows, 1].reshape(keys.shape[1:]).T
    for i in range(tiles):
        columns = pl.ds(i * tile, tile)
        query = query_tile(queries, far, 0, core, i, tile)
        start = start_row[:, columns]
        lo = jnp.maximum(lo_ref[i] - before, 0)

        def score_tile(j, causal):
            raw = masked_scores(keys[j], query, start, j + before, tile, causal)
            scores[j] = raw
            return column_max(raw)

        top = lax.fori_loop(
            lo, i, lambda j, m: jnp.maximum(m, score_tile(j, False)), score_tile(i, True)
        )

        def forward(j, carry):
            total, acc = carry
            prob = jnp.exp2(scores[j] - top)
            return total + column_sum(prob), acc + matmul(values_t[j], prob.astype(jnp.bfloat16))

        total, acc = lax.fori_loop(
            lo, i + 1, forward, (jnp.zeros_like(top), jnp.zeros(acc_out.shape[1:], jnp.float32))
        )
        top_row[:, columns] = top
        total_row[:, columns] = total
        acc_out[i] = acc


def earlier_kernel(
    lo_ref, place_ref, start_row, queries, out_grad, far, top_row, total_row, acc_in, kv_prev,
    attended_out, lse_row, delta_row, acc_out, p_near, p_next,
    keys_t, values_t, scores, key_acc, value_acc,
):
    tile, before = scores.shape[1], scores.shape[0]
    tiles = acc_in.shape[0]
    scale = queries.shape[2] ** -0.5
    core = place_ref[0]
    bf16, f32 = jnp.bfloat16, jnp.float32
    first = lo_ref[0]

    @pl.when(first < before)
    def _():
        key_acc[...] = jnp.zeros_like(key_acc)
        value_acc[...] = jnp.zeros_like(value_acc)

        def turn(j, carry):
            keys_t[j] = key_tile(kv_prev, j, 0, tile).T
            values_t[j] = key_tile(kv_prev, j, 1, tile).T
            return carry

        lax.fori_loop(first, before, turn, 0)

    for i in range(tiles):
        columns = pl.ds(i * tile, tile)
        query = query_tile(queries, far, 0, core, i, tile)
        grad = query_tile(out_grad, far, 1, core, i, tile)
        start = start_row[:, columns]
        lo = jnp.minimum(lo_ref[i], before)
        own_top = top_row[:, columns]

        def score_tile(j, top):
            raw = masked_scores(key_tile(kv_prev, j, 0, tile), query, start, j, tile, False)
            scores[j] = raw
            return jnp.maximum(top, column_max(raw))

        top = lax.fori_loop(lo, before, score_tile, own_top)
        shrink = jnp.exp2(own_top - top)

        def forward(j, carry):
            total, acc = carry
            prob = jnp.exp2(scores[j] - top)
            scores[j] = prob
            return total + column_sum(prob), acc + matmul(values_t[j], prob.astype(bf16))

        total, acc = lax.fori_loop(
            lo, before, forward, (total_row[:, columns] * shrink, acc_in[i] * shrink)
        )
        inv = 1.0 / total
        attended_t = (acc * inv).astype(bf16).astype(f32)
        delta = column_sum(grad.astype(f32).T * attended_t)
        half, part = divmod(i, tiles // 2)
        attended_out[half, pl.ds(part * tile, tile)] = attended_t.T.astype(bf16)
        lse_row[:, columns] = top + jnp.log2(total)
        delta_row[:, columns] = delta

        def backward(j, acc):
            prob = scores[j] * inv
            here = pl.ds(pl.multiple_of(j * tile, tile), tile)
            value_acc[here] += matmul(prob.astype(bf16), grad)
            dot_grad = matmul(key_tile(kv_prev, j, 1, tile), grad, NT)
            score_grad = (prob * (dot_grad - delta)).astype(bf16)
            key_acc[here] += matmul(score_grad, query)
            return acc + matmul(keys_t[j], score_grad)

        acc_out[i] = lax.fori_loop(lo, before, backward, jnp.zeros(acc_out.shape[1:], f32))

    shards, shard = kv_prev.shape[1], kv_prev.shape[3]

    @pl.when(first < before)
    def _():
        for slot, target in enumerate((p_next, p_near.at[0], p_near.at[1])):
            for row in range(shards):
                here = pl.ds((slot * shards + row) * shard, shard)
                target[row, 0] = (key_acc[here] * scale).astype(bf16)
                target[row, 1] = value_acc[here].astype(bf16)

    @pl.when(first >= before)
    def _():
        p_next[...] = jnp.zeros_like(p_next)
        p_near[...] = jnp.zeros_like(p_near)


def own_backward_kernel(
    lo_ref, place_ref, start_row, queries, out_grad, far, kv_own, attended, lse_row, delta_row,
    acc_in, out_own, out_far, p_own,
    keys, values, keys_t, key_acc, value_acc,
):
    tiles, tile = keys.shape[0], keys.shape[1]
    scale = queries.shape[2] ** -0.5
    core = place_ref[0]
    bf16, f32 = jnp.bfloat16, jnp.float32
    before = REACH * tiles // 2
    for j in range(tiles):
        span = core if j < tiles // 2 else 1 - core
        rows = pl.ds(j % (tiles // 2) * (tile // kv_own.shape[3]), tile // kv_own.shape[3])
        block = kv_own[span, rows, 0].reshape(keys.shape[1:])
        keys[j] = block
        keys_t[j] = block.T
        values[j] = kv_own[span, rows, 1].reshape(keys.shape[1:])
    key_acc[...] = jnp.zeros_like(key_acc)
    value_acc[...] = jnp.zeros_like(value_acc)
    for i in range(tiles):
        columns = pl.ds(i * tile, tile)
        query = query_tile(queries, far, 0, core, i, tile)
        grad = query_tile(out_grad, far, 1, core, i, tile)
        start = start_row[:, columns]
        lse, delta = lse_row[:, columns], delta_row[:, columns]

        def backward(j, acc, causal):
            raw = masked_scores(keys[j], query, start, j + before, tile, causal)
            prob = jnp.exp2(raw - lse)
            value_acc[j] += matmul(prob.astype(bf16), grad)
            score_grad = (prob * (matmul(values[j], grad, NT) - delta)).astype(bf16)
            key_acc[j] += matmul(score_grad, query)
            return acc + matmul(keys_t[j], score_grad)

        acc = backward(i, acc_in[i], True)
        acc = lax.fori_loop(
            jnp.maximum(lo_ref[i] - before, 0), i, lambda j, acc: backward(j, acc, False), acc
        )
        half, part = divmod(i, tiles // 2)
        rows = pl.ds(part * tile, tile)
        (out_own, out_far)[half][1, rows] = (acc.T * scale).astype(bf16)
    out_own[0] = attended[0]
    out_far[0] = attended[1]
    shards, shard = kv_own.shape[1], kv_own.shape[3]
    for span in range(2):
        for row in range(shards):
            j, part = divmod((span * shards + row) * shard, tile)
            here = pl.ds(part, shard)
            p_own[span, row, 0] = key_acc[j, here] * scale
            p_own[span, row, 1] = value_acc[j, here]


def vmem_kernel(kernel, name, outputs, scratch, tiles, tile, head_dim, matmuls):
    def call(*operands):
        rest = [pl.BlockSpec(memory_space=pltpu.VMEM)] * (len(operands) - 2)
        return pl.pallas_call(
            kernel,
            out_shape=outputs,
            in_specs=[pl.BlockSpec(memory_space=pltpu.SMEM)] * 2 + rest,
            out_specs=[pl.BlockSpec(memory_space=pltpu.VMEM)] * len(outputs),
            scratch_shapes=[pltpu.VMEM(shape, dtype) for shape, dtype in scratch],
            compiler_params=pltpu.CompilerParams(vmem_limit_bytes=24 * 1024 * 1024),
            cost_estimate=pl.CostEstimate(
                flops=2 * matmuls * tiles * tile * tile * head_dim,
                bytes_accessed=4 * 1024 * 1024,
                transcendentals=tiles * tile * tile,
            ),
            name=name,
        )(*operands)

    return call


def body(queries, key_states, value_states, out_grad, segments):
    ctx = lax.axis_size("pair") * 2
    core = lax.axis_index("core")
    position = lax.axis_index("pair") * 2 + core
    place = position % GROUP
    width = queries.shape[2]
    heads = lax.axis_size("head")
    shard = key_states.shape[2]
    head_dim = key_states.shape[3]
    bf16, f32 = jnp.bfloat16, jnp.float32

    swap, near, far_chip = swap_pairs(ctx), near_pairs(ctx), next_pairs(ctx)
    edge1 = within(ctx, [(2, 0), (GROUP - 3, GROUP - 1)])
    edge2 = within(ctx, [(1, 0), (GROUP - 2, GROUP - 1)])
    everywhere = CTX + ("head",)
    even = core == 0
    sends_lower = place >= GROUP - REACH
    head = lax.axis_index("head")
    bits = folds(heads)
    high = {bit: (head & bit) != 0 for bit in bits}
    edge = edge_pairs(ctx, heads)

    lower = jnp.stack([key_states[0, 0], value_states[0, 0]])
    upper = jnp.stack([key_states[0, 1], value_states[0, 1]])
    leaving = pick(sends_lower, upper, lower)
    half = by_bit(core, pick(even, upper, lower), lax.ppermute(pick(even, lower, upper), CTX, swap), 0)
    crossed = lax.ppermute(leaving, everywhere, edge)
    kv_all = jnp.concatenate([half, crossed[None]])[:, None]
    is_edge = lax.broadcasted_iota(jnp.int32, (3, 1, 1, 1, 1, 1), 0) == 2
    slot = lax.broadcasted_iota(jnp.int32, (1, 1, 2, 1, 1, 1), 2) == 1
    for bit in bits:
        other = lax.ppermute(kv_all, everywhere, head_pairs(ctx, heads, bit))
        stays = slot == (high[bit] ^ is_edge)
        kv_all = jnp.where(stays, kv_all[:, :, None], other[:, :, None])
        kv_all = kv_all.reshape((3, -1) + half.shape[1:])
    kv_own, kv_edge = kv_all[:2], kv_all[2]

    queries, out_grad = queries[0], out_grad[0]
    far = lax.ppermute(
        jnp.where(
            even,
            jnp.stack([queries[1], out_grad[1]]),
            jnp.stack([queries[0], out_grad[0]]),
        ),
        CTX,
        swap,
    )

    kv_next = lax.ppermute(jnp.where(even, kv_own[1], kv_own[0]), CTX, far_chip)
    kv_near = lax.ppermute(kv_own, CTX, near)
    kv_edge1 = lax.ppermute(kv_edge, CTX, edge1)
    kv_edge2 = lax.ppermute(kv_edge, CTX, edge2)

    first = jnp.where(even, position, 2 * ctx - 1 - position)
    window = (REACH + 2) * width
    padded = jnp.concatenate([jnp.full((REACH * width,), -1, jnp.int32), segments])
    seg_window = lax.dynamic_slice_in_dim(padded, first * width, window)
    start = jnp.sum(
        seg_window[:, None] < seg_window[None, REACH * width :], axis=0, dtype=jnp.int32
    )
    tile = max(min(256, width // 2), shard)
    tiles, earlier = 2 * width // tile, REACH * width // tile
    lo = start[::tile] // tile
    edge_next = jnp.where(even, place <= 2, place >= GROUP - 3)
    edge_near = jnp.where(even, place == 0, place == GROUP - 1)
    places = core[None].astype(jnp.int32)
    start = start[None, :]

    near_ordered = jnp.where(even, kv_near, kv_near[::-1])
    kv_prev = jnp.stack(
        [
            jnp.where(edge_next, kv_edge, kv_next),
            jnp.where(edge_near, kv_edge2, near_ordered[0]),
            jnp.where(edge_near, kv_edge1, near_ordered[1]),
        ]
    )

    row = jax.ShapeDtypeStruct((1, 2 * width), f32)
    turned = jax.ShapeDtypeStruct((tiles, head_dim, tile), f32)
    part = jax.ShapeDtypeStruct((2, width, head_dim), bf16)
    span_like = kv_next.shape
    natural = ((tiles, tile, head_dim), bf16)
    top, total, acc = vmem_kernel(
        own_forward_kernel, "own_forward", (row, row, turned),
        [natural, natural, ((tiles, head_dim, tile), bf16), ((tiles, tile, tile), f32)],
        6, tile, head_dim, 2,
    )(lo, places, start, queries, far, kv_own)
    attended, lse, delta, acc, p_near, p_next = vmem_kernel(
        earlier_kernel, "earlier",
        (
            part, row, row, turned,
            jax.ShapeDtypeStruct((2,) + span_like, bf16),
            jax.ShapeDtypeStruct(span_like, bf16),
        ),
        [
            ((earlier, head_dim, tile), bf16),
            ((earlier, head_dim, tile), bf16),
            ((earlier, tile, tile), f32),
            ((earlier * tile, head_dim), f32),
            ((earlier * tile, head_dim), f32),
        ],
        6, tile, head_dim, 6,
    )(lo, places, start, queries, out_grad, far, top, total, acc, kv_prev)

    r_edge1 = lax.ppermute(p_near[1], CTX, inverse(edge1)).astype(f32)
    r_edge2 = lax.ppermute(p_near[0], CTX, inverse(edge2)).astype(f32)
    r_next = lax.ppermute(p_next, CTX, inverse(far_chip)).astype(f32)
    r_near = lax.ppermute(p_near, CTX, inverse(near)).astype(f32)

    out_own, out_far, p_own = vmem_kernel(
        own_backward_kernel, "own_backward",
        (part, part, jax.ShapeDtypeStruct((2,) + span_like, f32)),
        [natural, natural, ((tiles, head_dim, tile), bf16)]
        + [((tiles, tile, head_dim), f32)] * 2,
        6, tile, head_dim, 5,
    )(lo, places, start, queries, out_grad, far, kv_own, attended, lse, delta, acc)

    edge_sum = jnp.where(edge_next, p_next.astype(f32), 0.0) + r_edge1 + r_edge2
    sums = p_own + r_near
    first_sum, second_sum = sums[0], sums[1] + r_next
    sums = jnp.stack([pick(even, second_sum, first_sum), pick(even, first_sum, second_sum)])
    for bit in reversed(bits):
        halves = sums.reshape((2, -1, 2) + half.shape[1:])
        edge_halves = edge_sum.reshape((-1, 2) + half.shape[1:])
        away = pick(high[bit], halves[:, :, 1], halves[:, :, 0]).astype(bf16)
        edge_away = pick(high[bit], edge_halves[:, 0], edge_halves[:, 1]).astype(bf16)
        other = lax.ppermute(away, everywhere, head_pairs(ctx, heads, bit))
        edge_other = lax.ppermute(edge_away, everywhere, holder_pairs(ctx, heads, bit))
        other, edge_other = lax.optimization_barrier((other, edge_other))
        sums = pick(high[bit], halves[:, :, 0], halves[:, :, 1]) + other.astype(f32)
        edge_sum = pick(high[bit], edge_halves[:, 1], edge_halves[:, 0]) + edge_other.astype(f32)
    returned = lax.ppermute(edge_sum[0].astype(bf16), everywhere, inverse(edge)).astype(f32)
    stays = sums[:, 0]
    own_half = pick(even, stays[1], stays[0])
    far_half = lax.ppermute(
        pick(even, stays[0], stays[1]).astype(bf16), CTX, swap
    ).astype(f32)
    lower = pick(even, far_half, own_half) + jnp.where(sends_lower, returned, 0.0)
    upper = pick(even, own_half, far_half) + jnp.where(sends_lower, 0.0, returned)
    grads = jnp.stack([lower, upper]).astype(bf16)

    back = lax.ppermute(out_far, CTX, swap)
    results = []
    for k in range(2):
        results.append(
            jnp.where(
                even, jnp.stack([out_own[k], back[k]]), jnp.stack([back[k], out_own[k]])
            )[None]
        )
    return results[0], results[1], grads[:, 0][None], grads[:, 1][None]


def solution(mesh):
    ctx, heads = mesh.devices.shape
    mesh = Mesh(mesh.devices.reshape(ctx // 2, 2, heads), CTX + ("head",))
    by_head = P(CTX, None, None, "head")
    by_row = P(CTX, None, "head", None)
    return jax.shard_map(
        body,
        mesh=mesh,
        in_specs=(by_head, by_row, by_row, by_head, P()),
        out_specs=(by_head, by_head, by_row, by_row),
        check_vma=False,
    )
```

```python
import math

import jax
import jax.numpy as jnp
from jax import lax
from jax.experimental import pallas as pl
from jax.experimental.pallas import tpu as pltpu
from jax.sharding import Mesh
from jax.sharding import PartitionSpec as P

REACH = 3
GROUP = 8
NEG_FILL = -1e30
CTX = ("pair", "core")


def within(ctx, moves):
    return [(base + a, base + b) for base in range(0, ctx, GROUP) for a, b in moves]


def swap_pairs(ctx):
    return within(ctx, [(r, r ^ 1) for r in range(GROUP)])


def near_pairs(ctx):
    forth = [(r, r + 2) for r in range(0, GROUP - 2, 2)]
    return within(ctx, forth + [(r, r - 2) for r in range(3, GROUP, 2)])


def next_pairs(ctx):
    forth = [(r, r + 4) for r in range(0, GROUP - 4, 2)]
    return within(ctx, forth + [(r, r - 4) for r in range(5, GROUP, 2)])


def head_pairs(ctx, heads, bit):
    return [(d, d ^ bit) for d in range(ctx * heads)]


def holder_pairs(ctx, heads, bit):
    holders = [r for r in range(GROUP) if r < REACH or r >= GROUP - REACH]
    return [
        ((base + r) * heads + h, (base + r) * heads + (h ^ bit))
        for base in range(0, ctx, GROUP)
        for r in holders
        for h in range(heads)
    ]


def edge_pairs(ctx, heads):
    moves = []
    for base in range(0, ctx, GROUP):
        for k in range(REACH):
            top = base + GROUP - 1 - k
            if base + GROUP < ctx:
                moves.append((top, base + GROUP + REACH - 1 - k))
            else:
                moves.append((top, base + GROUP - REACH + k))
            if base > 0:
                moves.append((base + k, base - REACH + k))
    return [
        (a * heads + h, b * heads + heads - 1 - h) for a, b in moves for h in range(heads)
    ]


def folds(heads):
    return [1 << k for k in reversed(range(heads.bit_length() - 1))]


def pick(bit, low, high):
    return jnp.where(bit, high, low)


def by_bit(bit, mine, other, axis):
    mine, other = jnp.expand_dims(mine, axis), jnp.expand_dims(other, axis)
    place = lax.broadcasted_iota(jnp.int32, (2,) + (1,) * (mine.ndim - axis - 1), 0)
    return jnp.where(place == bit.astype(jnp.int32), mine, other)


def inverse(pairs):
    return [(b, a) for a, b in pairs]


NT = (((1,), (1,)), ((), ()))
NN = (((1,), (0,)), ((), ()))


def matmul(a, b, dims=NN):
    return lax.dot_general(a, b, dims, preferred_element_type=jnp.float32)


def key_tile(ref, j, which, tile):
    _, shards, _, shard, head_dim = ref.shape
    per_span = shards * shard // tile
    rows = pl.ds((j % per_span) * (tile // shard), tile // shard)
    return ref[j // per_span, rows, which].reshape(tile, head_dim)


def query_tile(own_ref, far_ref, far_index, core, i, tile):
    width = far_ref.shape[1]
    span, part = divmod(i, width // tile)
    rows = pl.ds(part * tile, tile)
    return own_ref[core, rows] if span == 0 else far_ref[far_index, rows]


def masked_scores(keys, query, start, j, tile, causal):
    raw = matmul(keys, query, NT) * (query.shape[1] ** -0.5 * math.log2(math.e))
    at_key = lax.broadcasted_iota(jnp.int32, raw.shape, 0)
    allowed = at_key >= start - j * tile
    if causal:
        allowed = allowed & (at_key <= lax.broadcasted_iota(jnp.int32, raw.shape, 1))
    return jnp.where(allowed, raw, NEG_FILL)


def column_max(a):
    return jnp.max(a, axis=0, keepdims=True)


def column_sum(a):
    return jnp.sum(a, axis=0, keepdims=True)


def own_forward_kernel(
    lo_ref, place_ref, start_row, queries, far, kv_own, top_row, total_row, acc_out,
    keys, values, values_t, scores,
):
    tile, tiles = scores.shape[1], scores.shape[0]
    core = place_ref[0]
    before = REACH * tiles // 2
    for j in range(tiles):
        span = core if j < tiles // 2 else 1 - core
        rows = pl.ds(j % (tiles // 2) * (tile // kv_own.shape[3]), tile // kv_own.shape[3])
        keys[j] = kv_own[span, rows, 0].reshape(keys.shape[1:])
        values_t[j] = kv_own[span, rows, 1].reshape(keys.shape[1:]).T
    for i in range(tiles):
        columns = pl.ds(i * tile, tile)
        query = query_tile(queries, far, 0, core, i, tile)
        start = start_row[:, columns]
        lo = jnp.maximum(lo_ref[i] - before, 0)

        def score_tile(j, causal):
            raw = masked_scores(keys[j], query, start, j + before, tile, causal)
            scores[j] = raw
            return column_max(raw)

        top = lax.fori_loop(
            lo, i, lambda j, m: jnp.maximum(m, score_tile(j, False)), score_tile(i, True)
        )

        def forward(j, carry):
            total, acc = carry
            prob = jnp.exp2(scores[j] - top)
            return total + column_sum(prob), acc + matmul(values_t[j], prob.astype(jnp.bfloat16))

        total, acc = lax.fori_loop(
            lo, i + 1, forward, (jnp.zeros_like(top), jnp.zeros(acc_out.shape[1:], jnp.float32))
        )
        top_row[:, columns] = top
        total_row[:, columns] = total
        acc_out[i] = acc


def earlier_kernel(
    lo_ref, place_ref, start_row, queries, out_grad, far, top_row, total_row, acc_in, kv_prev,
    attended_out, lse_row, delta_row, acc_out, p_near, p_next,
    keys_t, values_t, scores, key_acc, value_acc,
):
    tile, before = scores.shape[1], scores.shape[0]
    tiles = acc_in.shape[0]
    scale = queries.shape[2] ** -0.5
    core = place_ref[0]
    bf16, f32 = jnp.bfloat16, jnp.float32
    first = lo_ref[0]

    @pl.when(first < before)
    def _():
        key_acc[...] = jnp.zeros_like(key_acc)
        value_acc[...] = jnp.zeros_like(value_acc)

        def turn(j, carry):
            keys_t[j] = key_tile(kv_prev, j, 0, tile).T
            values_t[j] = key_tile(kv_prev, j, 1, tile).T
            return carry

        lax.fori_loop(first, before, turn, 0)

    for i in range(tiles):
        columns = pl.ds(i * tile, tile)
        query = query_tile(queries, far, 0, core, i, tile)
        grad = query_tile(out_grad, far, 1, core, i, tile)
        start = start_row[:, columns]
        lo = jnp.minimum(lo_ref[i], before)
        own_top = top_row[:, columns]

        def score_tile(j, top):
            raw = masked_scores(key_tile(kv_prev, j, 0, tile), query, start, j, tile, False)
            scores[j] = raw
            return jnp.maximum(top, column_max(raw))

        top = lax.fori_loop(lo, before, score_tile, own_top)
        shrink = jnp.exp2(own_top - top)

        def forward(j, carry):
            total, acc = carry
            prob = jnp.exp2(scores[j] - top)
            scores[j] = prob
            return total + column_sum(prob), acc + matmul(values_t[j], prob.astype(bf16))

        total, acc = lax.fori_loop(
            lo, before, forward, (total_row[:, columns] * shrink, acc_in[i] * shrink)
        )
        inv = 1.0 / total
        attended_t = (acc * inv).astype(bf16).astype(f32)
        delta = column_sum(grad.astype(f32).T * attended_t)
        half, part = divmod(i, tiles // 2)
        attended_out[half, pl.ds(part * tile, tile)] = attended_t.T.astype(bf16)
        lse_row[:, columns] = top + jnp.log2(total)
        delta_row[:, columns] = delta

        def backward(j, acc):
            prob = scores[j] * inv
            here = pl.ds(pl.multiple_of(j * tile, tile), tile)
            value_acc[here] += matmul(prob.astype(bf16), grad)
            dot_grad = matmul(key_tile(kv_prev, j, 1, tile), grad, NT)
            score_grad = (prob * (dot_grad - delta)).astype(bf16)
            key_acc[here] += matmul(score_grad, query)
            return acc + matmul(keys_t[j], score_grad)

        acc_out[i] = lax.fori_loop(lo, before, backward, jnp.zeros(acc_out.shape[1:], f32))

    shards, shard = kv_prev.shape[1], kv_prev.shape[3]

    @pl.when(first < before)
    def _():
        for slot, target in enumerate((p_next, p_near.at[0], p_near.at[1])):
            for row in range(shards):
                here = pl.ds((slot * shards + row) * shard, shard)
                target[row, 0] = (key_acc[here] * scale).astype(bf16)
                target[row, 1] = value_acc[here].astype(bf16)

    @pl.when(first >= before)
    def _():
        p_next[...] = jnp.zeros_like(p_next)
        p_near[...] = jnp.zeros_like(p_near)


def own_backward_kernel(
    lo_ref, place_ref, start_row, queries, out_grad, far, kv_own, attended, lse_row, delta_row,
    acc_in, out_own, out_far, p_own,
    keys, values, keys_t, key_acc, value_acc,
):
    tiles, tile = keys.shape[0], keys.shape[1]
    scale = queries.shape[2] ** -0.5
    core = place_ref[0]
    bf16, f32 = jnp.bfloat16, jnp.float32
    before = REACH * tiles // 2
    for j in range(tiles):
        span = core if j < tiles // 2 else 1 - core
        rows = pl.ds(j % (tiles // 2) * (tile // kv_own.shape[3]), tile // kv_own.shape[3])
        block = kv_own[span, rows, 0].reshape(keys.shape[1:])
        keys[j] = block
        keys_t[j] = block.T
        values[j] = kv_own[span, rows, 1].reshape(keys.shape[1:])
    key_acc[...] = jnp.zeros_like(key_acc)
    value_acc[...] = jnp.zeros_like(value_acc)
    for i in range(tiles):
        columns = pl.ds(i * tile, tile)
        query = query_tile(queries, far, 0, core, i, tile)
        grad = query_tile(out_grad, far, 1, core, i, tile)
        start = start_row[:, columns]
        lse, delta = lse_row[:, columns], delta_row[:, columns]

        def backward(j, acc, causal):
            raw = masked_scores(keys[j], query, start, j + before, tile, causal)
            prob = jnp.exp2(raw - lse)
            value_acc[j] += matmul(prob.astype(bf16), grad)
            score_grad = (prob * (matmul(values[j], grad, NT) - delta)).astype(bf16)
            key_acc[j] += matmul(score_grad, query)
            return acc + matmul(keys_t[j], score_grad)

        acc = backward(i, acc_in[i], True)
        acc = lax.fori_loop(
            jnp.maximum(lo_ref[i] - before, 0), i, lambda j, acc: backward(j, acc, False), acc
        )
        half, part = divmod(i, tiles // 2)
        rows = pl.ds(part * tile, tile)
        (out_own, out_far)[half][1, rows] = (acc.T * scale).astype(bf16)
    out_own[0] = attended[0]
    out_far[0] = attended[1]
    shards, shard = kv_own.shape[1], kv_own.shape[3]
    for span in range(2):
        for row in range(shards):
            j, part = divmod((span * shards + row) * shard, tile)
            here = pl.ds(part, shard)
            p_own[span, row, 0] = key_acc[j, here] * scale
            p_own[span, row, 1] = value_acc[j, here]


def vmem_kernel(kernel, name, outputs, scratch, tiles, tile, head_dim, matmuls):
    def call(*operands):
        rest = [pl.BlockSpec(memory_space=pltpu.VMEM)] * (len(operands) - 2)
        return pl.pallas_call(
            kernel,
            out_shape=outputs,
            in_specs=[pl.BlockSpec(memory_space=pltpu.SMEM)] * 2 + rest,
            out_specs=[pl.BlockSpec(memory_space=pltpu.VMEM)] * len(outputs),
            scratch_shapes=[pltpu.VMEM(shape, dtype) for shape, dtype in scratch],
            compiler_params=pltpu.CompilerParams(vmem_limit_bytes=24 * 1024 * 1024),
            cost_estimate=pl.CostEstimate(
                flops=2 * matmuls * tiles * tile * tile * head_dim,
                bytes_accessed=4 * 1024 * 1024,
                transcendentals=tiles * tile * tile,
            ),
            name=name,
        )(*operands)

    return call


def body(queries, key_states, value_states, out_grad, segments):
    ctx = lax.axis_size("pair") * 2
    core = lax.axis_index("core")
    position = lax.axis_index("pair") * 2 + core
    place = position % GROUP
    width = queries.shape[2]
    heads = lax.axis_size("head")
    shard = key_states.shape[2]
    head_dim = key_states.shape[3]
    bf16, f32 = jnp.bfloat16, jnp.float32

    swap, near, far_chip = swap_pairs(ctx), near_pairs(ctx), next_pairs(ctx)
    edge1 = within(ctx, [(2, 0), (GROUP - 3, GROUP - 1)])
    edge2 = within(ctx, [(1, 0), (GROUP - 2, GROUP - 1)])
    everywhere = CTX + ("head",)
    even = core == 0
    sends_lower = place >= GROUP - REACH
    head = lax.axis_index("head")
    bits = folds(heads)
    high = {bit: (head & bit) != 0 for bit in bits}
    edge = edge_pairs(ctx, heads)

    lower = jnp.stack([key_states[0, 0], value_states[0, 0]])
    upper = jnp.stack([key_states[0, 1], value_states[0, 1]])
    leaving = pick(sends_lower, upper, lower)
    half = by_bit(core, pick(even, upper, lower), lax.ppermute(pick(even, lower, upper), CTX, swap), 0)
    crossed = lax.ppermute(leaving, everywhere, edge)
    kv_all = jnp.concatenate([half, crossed[None]])[:, None]
    is_edge = lax.broadcasted_iota(jnp.int32, (3, 1, 1, 1, 1, 1), 0) == 2
    slot = lax.broadcasted_iota(jnp.int32, (1, 1, 2, 1, 1, 1), 2) == 1
    for bit in bits:
        other = lax.ppermute(kv_all, everywhere, head_pairs(ctx, heads, bit))
        stays = slot == (high[bit] ^ is_edge)
        kv_all = jnp.where(stays, kv_all[:, :, None], other[:, :, None])
        kv_all = kv_all.reshape((3, -1) + half.shape[1:])
    kv_own, kv_edge = kv_all[:2], kv_all[2]

    queries, out_grad = queries[0], out_grad[0]
    far = lax.ppermute(
        jnp.where(
            even,
            jnp.stack([queries[1], out_grad[1]]),
            jnp.stack([queries[0], out_grad[0]]),
        ),
        CTX,
        swap,
    )

    hands_edge = (place == 1) | (place == GROUP - 2)
    kv_next = jnp.where(hands_edge, kv_edge, jnp.where(even, kv_own[1], kv_own[0]))
    kv_next = lax.ppermute(kv_next, CTX, far_chip + edge2)
    kv_near = lax.ppermute(kv_own, CTX, near)
    kv_edge1 = lax.ppermute(kv_edge, CTX, edge1)

    first = jnp.where(even, position, 2 * ctx - 1 - position)
    window = (REACH + 2) * width
    padded = jnp.concatenate([jnp.full((REACH * width,), -1, jnp.int32), segments])
    seg_window = lax.dynamic_slice_in_dim(padded, first * width, window)
    start = jnp.sum(
        seg_window[:, None] < seg_window[None, REACH * width :], axis=0, dtype=jnp.int32
    )
    tile = max(min(256, width // 2), shard)
    tiles, earlier = 2 * width // tile, REACH * width // tile
    lo = start[::tile] // tile
    edge_next = jnp.where(even, place <= 2, place >= GROUP - 3)
    edge_near = jnp.where(even, place == 0, place == GROUP - 1)
    places = core[None].astype(jnp.int32)
    start = start[None, :]

    near_ordered = jnp.where(even, kv_near, kv_near[::-1])
    kv_prev = jnp.stack(
        [
            jnp.where(edge_next, kv_edge, kv_next),
            jnp.where(edge_near, kv_next, near_ordered[0]),
            jnp.where(edge_near, kv_edge1, near_ordered[1]),
        ]
    )

    row = jax.ShapeDtypeStruct((1, 2 * width), f32)
    turned = jax.ShapeDtypeStruct((tiles, head_dim, tile), f32)
    part = jax.ShapeDtypeStruct((2, width, head_dim), bf16)
    span_like = kv_next.shape
    natural = ((tiles, tile, head_dim), bf16)
    top, total, acc = vmem_kernel(
        own_forward_kernel, "own_forward", (row, row, turned),
        [natural, natural, ((tiles, head_dim, tile), bf16), ((tiles, tile, tile), f32)],
        6, tile, head_dim, 2,
    )(lo, places, start, queries, far, kv_own)
    attended, lse, delta, acc, p_near, p_next = vmem_kernel(
        earlier_kernel, "earlier",
        (
            part, row, row, turned,
            jax.ShapeDtypeStruct((2,) + span_like, bf16),
            jax.ShapeDtypeStruct(span_like, bf16),
        ),
        [
            ((earlier, head_dim, tile), bf16),
            ((earlier, head_dim, tile), bf16),
            ((earlier, tile, tile), f32),
            ((earlier * tile, head_dim), f32),
            ((earlier * tile, head_dim), f32),
        ],
        6, tile, head_dim, 6,
    )(lo, places, start, queries, out_grad, far, top, total, acc, kv_prev)

    r_edge1 = lax.ppermute(p_near[1], CTX, inverse(edge1))
    r_edge2 = lax.ppermute(p_near[0], CTX, inverse(edge2))
    r_next = lax.ppermute(p_next, CTX, inverse(far_chip))
    r_near = lax.ppermute(p_near, CTX, inverse(near))

    out_own, out_far, p_own = vmem_kernel(
        own_backward_kernel, "own_backward",
        (part, part, jax.ShapeDtypeStruct((2,) + span_like, f32)),
        [natural, natural, ((tiles, head_dim, tile), bf16)]
        + [((tiles, tile, head_dim), f32)] * 2,
        6, tile, head_dim, 5,
    )(lo, places, start, queries, out_grad, far, kv_own, attended, lse, delta, acc)

    r_edge1, r_edge2, r_next, r_near, p_own = lax.optimization_barrier(
        (r_edge1, r_edge2, r_next, r_near, p_own)
    )
    edge_sum = jnp.where(edge_next, p_next.astype(f32), 0.0) + r_edge1.astype(f32)
    edge_sum = edge_sum + r_edge2.astype(f32)
    for bit in reversed(bits):
        halves = edge_sum.reshape((-1, 2) + half.shape[1:])
        away = pick(high[bit], halves[:, 0], halves[:, 1]).astype(bf16)
        other = lax.ppermute(away, everywhere, holder_pairs(ctx, heads, bit))
        edge_sum = pick(high[bit], halves[:, 1], halves[:, 0]) + other.astype(f32)
    returned = lax.ppermute(edge_sum[0].astype(bf16), everywhere, inverse(edge)).astype(f32)

    sums = p_own + r_near.astype(f32)
    first_sum, second_sum = sums[0], sums[1] + r_next.astype(f32)
    sums = jnp.stack([pick(even, second_sum, first_sum), pick(even, first_sum, second_sum)])
    for bit in reversed(bits):
        halves = sums.reshape((2, -1, 2) + half.shape[1:])
        away = pick(high[bit], halves[:, :, 1], halves[:, :, 0]).astype(bf16)
        other = lax.ppermute(away, everywhere, head_pairs(ctx, heads, bit))
        if bit == bits[-1]:
            other, out_far = lax.optimization_barrier((other, out_far))
            back = lax.ppermute(out_far, CTX, swap)
        elif bit == bits[0]:
            other, back = lax.optimization_barrier((other, back))
        sums = pick(high[bit], halves[:, :, 0], halves[:, :, 1]) + other.astype(f32)
    stays = sums[:, 0]
    own_half = pick(even, stays[1], stays[0])
    far_half = lax.ppermute(
        pick(even, stays[0], stays[1]).astype(bf16), CTX, swap
    ).astype(f32)
    lower = pick(even, far_half, own_half) + jnp.where(sends_lower, returned, 0.0)
    upper = pick(even, own_half, far_half) + jnp.where(sends_lower, 0.0, returned)
    grads = jnp.stack([lower, upper]).astype(bf16)

    results = []
    for k in range(2):
        results.append(
            jnp.where(
                even, jnp.stack([out_own[k], back[k]]), jnp.stack([back[k], out_own[k]])
            )[None]
        )
    return results[0], results[1], grads[:, 0][None], grads[:, 1][None]


def solution(mesh):
    ctx, heads = mesh.devices.shape
    mesh = Mesh(mesh.devices.reshape(ctx // 2, 2, heads), CTX + ("head",))
    by_head = P(CTX, None, None, "head")
    by_row = P(CTX, None, "head", None)
    return jax.shard_map(
        body,
        mesh=mesh,
        in_specs=(by_head, by_row, by_row, by_head, P()),
        out_specs=(by_head, by_head, by_row, by_row),
        check_vma=False,
    )
```

```python
import math

import jax
import jax.numpy as jnp
from jax import lax
from jax.experimental import pallas as pl
from jax.experimental.pallas import tpu as pltpu
from jax.sharding import Mesh
from jax.sharding import PartitionSpec as P

REACH = 3
GROUP = 8
NEG_FILL = -1e30
CTX = ("pair", "core")


def within(ctx, moves):
    return [(base + a, base + b) for base in range(0, ctx, GROUP) for a, b in moves]


def swap_pairs(ctx):
    return within(ctx, [(r, r ^ 1) for r in range(GROUP)])


def near_pairs(ctx):
    forth = [(r, r + 2) for r in range(0, GROUP - 2, 2)]
    return within(ctx, forth + [(r, r - 2) for r in range(3, GROUP, 2)])


def next_pairs(ctx):
    forth = [(r, r + 4) for r in range(0, GROUP - 4, 2)]
    return within(ctx, forth + [(r, r - 4) for r in range(5, GROUP, 2)])


def head_pairs(ctx, heads, bit):
    return [(d, d ^ bit) for d in range(ctx * heads)]


def holder_pairs(ctx, heads, bit):
    holders = [r for r in range(GROUP) if r < REACH or r >= GROUP - REACH]
    return [
        ((base + r) * heads + h, (base + r) * heads + (h ^ bit))
        for base in range(0, ctx, GROUP)
        for r in holders
        for h in range(heads)
    ]


def edge_pairs(ctx, heads):
    moves = []
    for base in range(0, ctx, GROUP):
        for k in range(REACH):
            top = base + GROUP - 1 - k
            if base + GROUP < ctx:
                moves.append((top, base + GROUP + REACH - 1 - k))
            else:
                moves.append((top, base + GROUP - REACH + k))
            if base > 0:
                moves.append((base + k, base - REACH + k))
    return [
        (a * heads + h, b * heads + heads - 1 - h) for a, b in moves for h in range(heads)
    ]


def folds(heads):
    return [1 << k for k in reversed(range(heads.bit_length() - 1))]


def pick(bit, low, high):
    return jnp.where(bit, high, low)


def by_bit(bit, mine, other, axis):
    mine, other = jnp.expand_dims(mine, axis), jnp.expand_dims(other, axis)
    place = lax.broadcasted_iota(jnp.int32, (2,) + (1,) * (mine.ndim - axis - 1), 0)
    return jnp.where(place == bit.astype(jnp.int32), mine, other)


def inverse(pairs):
    return [(b, a) for a, b in pairs]


NT = (((1,), (1,)), ((), ()))
NN = (((1,), (0,)), ((), ()))


def matmul(a, b, dims=NN):
    return lax.dot_general(a, b, dims, preferred_element_type=jnp.float32)


def key_tile(ref, j, which, tile):
    _, shards, _, shard, head_dim = ref.shape
    per_span = shards * shard // tile
    rows = pl.ds((j % per_span) * (tile // shard), tile // shard)
    return ref[j // per_span, rows, which].reshape(tile, head_dim)


def query_tile(own_ref, far_ref, far_index, core, i, tile):
    width = far_ref.shape[1]
    span, part = divmod(i, width // tile)
    rows = pl.ds(part * tile, tile)
    return own_ref[core, rows] if span == 0 else far_ref[far_index, rows]


def masked_scores(keys, query, start, j, tile, causal):
    raw = matmul(keys, query, NT) * (query.shape[1] ** -0.5 * math.log2(math.e))
    at_key = lax.broadcasted_iota(jnp.int32, raw.shape, 0)
    allowed = at_key >= start - j * tile
    if causal:
        allowed = allowed & (at_key <= lax.broadcasted_iota(jnp.int32, raw.shape, 1))
    return jnp.where(allowed, raw, NEG_FILL)


def column_max(a):
    return jnp.max(a, axis=0, keepdims=True)


def column_sum(a):
    return jnp.sum(a, axis=0, keepdims=True)


def own_forward_kernel(
    lo_ref, place_ref, start_row, queries, far, kv_own, top_row, total_row, acc_out,
    keys, values, values_t, scores,
):
    tile, tiles = scores.shape[1], scores.shape[0]
    core = place_ref[0]
    before = REACH * tiles // 2
    for j in range(tiles):
        span = core if j < tiles // 2 else 1 - core
        rows = pl.ds(j % (tiles // 2) * (tile // kv_own.shape[3]), tile // kv_own.shape[3])
        keys[j] = kv_own[span, rows, 0].reshape(keys.shape[1:])
        values_t[j] = kv_own[span, rows, 1].reshape(keys.shape[1:]).T
    for i in range(tiles):
        columns = pl.ds(i * tile, tile)
        query = query_tile(queries, far, 0, core, i, tile)
        start = start_row[:, columns]
        lo = jnp.maximum(lo_ref[i] - before, 0)

        def score_tile(j, causal):
            raw = masked_scores(keys[j], query, start, j + before, tile, causal)
            scores[j] = raw
            return column_max(raw)

        top = lax.fori_loop(
            lo, i, lambda j, m: jnp.maximum(m, score_tile(j, False)), score_tile(i, True)
        )

        def forward(j, carry):
            total, acc = carry
            prob = jnp.exp2(scores[j] - top)
            return total + column_sum(prob), acc + matmul(values_t[j], prob.astype(jnp.bfloat16))

        total, acc = lax.fori_loop(
            lo, i + 1, forward, (jnp.zeros_like(top), jnp.zeros(acc_out.shape[1:], jnp.float32))
        )
        top_row[:, columns] = top
        total_row[:, columns] = total
        acc_out[i] = acc


def earlier_kernel(
    lo_ref, place_ref, start_row, queries, out_grad, far, top_row, total_row, acc_in, kv_prev,
    attended_out, lse_row, delta_row, acc_out, p_near, p_next,
    keys_t, values_t, scores, key_acc, value_acc,
):
    tile, before = scores.shape[1], scores.shape[0]
    tiles = acc_in.shape[0]
    scale = queries.shape[2] ** -0.5
    core = place_ref[0]
    bf16, f32 = jnp.bfloat16, jnp.float32
    first = lo_ref[0]

    @pl.when(first < before)
    def _():
        key_acc[...] = jnp.zeros_like(key_acc)
        value_acc[...] = jnp.zeros_like(value_acc)

        def turn(j, carry):
            keys_t[j] = key_tile(kv_prev, j, 0, tile).T
            values_t[j] = key_tile(kv_prev, j, 1, tile).T
            return carry

        lax.fori_loop(first, before, turn, 0)

    for i in range(tiles):
        columns = pl.ds(i * tile, tile)
        query = query_tile(queries, far, 0, core, i, tile)
        grad = query_tile(out_grad, far, 1, core, i, tile)
        start = start_row[:, columns]
        lo = jnp.minimum(lo_ref[i], before)
        own_top = top_row[:, columns]

        def score_tile(j, top):
            raw = masked_scores(key_tile(kv_prev, j, 0, tile), query, start, j, tile, False)
            scores[j] = raw
            return jnp.maximum(top, column_max(raw))

        top = lax.fori_loop(lo, before, score_tile, own_top)
        shrink = jnp.exp2(own_top - top)

        def forward(j, carry):
            total, acc = carry
            prob = jnp.exp2(scores[j] - top)
            scores[j] = prob
            return total + column_sum(prob), acc + matmul(values_t[j], prob.astype(bf16))

        total, acc = lax.fori_loop(
            lo, before, forward, (total_row[:, columns] * shrink, acc_in[i] * shrink)
        )
        inv = 1.0 / total
        attended_t = (acc * inv).astype(bf16).astype(f32)
        delta = column_sum(grad.astype(f32).T * attended_t)
        half, part = divmod(i, tiles // 2)
        attended_out[half, pl.ds(part * tile, tile)] = attended_t.T.astype(bf16)
        lse_row[:, columns] = top + jnp.log2(total)
        delta_row[:, columns] = delta

        def backward(j, acc):
            prob = scores[j] * inv
            here = pl.ds(pl.multiple_of(j * tile, tile), tile)
            value_acc[here] += matmul(prob.astype(bf16), grad)
            dot_grad = matmul(key_tile(kv_prev, j, 1, tile), grad, NT)
            score_grad = (prob * (dot_grad - delta)).astype(bf16)
            key_acc[here] += matmul(score_grad, query)
            return acc + matmul(keys_t[j], score_grad)

        acc_out[i] = lax.fori_loop(lo, before, backward, jnp.zeros(acc_out.shape[1:], f32))

    shards, shard = kv_prev.shape[1], kv_prev.shape[3]

    @pl.when(first < before)
    def _():
        for slot, target in enumerate((p_next, p_near.at[0], p_near.at[1])):
            for row in range(shards):
                here = pl.ds((slot * shards + row) * shard, shard)
                target[row, 0] = (key_acc[here] * scale).astype(bf16)
                target[row, 1] = value_acc[here].astype(bf16)

    @pl.when(first >= before)
    def _():
        p_next[...] = jnp.zeros_like(p_next)
        p_near[...] = jnp.zeros_like(p_near)


def own_backward_kernel(
    lo_ref, place_ref, start_row, queries, out_grad, far, kv_own, attended, lse_row, delta_row,
    acc_in, out_own, out_far, p_own,
    keys, values, keys_t, key_acc, value_acc,
):
    tiles, tile = keys.shape[0], keys.shape[1]
    scale = queries.shape[2] ** -0.5
    core = place_ref[0]
    bf16, f32 = jnp.bfloat16, jnp.float32
    before = REACH * tiles // 2
    for j in range(tiles):
        span = core if j < tiles // 2 else 1 - core
        rows = pl.ds(j % (tiles // 2) * (tile // kv_own.shape[3]), tile // kv_own.shape[3])
        block = kv_own[span, rows, 0].reshape(keys.shape[1:])
        keys[j] = block
        keys_t[j] = block.T
        values[j] = kv_own[span, rows, 1].reshape(keys.shape[1:])
    key_acc[...] = jnp.zeros_like(key_acc)
    value_acc[...] = jnp.zeros_like(value_acc)
    for i in range(tiles):
        columns = pl.ds(i * tile, tile)
        query = query_tile(queries, far, 0, core, i, tile)
        grad = query_tile(out_grad, far, 1, core, i, tile)
        start = start_row[:, columns]
        lse, delta = lse_row[:, columns], delta_row[:, columns]

        def backward(j, acc, causal):
            raw = masked_scores(keys[j], query, start, j + before, tile, causal)
            prob = jnp.exp2(raw - lse)
            value_acc[j] += matmul(prob.astype(bf16), grad)
            score_grad = (prob * (matmul(values[j], grad, NT) - delta)).astype(bf16)
            key_acc[j] += matmul(score_grad, query)
            return acc + matmul(keys_t[j], score_grad)

        acc = backward(i, acc_in[i], True)
        acc = lax.fori_loop(
            jnp.maximum(lo_ref[i] - before, 0), i, lambda j, acc: backward(j, acc, False), acc
        )
        half, part = divmod(i, tiles // 2)
        rows = pl.ds(part * tile, tile)
        (out_own, out_far)[half][1, rows] = (acc.T * scale).astype(bf16)
    out_own[0] = attended[0]
    out_far[0] = attended[1]
    shards, shard = kv_own.shape[1], kv_own.shape[3]
    for span in range(2):
        for row in range(shards):
            j, part = divmod((span * shards + row) * shard, tile)
            here = pl.ds(part, shard)
            p_own[span, row, 0] = key_acc[j, here] * scale
            p_own[span, row, 1] = value_acc[j, here]


def vmem_kernel(kernel, name, outputs, scratch, tiles, tile, head_dim, matmuls):
    def call(*operands):
        rest = [pl.BlockSpec(memory_space=pltpu.VMEM)] * (len(operands) - 2)
        return pl.pallas_call(
            kernel,
            out_shape=outputs,
            in_specs=[pl.BlockSpec(memory_space=pltpu.SMEM)] * 2 + rest,
            out_specs=[pl.BlockSpec(memory_space=pltpu.VMEM)] * len(outputs),
            scratch_shapes=[pltpu.VMEM(shape, dtype) for shape, dtype in scratch],
            compiler_params=pltpu.CompilerParams(vmem_limit_bytes=24 * 1024 * 1024),
            cost_estimate=pl.CostEstimate(
                flops=2 * matmuls * tiles * tile * tile * head_dim,
                bytes_accessed=4 * 1024 * 1024,
                transcendentals=tiles * tile * tile,
            ),
            name=name,
        )(*operands)

    return call


def body(queries, key_states, value_states, out_grad, segments):
    ctx = lax.axis_size("pair") * 2
    core = lax.axis_index("core")
    position = lax.axis_index("pair") * 2 + core
    place = position % GROUP
    width = queries.shape[2]
    heads = lax.axis_size("head")
    shard = key_states.shape[2]
    head_dim = key_states.shape[3]
    bf16, f32 = jnp.bfloat16, jnp.float32

    swap, near, far_chip = swap_pairs(ctx), near_pairs(ctx), next_pairs(ctx)
    edge1 = within(ctx, [(2, 0), (GROUP - 3, GROUP - 1)])
    edge2 = within(ctx, [(1, 0), (GROUP - 2, GROUP - 1)])
    everywhere = CTX + ("head",)
    even = core == 0
    sends_lower = place >= GROUP - REACH
    head = lax.axis_index("head")
    bits = folds(heads)
    high = {bit: (head & bit) != 0 for bit in bits}
    edge = edge_pairs(ctx, heads)

    lower = jnp.stack([key_states[0, 0], value_states[0, 0]])
    upper = jnp.stack([key_states[0, 1], value_states[0, 1]])
    leaving = pick(sends_lower, upper, lower)
    half = by_bit(core, pick(even, upper, lower), lax.ppermute(pick(even, lower, upper), CTX, swap), 0)
    crossed = lax.ppermute(leaving, everywhere, edge)
    kv_all = jnp.concatenate([half, crossed[None]])[:, None]
    is_edge = lax.broadcasted_iota(jnp.int32, (3, 1, 1, 1, 1, 1), 0) == 2
    slot = lax.broadcasted_iota(jnp.int32, (1, 1, 2, 1, 1, 1), 2) == 1
    for bit in bits:
        other = lax.ppermute(kv_all, everywhere, head_pairs(ctx, heads, bit))
        stays = slot == (high[bit] ^ is_edge)
        kv_all = jnp.where(stays, kv_all[:, :, None], other[:, :, None])
        kv_all = kv_all.reshape((3, -1) + half.shape[1:])
    kv_own, kv_edge = kv_all[:2], kv_all[2]

    queries, out_grad = queries[0], out_grad[0]
    far = lax.ppermute(
        jnp.where(
            even,
            jnp.stack([queries[1], out_grad[1]]),
            jnp.stack([queries[0], out_grad[0]]),
        ),
        CTX,
        swap,
    )

    hands_edge = (place == 1) | (place == GROUP - 2)
    kv_next = jnp.where(hands_edge, kv_edge, jnp.where(even, kv_own[1], kv_own[0]))
    kv_next = lax.ppermute(kv_next, CTX, far_chip + edge2)
    kv_near = lax.ppermute(kv_own, CTX, near)
    kv_edge1 = lax.ppermute(kv_edge, CTX, edge1)

    first = jnp.where(even, position, 2 * ctx - 1 - position)
    window = (REACH + 2) * width
    padded = jnp.concatenate([jnp.full((REACH * width,), -1, jnp.int32), segments])
    seg_window = lax.dynamic_slice_in_dim(padded, first * width, window)
    start = jnp.sum(
        seg_window[:, None] < seg_window[None, REACH * width :], axis=0, dtype=jnp.int32
    )
    tile = max(min(256, width // 2), shard)
    tiles, earlier = 2 * width // tile, REACH * width // tile
    lo = start[::tile] // tile
    edge_next = jnp.where(even, place <= 2, place >= GROUP - 3)
    edge_near = jnp.where(even, place == 0, place == GROUP - 1)
    places = core[None].astype(jnp.int32)
    start = start[None, :]

    near_ordered = jnp.where(even, kv_near, kv_near[::-1])
    kv_prev = jnp.stack(
        [
            jnp.where(edge_next, kv_edge, kv_next),
            jnp.where(edge_near, kv_next, near_ordered[0]),
            jnp.where(edge_near, kv_edge1, near_ordered[1]),
        ]
    )

    row = jax.ShapeDtypeStruct((1, 2 * width), f32)
    turned = jax.ShapeDtypeStruct((tiles, head_dim, tile), f32)
    part = jax.ShapeDtypeStruct((2, width, head_dim), bf16)
    span_like = kv_next.shape
    natural = ((tiles, tile, head_dim), bf16)
    top, total, acc = vmem_kernel(
        own_forward_kernel, "own_forward", (row, row, turned),
        [natural, natural, ((tiles, head_dim, tile), bf16), ((tiles, tile, tile), f32)],
        6, tile, head_dim, 2,
    )(lo, places, start, queries, far, kv_own)
    attended, lse, delta, acc, p_near, p_next = vmem_kernel(
        earlier_kernel, "earlier",
        (
            part, row, row, turned,
            jax.ShapeDtypeStruct((2,) + span_like, bf16),
            jax.ShapeDtypeStruct(span_like, bf16),
        ),
        [
            ((earlier, head_dim, tile), bf16),
            ((earlier, head_dim, tile), bf16),
            ((earlier, tile, tile), f32),
            ((earlier * tile, head_dim), f32),
            ((earlier * tile, head_dim), f32),
        ],
        6, tile, head_dim, 6,
    )(lo, places, start, queries, out_grad, far, top, total, acc, kv_prev)

    r_edge1 = lax.ppermute(p_near[1], CTX, inverse(edge1))
    r_next = lax.ppermute(
        jnp.where(edge_near, p_near[0], p_next), CTX, inverse(far_chip + edge2)
    )
    r_near = lax.ppermute(p_near, CTX, inverse(near))

    out_own, out_far, p_own = vmem_kernel(
        own_backward_kernel, "own_backward",
        (part, part, jax.ShapeDtypeStruct((2,) + span_like, f32)),
        [natural, natural, ((tiles, head_dim, tile), bf16)]
        + [((tiles, tile, head_dim), f32)] * 2,
        6, tile, head_dim, 5,
    )(lo, places, start, queries, out_grad, far, kv_own, attended, lse, delta, acc)

    r_edge1, r_next, r_near, p_own = lax.optimization_barrier((r_edge1, r_next, r_near, p_own))
    edge_sum = jnp.where(edge_next, p_next.astype(f32), 0.0) + r_edge1.astype(f32)
    r_next = r_next.astype(f32)
    edge_sum = edge_sum + jnp.where(hands_edge, r_next, 0.0)
    for bit in reversed(bits):
        halves = edge_sum.reshape((-1, 2) + half.shape[1:])
        away = pick(high[bit], halves[:, 0], halves[:, 1]).astype(bf16)
        other = lax.ppermute(away, everywhere, holder_pairs(ctx, heads, bit))
        edge_sum = pick(high[bit], halves[:, 1], halves[:, 0]) + other.astype(f32)
    returned = lax.ppermute(edge_sum[0].astype(bf16), everywhere, inverse(edge)).astype(f32)

    sums = p_own + r_near.astype(f32)
    first_sum, second_sum = sums[0], sums[1] + jnp.where(hands_edge, 0.0, r_next)
    sums = jnp.stack([pick(even, second_sum, first_sum), pick(even, first_sum, second_sum)])
    for bit in reversed(bits):
        halves = sums.reshape((2, -1, 2) + half.shape[1:])
        away = pick(high[bit], halves[:, :, 1], halves[:, :, 0]).astype(bf16)
        other = lax.ppermute(away, everywhere, head_pairs(ctx, heads, bit))
        if bit == bits[-1]:
            other, out_far = lax.optimization_barrier((other, out_far))
            back = lax.ppermute(out_far, CTX, swap)
        elif bit == bits[0]:
            other, back = lax.optimization_barrier((other, back))
        sums = pick(high[bit], halves[:, :, 0], halves[:, :, 1]) + other.astype(f32)
    stays = sums[:, 0]
    own_half = pick(even, stays[1], stays[0])
    far_half = lax.ppermute(
        pick(even, stays[0], stays[1]).astype(bf16), CTX, swap
    ).astype(f32)
    lower = pick(even, far_half, own_half) + jnp.where(sends_lower, returned, 0.0)
    upper = pick(even, own_half, far_half) + jnp.where(sends_lower, 0.0, returned)
    grads = jnp.stack([lower, upper]).astype(bf16)

    results = []
    for k in range(2):
        results.append(
            jnp.where(
                even, jnp.stack([out_own[k], back[k]]), jnp.stack([back[k], out_own[k]])
            )[None]
        )
    return results[0], results[1], grads[:, 0][None], grads[:, 1][None]


def solution(mesh):
    ctx, heads = mesh.devices.shape
    mesh = Mesh(mesh.devices.reshape(ctx // 2, 2, heads), CTX + ("head",))
    by_head = P(CTX, None, None, "head")
    by_row = P(CTX, None, "head", None)
    return jax.shard_map(
        body,
        mesh=mesh,
        in_specs=(by_head, by_row, by_row, by_head, P()),
        out_specs=(by_head, by_head, by_row, by_row),
        check_vma=False,
    )
```

```python
import math

import jax
import jax.numpy as jnp
from jax import lax
from jax.experimental import pallas as pl
from jax.experimental.pallas import tpu as pltpu
from jax.sharding import Mesh
from jax.sharding import PartitionSpec as P

REACH = 3
GROUP = 8
NEG_FILL = -1e30
CTX = ("pair", "core")


def within(ctx, moves):
    return [(base + a, base + b) for base in range(0, ctx, GROUP) for a, b in moves]


def swap_pairs(ctx):
    return within(ctx, [(r, r ^ 1) for r in range(GROUP)])


def near_pairs(ctx):
    forth = [(r, r + 2) for r in range(0, GROUP - 2, 2)]
    return within(ctx, forth + [(r, r - 2) for r in range(3, GROUP, 2)])


def next_pairs(ctx):
    forth = [(r, r + 4) for r in range(0, GROUP - 4, 2)]
    return within(ctx, forth + [(r, r - 4) for r in range(5, GROUP, 2)])


def head_pairs(ctx, heads, bit):
    return [(d, d ^ bit) for d in range(ctx * heads)]


def holder_pairs(ctx, heads, bit):
    holders = [r for r in range(GROUP) if r < REACH or r >= GROUP - REACH]
    return [
        ((base + r) * heads + h, (base + r) * heads + (h ^ bit))
        for base in range(0, ctx, GROUP)
        for r in holders
        for h in range(heads)
    ]


def edge_pairs(ctx, heads):
    moves = []
    for base in range(0, ctx, GROUP):
        for k in range(REACH):
            top = base + GROUP - 1 - k
            if base + GROUP < ctx:
                moves.append((top, base + GROUP + REACH - 1 - k))
            else:
                moves.append((top, base + GROUP - REACH + k))
            if base > 0:
                moves.append((base + k, base - REACH + k))
    return [
        (a * heads + h, b * heads + heads - 1 - h) for a, b in moves for h in range(heads)
    ]


def folds(heads):
    return [1 << k for k in reversed(range(heads.bit_length() - 1))]


def pick(bit, low, high):
    return jnp.where(bit, high, low)


def by_bit(bit, mine, other, axis):
    mine, other = jnp.expand_dims(mine, axis), jnp.expand_dims(other, axis)
    place = lax.broadcasted_iota(jnp.int32, (2,) + (1,) * (mine.ndim - axis - 1), 0)
    return jnp.where(place == bit.astype(jnp.int32), mine, other)


def inverse(pairs):
    return [(b, a) for a, b in pairs]


NT = (((1,), (1,)), ((), ()))
NN = (((1,), (0,)), ((), ()))


def matmul(a, b, dims=NN):
    return lax.dot_general(a, b, dims, preferred_element_type=jnp.float32)


def key_tile(ref, j, which, tile):
    _, shards, _, shard, head_dim = ref.shape
    per_span = shards * shard // tile
    rows = pl.ds((j % per_span) * (tile // shard), tile // shard)
    return ref[j // per_span, rows, which].reshape(tile, head_dim)


def query_tile(own_ref, far_ref, far_index, core, i, tile):
    width = far_ref.shape[1]
    span, part = divmod(i, width // tile)
    rows = pl.ds(part * tile, tile)
    return own_ref[core, rows] if span == 0 else far_ref[far_index, rows]


def masked_scores(keys, query, start, j, tile, causal):
    raw = matmul(keys, query, NT) * (query.shape[1] ** -0.5 * math.log2(math.e))
    at_key = lax.broadcasted_iota(jnp.int32, raw.shape, 0)
    allowed = at_key >= start - j * tile
    if causal:
        allowed = allowed & (at_key <= lax.broadcasted_iota(jnp.int32, raw.shape, 1))
    return jnp.where(allowed, raw, NEG_FILL)


def column_max(a):
    return jnp.max(a, axis=0, keepdims=True)


def column_sum(a):
    return jnp.sum(a, axis=0, keepdims=True)


def own_forward_kernel(
    lo_ref, place_ref, start_row, queries, out_grad, far, kv_own, top_row, total_row, acc_out,
    grad_out,
    keys, values, values_t, scores,
):
    tile, tiles = scores.shape[1], scores.shape[0]
    core = place_ref[0]
    before = REACH * tiles // 2
    for j in range(tiles):
        span = core if j < tiles // 2 else 1 - core
        rows = pl.ds(j % (tiles // 2) * (tile // kv_own.shape[3]), tile // kv_own.shape[3])
        keys[j] = kv_own[span, rows, 0].reshape(keys.shape[1:])
        values_t[j] = kv_own[span, rows, 1].reshape(keys.shape[1:]).T
    for i in range(tiles):
        columns = pl.ds(i * tile, tile)
        query = query_tile(queries, far, 0, core, i, tile)
        start = start_row[:, columns]
        lo = jnp.maximum(lo_ref[i] - before, 0)

        def score_tile(j, causal):
            raw = masked_scores(keys[j], query, start, j + before, tile, causal)
            scores[j] = raw
            return column_max(raw)

        top = lax.fori_loop(
            lo, i, lambda j, m: jnp.maximum(m, score_tile(j, False)), score_tile(i, True)
        )

        def forward(j, carry):
            total, acc = carry
            prob = jnp.exp2(scores[j] - top)
            return total + column_sum(prob), acc + matmul(values_t[j], prob.astype(jnp.bfloat16))

        total, acc = lax.fori_loop(
            lo, i + 1, forward, (jnp.zeros_like(top), jnp.zeros(acc_out.shape[1:], jnp.float32))
        )
        top_row[:, columns] = top
        total_row[:, columns] = total
        acc_out[i] = acc
        grad_out[i] = query_tile(out_grad, far, 1, core, i, tile).T


def earlier_kernel(
    lo_ref, place_ref, start_row, queries, out_grad, far, top_row, total_row, acc_in, grad_t, kv_prev,
    attended_out, lse_row, delta_row, acc_out, p_near, p_next,
    keys_t, values_t, scores, key_acc, value_acc,
):
    tile, before = scores.shape[1], scores.shape[0]
    tiles = acc_in.shape[0]
    scale = queries.shape[2] ** -0.5
    core = place_ref[0]
    bf16, f32 = jnp.bfloat16, jnp.float32
    first = lo_ref[0]

    @pl.when(first < before)
    def _():
        key_acc[...] = jnp.zeros_like(key_acc)
        value_acc[...] = jnp.zeros_like(value_acc)

        def turn(j, carry):
            keys_t[j] = key_tile(kv_prev, j, 0, tile).T
            values_t[j] = key_tile(kv_prev, j, 1, tile).T
            return carry

        lax.fori_loop(first, before, turn, 0)

    for i in range(tiles):
        columns = pl.ds(i * tile, tile)
        query = query_tile(queries, far, 0, core, i, tile)
        grad = query_tile(out_grad, far, 1, core, i, tile)
        start = start_row[:, columns]
        lo = jnp.minimum(lo_ref[i], before)
        own_top = top_row[:, columns]

        def score_tile(j, top):
            raw = masked_scores(key_tile(kv_prev, j, 0, tile), query, start, j, tile, False)
            scores[j] = raw
            return jnp.maximum(top, column_max(raw))

        top = lax.fori_loop(lo, before, score_tile, own_top)
        shrink = jnp.exp2(own_top - top)

        def forward(j, carry):
            total, acc = carry
            prob = jnp.exp2(scores[j] - top)
            scores[j] = prob
            return total + column_sum(prob), acc + matmul(values_t[j], prob.astype(bf16))

        total, acc = lax.fori_loop(
            lo, before, forward, (total_row[:, columns] * shrink, acc_in[i] * shrink)
        )
        inv = 1.0 / total
        attended_t = (acc * inv).astype(bf16).astype(f32)
        delta = column_sum(grad_t[i].astype(f32) * attended_t)
        half, part = divmod(i, tiles // 2)
        attended_out[half, pl.ds(part * tile, tile)] = attended_t.T.astype(bf16)
        lse_row[:, columns] = top + jnp.log2(total)
        delta_row[:, columns] = delta

        def backward(j, acc):
            prob = scores[j] * inv
            here = pl.ds(pl.multiple_of(j * tile, tile), tile)
            value_acc[here] += matmul(prob.astype(bf16), grad)
            dot_grad = matmul(key_tile(kv_prev, j, 1, tile), grad, NT)
            score_grad = (prob * (dot_grad - delta)).astype(bf16)
            key_acc[here] += matmul(score_grad, query)
            return acc + matmul(keys_t[j], score_grad)

        acc_out[i] = lax.fori_loop(lo, before, backward, jnp.zeros(acc_out.shape[1:], f32))

    shards, shard = kv_prev.shape[1], kv_prev.shape[3]

    @pl.when(first < before)
    def _():
        for slot, target in enumerate((p_next, p_near.at[0], p_near.at[1])):
            for row in range(shards):
                here = pl.ds((slot * shards + row) * shard, shard)
                target[row, 0] = (key_acc[here] * scale).astype(bf16)
                target[row, 1] = value_acc[here].astype(bf16)

    @pl.when(first >= before)
    def _():
        p_next[...] = jnp.zeros_like(p_next)
        p_near[...] = jnp.zeros_like(p_near)


def own_backward_kernel(
    lo_ref, place_ref, start_row, queries, out_grad, far, kv_own, attended, lse_row, delta_row,
    acc_in, out_own, out_far, p_own,
    keys, values, keys_t, key_acc, value_acc,
):
    tiles, tile = keys.shape[0], keys.shape[1]
    scale = queries.shape[2] ** -0.5
    core = place_ref[0]
    bf16, f32 = jnp.bfloat16, jnp.float32
    before = REACH * tiles // 2
    for j in range(tiles):
        span = core if j < tiles // 2 else 1 - core
        rows = pl.ds(j % (tiles // 2) * (tile // kv_own.shape[3]), tile // kv_own.shape[3])
        block = kv_own[span, rows, 0].reshape(keys.shape[1:])
        keys[j] = block
        keys_t[j] = block.T
        values[j] = kv_own[span, rows, 1].reshape(keys.shape[1:])
    key_acc[...] = jnp.zeros_like(key_acc)
    value_acc[...] = jnp.zeros_like(value_acc)
    for i in range(tiles):
        columns = pl.ds(i * tile, tile)
        query = query_tile(queries, far, 0, core, i, tile)
        grad = query_tile(out_grad, far, 1, core, i, tile)
        start = start_row[:, columns]
        lse, delta = lse_row[:, columns], delta_row[:, columns]

        def backward(j, acc, causal):
            raw = masked_scores(keys[j], query, start, j + before, tile, causal)
            prob = jnp.exp2(raw - lse)
            value_acc[j] += matmul(prob.astype(bf16), grad)
            score_grad = (prob * (matmul(values[j], grad, NT) - delta)).astype(bf16)
            key_acc[j] += matmul(score_grad, query)
            return acc + matmul(keys_t[j], score_grad)

        acc = backward(i, acc_in[i], True)
        acc = lax.fori_loop(
            jnp.maximum(lo_ref[i] - before, 0), i, lambda j, acc: backward(j, acc, False), acc
        )
        half, part = divmod(i, tiles // 2)
        rows = pl.ds(part * tile, tile)
        (out_own, out_far)[half][1, rows] = (acc.T * scale).astype(bf16)
    out_own[0] = attended[0]
    out_far[0] = attended[1]
    shards, shard = kv_own.shape[1], kv_own.shape[3]
    for span in range(2):
        for row in range(shards):
            j, part = divmod((span * shards + row) * shard, tile)
            here = pl.ds(part, shard)
            p_own[span, row, 0] = key_acc[j, here] * scale
            p_own[span, row, 1] = value_acc[j, here]


def vmem_kernel(kernel, name, outputs, scratch, tiles, tile, head_dim, matmuls):
    def call(*operands):
        rest = [pl.BlockSpec(memory_space=pltpu.VMEM)] * (len(operands) - 2)
        return pl.pallas_call(
            kernel,
            out_shape=outputs,
            in_specs=[pl.BlockSpec(memory_space=pltpu.SMEM)] * 2 + rest,
            out_specs=[pl.BlockSpec(memory_space=pltpu.VMEM)] * len(outputs),
            scratch_shapes=[pltpu.VMEM(shape, dtype) for shape, dtype in scratch],
            compiler_params=pltpu.CompilerParams(vmem_limit_bytes=24 * 1024 * 1024),
            cost_estimate=pl.CostEstimate(
                flops=2 * matmuls * tiles * tile * tile * head_dim,
                bytes_accessed=4 * 1024 * 1024,
                transcendentals=tiles * tile * tile,
            ),
            name=name,
        )(*operands)

    return call


def body(queries, key_states, value_states, out_grad, segments):
    ctx = lax.axis_size("pair") * 2
    core = lax.axis_index("core")
    position = lax.axis_index("pair") * 2 + core
    place = position % GROUP
    width = queries.shape[2]
    heads = lax.axis_size("head")
    shard = key_states.shape[2]
    head_dim = key_states.shape[3]
    bf16, f32 = jnp.bfloat16, jnp.float32

    swap, near, far_chip = swap_pairs(ctx), near_pairs(ctx), next_pairs(ctx)
    edge1 = within(ctx, [(2, 0), (GROUP - 3, GROUP - 1)])
    edge2 = within(ctx, [(1, 0), (GROUP - 2, GROUP - 1)])
    everywhere = CTX + ("head",)
    even = core == 0
    sends_lower = place >= GROUP - REACH
    head = lax.axis_index("head")
    bits = folds(heads)
    high = {bit: (head & bit) != 0 for bit in bits}
    edge = edge_pairs(ctx, heads)

    lower = jnp.stack([key_states[0, 0], value_states[0, 0]])
    upper = jnp.stack([key_states[0, 1], value_states[0, 1]])
    leaving = pick(sends_lower, upper, lower)
    half = by_bit(core, pick(even, upper, lower), lax.ppermute(pick(even, lower, upper), CTX, swap), 0)
    crossed = lax.ppermute(leaving, everywhere, edge)
    kv_all = jnp.concatenate([half, crossed[None]])[:, None]
    is_edge = lax.broadcasted_iota(jnp.int32, (3, 1, 1, 1, 1, 1), 0) == 2
    slot = lax.broadcasted_iota(jnp.int32, (1, 1, 2, 1, 1, 1), 2) == 1
    for bit in bits:
        other = lax.ppermute(kv_all, everywhere, head_pairs(ctx, heads, bit))
        stays = slot == (high[bit] ^ is_edge)
        kv_all = jnp.where(stays, kv_all[:, :, None], other[:, :, None])
        kv_all = kv_all.reshape((3, -1) + half.shape[1:])
    kv_own, kv_edge = kv_all[:2], kv_all[2]

    queries, out_grad = queries[0], out_grad[0]
    far = lax.ppermute(
        jnp.where(
            even,
            jnp.stack([queries[1], out_grad[1]]),
            jnp.stack([queries[0], out_grad[0]]),
        ),
        CTX,
        swap,
    )

    hands_edge = (place == 1) | (place == GROUP - 2)
    kv_next = jnp.where(hands_edge, kv_edge, jnp.where(even, kv_own[1], kv_own[0]))
    kv_next = lax.ppermute(kv_next, CTX, far_chip + edge2)
    kv_near = lax.ppermute(kv_own, CTX, near)
    kv_edge1 = lax.ppermute(kv_edge, CTX, edge1)

    first = jnp.where(even, position, 2 * ctx - 1 - position)
    window = (REACH + 2) * width
    padded = jnp.concatenate([jnp.full((REACH * width,), -1, jnp.int32), segments])
    seg_window = lax.dynamic_slice_in_dim(padded, first * width, window)
    start = jnp.sum(
        seg_window[:, None] < seg_window[None, REACH * width :], axis=0, dtype=jnp.int32
    )
    tile = max(min(256, width // 2), shard)
    tiles, earlier = 2 * width // tile, REACH * width // tile
    lo = start[::tile] // tile
    edge_next = jnp.where(even, place <= 2, place >= GROUP - 3)
    edge_near = jnp.where(even, place == 0, place == GROUP - 1)
    places = core[None].astype(jnp.int32)
    start = start[None, :]

    near_ordered = jnp.where(even, kv_near, kv_near[::-1])
    kv_prev = jnp.stack(
        [
            jnp.where(edge_next, kv_edge, kv_next),
            jnp.where(edge_near, kv_next, near_ordered[0]),
            jnp.where(edge_near, kv_edge1, near_ordered[1]),
        ]
    )

    row = jax.ShapeDtypeStruct((1, 2 * width), f32)
    turned = jax.ShapeDtypeStruct((tiles, head_dim, tile), f32)
    part = jax.ShapeDtypeStruct((2, width, head_dim), bf16)
    span_like = kv_next.shape
    natural = ((tiles, tile, head_dim), bf16)
    top, total, acc, grad_t = vmem_kernel(
        own_forward_kernel, "own_forward", (row, row, turned, jax.ShapeDtypeStruct(turned.shape, bf16)),
        [natural, natural, ((tiles, head_dim, tile), bf16), ((tiles, tile, tile), f32)],
        6, tile, head_dim, 2,
    )(lo, places, start, queries, out_grad, far, kv_own)
    attended, lse, delta, acc, p_near, p_next = vmem_kernel(
        earlier_kernel, "earlier",
        (
            part, row, row, turned,
            jax.ShapeDtypeStruct((2,) + span_like, bf16),
            jax.ShapeDtypeStruct(span_like, bf16),
        ),
        [
            ((earlier, head_dim, tile), bf16),
            ((earlier, head_dim, tile), bf16),
            ((earlier, tile, tile), f32),
            ((earlier * tile, head_dim), f32),
            ((earlier * tile, head_dim), f32),
        ],
        6, tile, head_dim, 6,
    )(lo, places, start, queries, out_grad, far, top, total, acc, grad_t, kv_prev)

    r_edge1 = lax.ppermute(p_near[1], CTX, inverse(edge1))
    r_edge2 = lax.ppermute(p_near[0], CTX, inverse(edge2))
    r_next = lax.ppermute(p_next, CTX, inverse(far_chip))
    r_near = lax.ppermute(p_near, CTX, inverse(near))

    out_own, out_far, p_own = vmem_kernel(
        own_backward_kernel, "own_backward",
        (part, part, jax.ShapeDtypeStruct((2,) + span_like, f32)),
        [natural, natural, ((tiles, head_dim, tile), bf16)]
        + [((tiles, tile, head_dim), f32)] * 2,
        6, tile, head_dim, 5,
    )(lo, places, start, queries, out_grad, far, kv_own, attended, lse, delta, acc)

    r_edge1, r_edge2, r_next, r_near, p_own = lax.optimization_barrier(
        (r_edge1, r_edge2, r_next, r_near, p_own)
    )
    edge_sum = jnp.where(edge_next, p_next.astype(f32), 0.0) + r_edge1.astype(f32)
    edge_sum = edge_sum + r_edge2.astype(f32)
    for bit in reversed(bits):
        halves = edge_sum.reshape((-1, 2) + half.shape[1:])
        away = pick(high[bit], halves[:, 0], halves[:, 1]).astype(bf16)
        other = lax.ppermute(away, everywhere, holder_pairs(ctx, heads, bit))
        edge_sum = pick(high[bit], halves[:, 1], halves[:, 0]) + other.astype(f32)
    returned = lax.ppermute(edge_sum[0].astype(bf16), everywhere, inverse(edge)).astype(f32)

    sums = p_own + r_near.astype(f32)
    first_sum, second_sum = sums[0], sums[1] + r_next.astype(f32)
    sums = jnp.stack([pick(even, second_sum, first_sum), pick(even, first_sum, second_sum)])
    for bit in reversed(bits):
        halves = sums.reshape((2, -1, 2) + half.shape[1:])
        away = pick(high[bit], halves[:, :, 1], halves[:, :, 0]).astype(bf16)
        other = lax.ppermute(away, everywhere, head_pairs(ctx, heads, bit))
        if bit == bits[-1]:
            other, out_far = lax.optimization_barrier((other, out_far))
            back = lax.ppermute(out_far, CTX, swap)
        elif bit == bits[0]:
            other, back = lax.optimization_barrier((other, back))
        sums = pick(high[bit], halves[:, :, 0], halves[:, :, 1]) + other.astype(f32)
    stays = sums[:, 0]
    own_half = pick(even, stays[1], stays[0])
    far_half = lax.ppermute(
        pick(even, stays[0], stays[1]).astype(bf16), CTX, swap
    ).astype(f32)
    lower = pick(even, far_half, own_half) + jnp.where(sends_lower, returned, 0.0)
    upper = pick(even, own_half, far_half) + jnp.where(sends_lower, 0.0, returned)
    grads = jnp.stack([lower, upper]).astype(bf16)

    results = []
    for k in range(2):
        results.append(
            jnp.where(
                even, jnp.stack([out_own[k], back[k]]), jnp.stack([back[k], out_own[k]])
            )[None]
        )
    return results[0], results[1], grads[:, 0][None], grads[:, 1][None]


def solution(mesh):
    ctx, heads = mesh.devices.shape
    mesh = Mesh(mesh.devices.reshape(ctx // 2, 2, heads), CTX + ("head",))
    by_head = P(CTX, None, None, "head")
    by_row = P(CTX, None, "head", None)
    return jax.shard_map(
        body,
        mesh=mesh,
        in_specs=(by_head, by_row, by_row, by_head, P()),
        out_specs=(by_head, by_head, by_row, by_row),
        check_vma=False,
    )
```
